32 devices in a mesh: group: 4 (over y, x), replica: 8 (over z, core).
Axes of the slice: x: 2, y: 2, z: 4, core: 2. Of those that a mesh axis runs over, the one named last changes fastest.
Arguments:
- tokens: bfloat16 [32, 1088, 1024], P('replica', 'group'), may hold values from -6 to 6
- segments: int32 [32, 1088], P('replica', 'group'), may hold values from 0 to 4, as said below
- routes: int32 [32, 1088, 8], P('replica', 'group'), may hold values from 0 to 31, all different within a row; in each aligned block of 272 rows (0 to 271, 272 to 543, ..., all dimensions but the last counted through in order) at most 96 rows name the same one
- norm_in: bfloat16 [1024], P('group'), may hold values from 0.25 to 1.75
- q_weight: bfloat16 [1024, 1024], P('group'), may hold values from -0.1875 to 0.1875
- key_weight: bfloat16 [1024, 512], P('group'), may hold values from -0.1875 to 0.1875
- value_weight: bfloat16 [1024, 512], P('group'), may hold values from -0.1875 to 0.1875
- q_gain: bfloat16 [64], P('group'), may hold values from 0.25 to 1.75
- k_gain: bfloat16 [64], P('group'), may hold values from 0.25 to 1.75
- o_weight: bfloat16 [1024, 1024], P('group'), may hold values from -1.5 to 1.5
- norm_post: bfloat16 [1024], P('group'), may hold values from 0.25 to 1.75
- router: bfloat16 [1024, 32], P('group'), may hold values from -0.09375 to 0.09375
- expert_in: bfloat16 [32, 1024, 1024], P('group'), may hold values from -0.1875 to 0.1875
- expert_out: bfloat16 [32, 512, 1024], P('group'), may hold values from -0.75 to 0.75
- cotangent: bfloat16 [32, 1088, 1024], P('replica', 'group'), may hold values from -6 to 6
Outputs:
- layer_out: bfloat16 [32, 1088, 1024], P('replica', 'group')
- tokens_grad: float32 [32, 1088, 1024], P('replica', 'group')
- norm_in_grad: float32 [1024], P('group')
- q_weight_grad: float32 [1024, 1024], P('group')
- k_weight_grad: float32 [1024, 512], P('group')
- v_weight_grad: float32 [1024, 512], P('group')
- q_gain_grad: float32 [64], P('group')
- k_gain_grad: float32 [64], P('group')
- o_weight_grad: float32 [1024, 1024], P('group')
- norm_post_grad: float32 [1024], P('group')
- router_grad: float32 [1024, 32], P('group')
- expert_in_grad: float32 [32, 1024, 1024], P('group')
- expert_out_grad: float32 [32, 512, 1024], P('group')
The draws below stay inside these ranges and needn't reach their ends.
Inputs may be any that keep to these rules, and one draw needn't show every extreme that they name: `routes`: each token names 8 different experts. In each piece of 272 consecutive positions of a sequence, starting at a multiple of 272, no expert is named by more than 96 tokens, and some piece has an expert named by exactly 96. `segments`: segment numbers never fall along a sequence; the first position of every sequence holds 0 and the last holds 4.
All inputs are finite; a program needn't handle non-finite values.
Results may differ from the reference program's by a relative error of at most 0.022.
Values may be sent and summed in bfloat16 or wider, within the bound.
No kernel may reach another device: no remote copies, remote signals or barrier semaphores. Data moves between devices by JAX's collectives and lax.ppermute only.
A program may use at most 448 MiB of HBM per device.

```python
import math
import jax
import jax.numpy as jnp
import numpy as np
from jax import lax

MODEL_DIM = 1024
QUERY_HEADS = 16
KEY_VALUE_HEADS = 8
HEAD_SIZE = 64
F = 512
E = 32
TOPK = 8
SEQUENCE_LENGTH = 1088
SEQUENCE_COUNT = 4
SHARD_LEN = 272
CAP = 96
NSEQ = 32
N_GROUP = 4


def draw_segments(key, part):
    key = jax.random.fold_in(key, 11)
    key_inner, key_lower, key_upper, key_pick = jax.random.split(key, 4)
    inner_cuts = jax.random.randint(key_inner, (NSEQ, 4), 1, SEQUENCE_LENGTH)
    lower_cuts = jax.random.randint(key_lower, (NSEQ, 2), 1, SHARD_LEN)
    upper_cuts = jax.random.randint(key_upper, (NSEQ, 2), SEQUENCE_LENGTH - SHARD_LEN + 1, SEQUENCE_LENGTH)
    spanning = jnp.concatenate([lower_cuts, upper_cuts], axis=1)
    chosen = jax.random.randint(key_pick, (NSEQ // SEQUENCE_COUNT, 1), 0, SEQUENCE_COUNT)
    selected = (jnp.arange(NSEQ).reshape(NSEQ // SEQUENCE_COUNT, SEQUENCE_COUNT) % SEQUENCE_COUNT == chosen).reshape(NSEQ, 1)
    cut_points = jnp.where(selected, spanning, inner_cuts)
    places = jnp.arange(SEQUENCE_LENGTH)
    return jnp.sum((places[None, :, None] >= cut_points[:, None, :]).astype(jnp.int32), axis=2)


def steps_of(rng, dims, shards, low, largest):
    factor_of = 1.0
    for position, shards_of in shards:
        steps = jax.random.uniform(jax.random.fold_in(jax.random.fold_in(rng, 6), position), (shards_of,), jnp.float32, low / len(shards), largest / len(shards))
        factor_of = factor_of * jnp.repeat(jnp.exp(steps), dims[position] // shards_of).reshape((-1,) + (1,) * (len(dims) - 1 - position))
    return factor_of


def assign_block(rng, own, number, rows, number_of, top, most, lean):
    sequence = jax.random.permutation(rng, number_of)
    crowded, ordinary = load_shares(number_of, rows * top, most, lean, True), load_shares(number_of, rows * top, most, lean, False)
    places = jnp.arange(number_of)

    def named(sizes, offset_by):
        used = int((sizes > 0).sum())
        fixed = max(1, used // 4)
        shifted = fixed + (places - fixed + offset_by * (used - fixed)) % max(1, number_of - fixed)
        return jnp.zeros((number_of,), jnp.int32).at[sequence[jnp.where(places < fixed, places, shifted)]].set(jnp.asarray(sizes, jnp.int32))

    sizes = jnp.where(number % 4 == 0, named(crowded, number // 4), named(ordinary, number - number // 4 - 1))
    mixed = jax.random.permutation(jax.random.fold_in(own, 3), number_of)
    source_of, taker = mixed[0:number_of // 2 * 2:2], mixed[1:number_of // 2 * 2:2]
    slack = jnp.minimum(sizes[source_of] - 1, most - sizes[taker]) // 2
    slack = jnp.where((source_of == sequence[0]) | (taker == sequence[0]) | (sizes[taker] == 0), 0, jnp.maximum(slack, 0))
    shifted = jax.random.randint(jax.random.fold_in(own, 4), (number_of // 2,), 0, 1 << 20) % (slack + 1)
    sizes = sizes.at[source_of].add(-shifted).at[taker].add(shifted)
    items = jnp.searchsorted(jnp.cumsum(sizes), jnp.arange(rows * top), side="right").astype(jnp.int32)
    listing = items.reshape(top, rows).T
    listing = listing[jax.random.permutation(jax.random.fold_in(own, 1), rows)]
    offset_by = jax.random.randint(jax.random.fold_in(own, 2), (rows, 1), 0, top)
    return jnp.take_along_axis(listing, (jnp.arange(top)[None, :] + offset_by) % top, axis=1)


def load_shares(number_of, total, reach, slope, full):
    weights = [(1 << 20) // math.isqrt(rank ** slope) + 1 for rank in range(1, number_of + 1)]
    largest = reach if full else min(reach, max(-(-total // number_of), total * weights[0] // sum(weights)))
    least = 1 if total - largest >= number_of - 1 else 0
    holding, spare = [largest] + [least] * (number_of - 1), total - largest - least * (number_of - 1)
    while spare > 0:
        candidates = [i for i in range(1, number_of) if holding[i] < largest] or [i for i in range(1, number_of) if holding[i] < reach]
        pool, budget = sum([weights[i] for i in candidates]), spare
        for i in candidates:
            extra = min(reach - holding[i], max(1, budget * weights[i] // pool), spare)
            holding[i] = holding[i] + extra
            spare = spare - extra
    return np.array(holding)


def centred(rng, shape, scale, most, shards=(), kind=jnp.bfloat16):
    entries = scale * jax.random.normal(rng, shape, jnp.float32)
    if shards:
        entries = entries * steps_of(rng, shape, shards, -0.22, 0.18)
    return jnp.clip(entries, -most, most).astype(kind)


def setup_inputs(seed: int = 0) -> dict:
    streams_of = jax.random.split(jax.random.key(seed), 16)
    tokens = centred(streams_of[0], (NSEQ, SEQUENCE_LENGTH, MODEL_DIM), 1.0, 6.0, ((0, 8), (1, 4)))
    segments = draw_segments(jax.random.fold_in(streams_of[15], 71), 0)
    routes_keys = jax.random.split(jax.random.fold_in(streams_of[2], 1), NSEQ * SEQUENCE_LENGTH // SHARD_LEN)
    routes_turns = jax.random.permutation(jax.random.fold_in(streams_of[2], 3), NSEQ * SEQUENCE_LENGTH // SHARD_LEN)
    routes = jax.vmap(lambda own, number: assign_block(jax.random.fold_in(streams_of[2], 2), own, number, SHARD_LEN, E, TOPK, CAP, 1))(routes_keys, routes_turns).reshape((NSEQ, SEQUENCE_LENGTH, TOPK))
    norm_in = jnp.clip(1.0 + 0.15 * jax.random.normal(streams_of[3], (MODEL_DIM,), jnp.float32), 0.25, 1.75).astype(jnp.bfloat16)
    q_weight = centred(streams_of[4], (MODEL_DIM, QUERY_HEADS * HEAD_SIZE), MODEL_DIM ** -0.5, 0.1875, ((0, 4),))
    key_weight = centred(streams_of[5], (MODEL_DIM, KEY_VALUE_HEADS * HEAD_SIZE), MODEL_DIM ** -0.5, 0.1875, ((0, 4),))
    value_weight = centred(streams_of[6], (MODEL_DIM, KEY_VALUE_HEADS * HEAD_SIZE), MODEL_DIM ** -0.5, 0.1875, ((0, 4),))
    q_gain = jnp.clip(1.0 + 0.15 * jax.random.normal(streams_of[7], (HEAD_SIZE,), jnp.float32), 0.25, 1.75).astype(jnp.bfloat16)
    k_gain = jnp.clip(1.0 + 0.15 * jax.random.normal(streams_of[8], (HEAD_SIZE,), jnp.float32), 0.25, 1.75).astype(jnp.bfloat16)
    o_weight = centred(streams_of[9], (QUERY_HEADS * HEAD_SIZE, MODEL_DIM), (max(QUERY_HEADS * HEAD_SIZE // 64, 1)) ** -0.5, 1.5, ((0, 4),))
    norm_post = jnp.clip(1.0 + 0.15 * jax.random.normal(streams_of[10], (MODEL_DIM,), jnp.float32), 0.25, 1.75).astype(jnp.bfloat16)
    router = centred(streams_of[11], (MODEL_DIM, E), (4 * MODEL_DIM) ** -0.5, 0.09375, ((0, 4),))
    expert_in = centred(streams_of[12], (E, MODEL_DIM, 2 * F), MODEL_DIM ** -0.5, 0.1875, ((0, 4),))
    expert_out = centred(streams_of[13], (E, F, MODEL_DIM), (F // 8) ** -0.5, 0.75, ((0, 4),))
    cotangent = centred(streams_of[14], (NSEQ, SEQUENCE_LENGTH, MODEL_DIM), 1.0, 6.0, ((0, 8), (1, 4)))
    return {"tokens": tokens, "segments": segments, "routes": routes, "norm_in": norm_in, "q_weight": q_weight, "key_weight": key_weight, "value_weight": value_weight, "q_gain": q_gain, "k_gain": k_gain, "o_weight": o_weight, "norm_post": norm_post, "router": router, "expert_in": expert_in, "expert_out": expert_out, "cotangent": cotangent}


EPSILON = 1e-06
ROPE_BASE = 10000.0
EXACT_MATMUL = lax.Precision.HIGHEST

@jax.custom_vjp
def lowered_input(v):
    return lax.optimization_barrier(v.astype(jnp.bfloat16)).astype(jnp.float32)

@jax.custom_vjp
def lowered_reverse(v):
    return v

def low_keep(v):
    return (lowered_input(v), None)

def low_pass(kept, grad):
    return (grad,)

def back_keep(v):
    return (v, None)

def back_low(kept, grad):
    return (lowered_input(grad),)
lowered_input.defvjp(low_keep, low_pass)
lowered_reverse.defvjp(back_keep, back_low)

def rms_scale(values):
    return lax.rsqrt(lax.optimization_barrier(jnp.mean(values * values, axis=-1, keepdims=True)) + EPSILON)

def angles(positions):
    half_dim = HEAD_SIZE // 2
    frequency = jnp.exp(-(2.0 * jnp.arange(half_dim, dtype=jnp.float32) / HEAD_SIZE) * math.log(ROPE_BASE))
    phase_table = positions.astype(jnp.float32)[..., None] * frequency
    phase_table = jnp.concatenate([phase_table, phase_table], axis=-1)
    return (jnp.cos(phase_table), jnp.sin(phase_table))

def rotate(values, cosine_table, sine_table):
    half_dim = values.shape[-1] // 2
    turned = jnp.concatenate([-values[..., half_dim:], values[..., :half_dim]], axis=-1)
    return values * cosine_table + turned * sine_table

def layer_block(inputs, seg_ids, route_ids, norm_in, q_weight, key_weight, value_weight, q_gain, k_gain, o_weight, norm_post, router, expert_in, expert_out):
    starts = lax.optimization_barrier(jnp.sum((seg_ids[:, None, :] < seg_ids[:, :, None]).astype(jnp.int32), axis=2))
    places = jnp.arange(SEQUENCE_LENGTH, dtype=jnp.int32)
    positions = places[None, :] - starts
    cosine_table, sine_table = angles(positions)
    cosine_per_head = cosine_table[:, :, None, :]
    sine_per_head = sine_table[:, :, None, :]
    allowed = (seg_ids[:, None, :] == seg_ids[:, :, None]) & (places[None, None, :] <= places[None, :, None])
    normalized_input = lowered_input(inputs * rms_scale(inputs) * norm_in)
    query_rows = lowered_reverse(jnp.dot(normalized_input, q_weight, precision=EXACT_MATMUL)).reshape(SEQUENCE_COUNT, SEQUENCE_LENGTH, QUERY_HEADS, HEAD_SIZE)
    query_rows = lowered_input(rotate(query_rows * rms_scale(query_rows) * q_gain, cosine_per_head, sine_per_head))
    keys_unrotated = lowered_reverse(jnp.dot(normalized_input, key_weight, precision=EXACT_MATMUL)).reshape(SEQUENCE_COUNT, SEQUENCE_LENGTH, KEY_VALUE_HEADS, HEAD_SIZE)
    keys_rot = lowered_input(rotate(keys_unrotated * rms_scale(keys_unrotated) * k_gain, cosine_per_head, sine_per_head))
    values_lowered = lowered_input(lowered_reverse(jnp.dot(normalized_input, value_weight, precision=EXACT_MATMUL))).reshape(SEQUENCE_COUNT, SEQUENCE_LENGTH, KEY_VALUE_HEADS, HEAD_SIZE)
    query_grouping = QUERY_HEADS // KEY_VALUE_HEADS
    query_heads_split = query_rows.reshape(SEQUENCE_COUNT, SEQUENCE_LENGTH, KEY_VALUE_HEADS, query_grouping, HEAD_SIZE).transpose(2, 0, 3, 1, 4)
    key_heads_split = keys_rot.transpose(2, 0, 1, 3)
    value_heads_split = values_lowered.transpose(2, 0, 1, 3)
    score_scale = 1.0 / math.sqrt(HEAD_SIZE)

    def attend(packed):
        q_head, k_head, v_head = packed
        scores = lowered_reverse(jnp.einsum('sgqd,skd->sgqk', q_head, k_head, precision=EXACT_MATMUL) * score_scale)
        scores = jnp.where(allowed[:, None], scores, -1e+30)
        row_max = lax.optimization_barrier(jnp.max(scores, axis=-1, keepdims=True))
        raised = jnp.exp(scores - row_max)
        soft_weights = lowered_input(raised / lax.optimization_barrier(jnp.sum(raised, axis=-1, keepdims=True)))
        return jnp.einsum('sgqk,skd->sgqd', soft_weights, v_head, precision=EXACT_MATMUL)
    attended = lax.map(jax.checkpoint(attend), (query_heads_split, key_heads_split, value_heads_split))
    attended = attended.transpose(1, 3, 0, 2, 4).reshape(SEQUENCE_COUNT, SEQUENCE_LENGTH, QUERY_HEADS * HEAD_SIZE)
    attended = lowered_input(lowered_reverse(attended))
    middle = inputs + lowered_reverse(jnp.dot(attended, o_weight, precision=EXACT_MATMUL))
    post = lowered_input(middle * rms_scale(middle) * norm_post)
    logits = lowered_reverse(jnp.dot(post, router, precision=EXACT_MATMUL))
    picked = jnp.take_along_axis(logits, route_ids, axis=2)
    picked_max = lax.optimization_barrier(jnp.max(picked, axis=2, keepdims=True))
    raised_gates = jnp.exp(picked - picked_max)
    gate_vals = raised_gates / lax.optimization_barrier(jnp.sum(raised_gates, axis=2, keepdims=True))
    pieces = SEQUENCE_COUNT * N_GROUP
    flat_routes = route_ids.reshape(pieces, SHARD_LEN * TOPK)
    hit_table = (flat_routes[:, :, None] == jnp.arange(E, dtype=jnp.int32)[None, None, :]).astype(jnp.int32)
    slot_rank = lax.optimization_barrier(jnp.sum(jnp.cumsum(hit_table, axis=1) * hit_table, axis=2)) - 1
    slot_index = flat_routes * CAP + slot_rank
    slot_table = jnp.zeros((pieces, E * CAP), jnp.int32).at[jnp.arange(pieces, dtype=jnp.int32)[:, None], slot_index].set(jnp.arange(SHARD_LEN * TOPK, dtype=jnp.int32)[None, :] + 1)
    filled = slot_table > 0
    source_row = jnp.maximum(slot_table - 1, 0) // TOPK
    piece_post = post.reshape(pieces, SHARD_LEN, MODEL_DIM)
    slot_rows = jnp.take_along_axis(piece_post, source_row[:, :, None], axis=1)
    slot_rows = lowered_reverse(jnp.where(filled[:, :, None], slot_rows, 0.0)).reshape(pieces, E, CAP, MODEL_DIM)
    gate_up = lowered_reverse(jnp.einsum('pecd,edf->pecf', slot_rows, expert_in, precision=EXACT_MATMUL))
    hidden = lowered_input(jax.nn.silu(gate_up[..., :F]) * gate_up[..., F:])
    produced = lowered_input(lowered_reverse(jnp.einsum('pecf,efd->pecd', hidden, expert_out, precision=EXACT_MATMUL)))
    chosen = jnp.take_along_axis(produced.reshape(pieces, E * CAP, MODEL_DIM), slot_index[:, :, None], axis=1)
    chosen = chosen.reshape(SEQUENCE_COUNT, SEQUENCE_LENGTH, TOPK, MODEL_DIM)
    return middle + lax.optimization_barrier(jnp.sum(gate_vals[..., None] * chosen, axis=2))

def reference(tokens, segments, routes, norm_in, q_weight, key_weight, value_weight, q_gain, k_gain, o_weight, norm_post, router, expert_in, expert_out, cotangent):
    params = tuple((matrix.astype(jnp.float32) for matrix in (norm_in, q_weight, key_weight, value_weight, q_gain, k_gain, o_weight, norm_post, router, expert_in, expert_out)))
    blocks = NSEQ // SEQUENCE_COUNT
    token_blocks = tokens.astype(jnp.float32).reshape(blocks, SEQUENCE_COUNT, SEQUENCE_LENGTH, MODEL_DIM)
    seg_blocks = segments.reshape(blocks, SEQUENCE_COUNT, SEQUENCE_LENGTH)
    route_blocks = routes.reshape(blocks, SEQUENCE_COUNT, SEQUENCE_LENGTH, TOPK)
    cot_blocks = cotangent.astype(jnp.float32).reshape(blocks, SEQUENCE_COUNT, SEQUENCE_LENGTH, MODEL_DIM)

    def advance(running, packed):
        block_in, block_seg, block_route, block_cot = packed

        def forward(layer_in, *weights):
            return layer_block(layer_in, block_seg, block_route, *weights)
        produced, pullback = jax.vjp(forward, block_in, *params)
        gradients = pullback(block_cot)
        running = tuple((earlier + addend for earlier, addend in zip(running, gradients[1:])))
        return (running, (produced, gradients[0]))
    zeros_init = tuple((jnp.zeros(matrix.shape, jnp.float32) for matrix in params))
    totals, (produced, input_grads) = lax.scan(advance, zeros_init, (token_blocks, seg_blocks, route_blocks, cot_blocks))
    layer_out = produced.reshape(NSEQ, SEQUENCE_LENGTH, MODEL_DIM).astype(jnp.bfloat16)
    tokens_grad = input_grads.reshape(NSEQ, SEQUENCE_LENGTH, MODEL_DIM)
    return (layer_out, tokens_grad, totals[0], totals[1], totals[2], totals[3], totals[4], totals[5], totals[6], totals[7], totals[8], totals[9], totals[10])
```

```python
import functools
import math

import jax
import jax.numpy as jnp
from jax import lax
from jax.experimental import pallas as pl
from jax.experimental.pallas import tpu as pltpu
from jax.sharding import PartitionSpec as P

QUERY_HEADS = 16
KEY_VALUE_HEADS = 8
HEAD_SIZE = 64
E = 32
TOPK = 8
EPSILON = 1e-06
ROPE_BASE = 10000.0
LANES = 128
VMEM_BYTES = 58 * 1024 * 1024

BF = jnp.bfloat16
F32 = jnp.float32
I32 = jnp.int32


def mm(a, b):
    return lax.dot_general(a, b, (((1,), (0,)), ((), ())), preferred_element_type=F32)


def mm_nt(a, b):
    return lax.dot_general(a, b, (((1,), (1,)), ((), ())), preferred_element_type=F32)


def mm_tn(a, b):
    return lax.dot_general(a, b, (((0,), (0,)), ((), ())), preferred_element_type=F32)


def shape(dims, dtype):
    return jax.ShapeDtypeStruct(dims, dtype)


def call(kernel, grid, in_specs, out_specs, out_shape, scratch=(), prefetch=0, flops=0, nbytes=0, aliases=None):
    return pl.pallas_call(
        kernel,
        grid_spec=pltpu.PrefetchScalarGridSpec(
            num_scalar_prefetch=prefetch,
            grid=grid,
            in_specs=in_specs,
            out_specs=out_specs,
            scratch_shapes=list(scratch),
        ),
        out_shape=out_shape,
        input_output_aliases=aliases or {},
        compiler_params=pltpu.CompilerParams(vmem_limit_bytes=VMEM_BYTES),
        cost_estimate=pl.CostEstimate(flops=int(flops), bytes_accessed=int(nbytes), transcendentals=0),
    )


def row_block(rows, most=272):
    best = 16
    for size in range(16, most + 1, 16):
        if rows % size == 0:
            best = size
    return best


def swap_bit(value, axis, bit, size):
    return lax.ppermute(value, axis, [(i, i ^ bit) for i in range(size)])


def gather_relative(value, axis, size, order):
    have = {0: value}
    for bit in order:
        have.update({j ^ bit: swap_bit(held, axis, bit, size) for j, held in list(have.items())})
    return [have[j] for j in range(size)]


def scatter_relative(blocks, axis, size, order):
    have = dict(enumerate(blocks))
    for bit in order:
        for j in [j for j in have if j & bit]:
            arrived = swap_bit(have.pop(j), axis, bit, size)
            kept = have[j ^ bit].astype(F32) + arrived.astype(F32)
            have[j ^ bit] = kept.astype(BF)
    return have[0]


def place(blocks, me):
    count = blocks[0].shape[0]
    whole = jnp.zeros((count * len(blocks),) + blocks[0].shape[1:], blocks[0].dtype)
    for j, block in enumerate(blocks):
        start = ((me ^ j) * count,) + (0,) * (block.ndim - 1)
        whole = lax.dynamic_update_slice(whole, block, start)
    return whole


def rms(values):
    return lax.rsqrt(jnp.mean(values * values, axis=-1, keepdims=True) + EPSILON)


def lane_index():
    return lax.broadcasted_iota(I32, (1, LANES), 1)


def head_ones():
    row = lax.broadcasted_iota(I32, (LANES, LANES), 0) // HEAD_SIZE
    col = lax.broadcasted_iota(I32, (LANES, LANES), 1) // HEAD_SIZE
    return jnp.where(row == col, 1.0 / HEAD_SIZE, 0.0).astype(BF)


def head_mean(values, ones):
    high = values.astype(BF)
    low = (values - high.astype(F32)).astype(BF)
    return mm(high, ones) + mm(low, ones)


def half_swap(values):
    half = HEAD_SIZE // 2
    first = (lane_index() % HEAD_SIZE) < half
    return jnp.where(
        first, pltpu.roll(values, LANES - half, 1), pltpu.roll(values, half, 1)
    )


def project_kernel(x, gain, wq, wk, wv, gq, gk, cos, sin, normed, q_pre, k_pre, q_out, k_out, v_out):
    ones = head_ones()
    values = x[...].astype(F32)
    low = (values * rms(values) * gain[...]).astype(BF)
    normed[...] = low
    q_pre[...] = mm(low, wq[...])
    k_pre[...] = mm(low, wk[...])
    v_out[...] = mm(low, wv[...]).astype(BF)
    for pre, gains, out, factor in ((q_pre, gq, q_out, HEAD_SIZE**-0.5), (k_pre, gk, k_out, 1.0)):
        for start in range(0, pre.shape[1], LANES):
            block = pre[:, start : start + LANES]
            scale = lax.rsqrt(head_mean(block * block, ones) + EPSILON)
            block = block * scale * gains[...]
            turned = block * cos[...] + half_swap(block) * sin[...]
            out[:, start : start + LANES] = (turned * factor).astype(BF)


def project(x, gain, wq, wk, wv, gq, gk, cos, sin):
    rows, width = x.shape
    block = row_block(rows)
    qw, kw = wq.shape[1], wk.shape[1]

    def rowwise(columns):
        return pl.BlockSpec((block, columns), lambda i: (i, 0))

    def whole(array):
        return pl.BlockSpec(array.shape, lambda i: (0,) * array.ndim)

    return call(
        project_kernel,
        (rows // block,),
        [rowwise(width)] + [whole(a) for a in (gain, wq, wk, wv, gq, gk)] + [rowwise(LANES)] * 2,
        [rowwise(c) for c in (width, qw, kw, qw, kw, kw)],
        [
            shape((rows, width), BF),
            shape((rows, qw), F32),
            shape((rows, kw), F32),
            shape((rows, qw), BF),
            shape((rows, kw), BF),
            shape((rows, kw), BF),
        ],
        flops=2 * rows * width * (qw + 2 * kw),
        nbytes=rows * (2 * width + 8 * qw + 14 * kw),
    )(x, gain, wq, wk, wv, gq, gk, cos, sin)


def head_back(pre, gain, incoming, ones, cos, sin):
    turned = incoming * cos - half_swap(incoming) * sin
    scale = lax.rsqrt(head_mean(pre * pre, ones) + EPSILON)
    weighted = turned * gain
    inner = head_mean(weighted * pre, ones)
    grad = scale * weighted - pre * (scale * scale * scale) * inner
    return grad.astype(BF), jnp.sum(turned * pre * scale, axis=0, keepdims=True)


def project_back_kernel(
    dq, dk, dv, q_pre, k_pre, x, normed, grad_middle, gain, wq, wk, wv, gq, gk, cos, sin,
    tokens_grad, dwq, dwk, dwv, d_gain, d_gq, d_gk,
    low_q, low_k, acc_q, acc_k, acc_v,
):
    step = pl.program_id(0)

    @pl.when(step == 0)
    def _():
        for ref in (acc_q, acc_k, acc_v, d_gain, d_gq, d_gk):
            ref[...] = jnp.zeros_like(ref)

    ones = head_ones()
    for incoming, pre, gains, low, total, factor in (
        (dq, q_pre, gq, low_q, d_gq, HEAD_SIZE**-0.5),
        (dk, k_pre, gk, low_k, d_gk, 1.0),
    ):
        for start in range(0, pre.shape[1], LANES):
            span = slice(start, start + LANES)
            grad, terms = head_back(
                pre[:, span], gains[...], incoming[:, span] * factor, ones, cos[...], sin[...]
            )
            low[:, span] = grad
            total[...] += terms
    low_v = dv[...].astype(BF)
    grad_normed = mm_nt(low_q[...], wq[...]) + mm_nt(low_k[...], wk[...]) + mm_nt(low_v, wv[...])
    values = x[...].astype(F32)
    scale = rms(values)
    weighted = grad_normed * gain[...]
    inner = jnp.mean(weighted * values, axis=-1, keepdims=True)
    tokens_grad[...] = (
        grad_middle[...] + scale * weighted - values * (scale * scale * scale) * inner
    ).astype(BF)
    d_gain[...] += jnp.sum(grad_normed * values * scale, axis=0, keepdims=True)
    rows = normed[...]
    acc_q[...] += mm_tn(rows, low_q[...])
    acc_k[...] += mm_tn(rows, low_k[...])
    acc_v[...] += mm_tn(rows, low_v)

    @pl.when(step == pl.num_programs(0) - 1)
    def _():
        dwq[...] = acc_q[...].astype(BF)
        dwk[...] = acc_k[...].astype(BF)
        dwv[...] = acc_v[...].astype(BF)


def project_back(dq, dk, dv, q_pre, k_pre, x, normed, grad_middle, gain, wq, wk, wv, gq, gk, cos, sin):
    rows, width = x.shape
    block = row_block(rows)
    qw, kw = wq.shape[1], wk.shape[1]

    def rowwise(array):
        return pl.BlockSpec((block, array.shape[1]), lambda i: (i, 0))

    def whole(array):
        return pl.BlockSpec(array.shape, lambda i: (0,) * len(array.shape))

    outs = [
        shape((rows, width), BF),
        shape(wq.shape, BF),
        shape(wk.shape, BF),
        shape(wv.shape, BF),
        shape((1, width), F32),
        shape((1, LANES), F32),
        shape((1, LANES), F32),
    ]
    return call(
        project_back_kernel,
        (rows // block,),
        [rowwise(a) for a in (dq, dk, dv, q_pre, k_pre, x, normed, grad_middle)]
        + [whole(a) for a in (gain, wq, wk, wv, gq, gk)]
        + [rowwise(a) for a in (cos, sin)],
        [rowwise(outs[0])] + [whole(a) for a in outs[1:]],
        outs,
        scratch=[
            pltpu.VMEM((block, qw), BF),
            pltpu.VMEM((block, kw), BF),
            pltpu.VMEM(wq.shape, F32),
            pltpu.VMEM(wk.shape, F32),
            pltpu.VMEM(wv.shape, F32),
        ],
        flops=4 * rows * width * (qw + 2 * kw),
        nbytes=rows * (10 * width + 8 * qw + 16 * kw),
    )(dq, dk, dv, q_pre, k_pre, x, normed, grad_middle, gain, wq, wk, wv, gq, gk, cos, sin)


def doubled(block, head):
    values = block.astype(F32)
    keep = (lane_index() // HEAD_SIZE) == (head % 2)
    return jnp.where(keep, values, pltpu.roll(values, HEAD_SIZE, 1)).astype(BF)


def stacked(block):
    low = jnp.where(lane_index() < HEAD_SIZE, 1.0, 0.0).astype(BF)
    high = jnp.where(lane_index() < HEAD_SIZE, 0.0, 1.0).astype(BF)
    return jnp.concatenate([block * low, block * high], axis=0)


def unstacked(values):
    count = values.shape[0] // 2
    return jnp.where(lane_index() < HEAD_SIZE, values[:count], values[count:])


def raised_scores(queries, keys, first, place_of):
    scores = mm_nt(queries, keys)
    columns = lax.broadcasted_iota(I32, scores.shape, 1)
    first = jnp.concatenate([first, first], axis=0)
    place_of = jnp.concatenate([place_of, place_of], axis=0)
    return jnp.where((columns >= first) & (columns <= place_of), jnp.exp(scores), 0.0)


def query_blocks(rows, size=128):
    return [(start, min(size, rows - start)) for start in range(0, rows, size)]


def attend_kernel(causal, q, k, v, first, place_of, out, keys, values):
    head = pl.program_id(0)
    keys[...] = doubled(k[...], head)
    values[...] = doubled(v[...], head)
    for start, count in query_blocks(q.shape[0]):
        span = slice(start, start + count)
        end = start + count if causal else keys.shape[0]
        raised = raised_scores(stacked(q[span, :]), keys[:end, :], first[span, :], place_of[span, :])
        total = jnp.sum(raised, axis=-1, keepdims=True)
        summed = mm(raised.astype(BF), values[:end, :])
        out[span, :] = unstacked(summed * (1.0 / total)).astype(BF)


def attend(q, k, v, first, place_of):
    rows, full = q.shape[0], k.shape[0]
    heads = q.shape[1] // LANES
    qspec = pl.BlockSpec((rows, LANES), lambda j: (0, j))
    kspec = pl.BlockSpec((full, LANES), lambda j: (0, j // 2))
    column = pl.BlockSpec((rows, 1), lambda j: (0, 0))
    return call(
        functools.partial(attend_kernel, rows == full),
        (heads,),
        [qspec, kspec, kspec, column, column],
        qspec,
        shape(q.shape, BF),
        scratch=[pltpu.VMEM((full, LANES), BF)] * 2,
        flops=4 * rows * full * q.shape[1],
        nbytes=4 * q.size + 4 * k.size,
    )(q, k, v, first, place_of)


def attend_back_kernel(causal, q, k, v, grad, first, place_of, dq, dk, dv, keys, values, acc_k, acc_v):
    head = pl.program_id(0)
    keys[...] = doubled(k[...], head)
    values[...] = doubled(v[...], head)
    acc_k[...] = jnp.zeros_like(acc_k)
    acc_v[...] = jnp.zeros_like(acc_v)
    for start, count in query_blocks(q.shape[0]):
        span = slice(start, start + count)
        end = start + count if causal else keys.shape[0]
        queries = stacked(q[span, :])
        grads = stacked(grad[span, :])
        raised = raised_scores(queries, keys[:end, :], first[span, :], place_of[span, :])
        probs = raised * (1.0 / jnp.sum(raised, axis=-1, keepdims=True))
        grad_probs = mm_nt(grads, values[:end, :])
        inner = jnp.sum(probs * grad_probs, axis=-1, keepdims=True)
        grad_scores = (probs * (grad_probs - inner)).astype(BF)
        dq[span, :] = unstacked(mm(grad_scores, keys[:end, :]))
        acc_k[:end, :] += mm_tn(grad_scores, queries)
        acc_v[:end, :] += mm_tn(probs.astype(BF), grads)
    mine = (lane_index() // HEAD_SIZE) == (head % 2)
    for acc, out in ((acc_k, dk), (acc_v, dv)):
        total = acc[...] + pltpu.roll(acc[...], HEAD_SIZE, 1)
        out[...] = jnp.where(mine, total, out[...])


def attend_back(q, k, v, grad, first, place_of):
    rows, full = q.shape[0], k.shape[0]
    heads = q.shape[1] // LANES
    qspec = pl.BlockSpec((rows, LANES), lambda j: (0, j))
    kspec = pl.BlockSpec((full, LANES), lambda j: (0, j // 2))
    column = pl.BlockSpec((rows, 1), lambda j: (0, 0))
    return call(
        functools.partial(attend_back_kernel, rows == full),
        (heads,),
        [qspec, kspec, kspec, qspec, column, column],
        [qspec, kspec, kspec],
        [shape(q.shape, F32), shape(k.shape, F32), shape(k.shape, F32)],
        scratch=[pltpu.VMEM((full, LANES), BF)] * 2 + [pltpu.VMEM((full, LANES), F32)] * 2,
        flops=10 * rows * full * q.shape[1],
        nbytes=8 * q.size + 12 * k.size,
    )(q, k, v, grad, first, place_of)


def split_low(values):
    high = values.astype(BF)
    return high, (values - high.astype(F32)).astype(BF)


def router_kernel(x, att, wo, gain, router, routes, middle, post_a, post_b, gates):
    mid = x[...].astype(F32) + mm(att[...], wo[...])
    middle[...] = mid
    post = (mid * rms(mid) * gain[...]).astype(BF)
    logits = mm(post, router[...])
    lane = lane_index()
    named = routes[:, 0:1] == lane
    for k in range(1, TOPK):
        named = named | (routes[:, k : k + 1] == lane)
    logits = jnp.where(named, logits, -1e30)
    raised = jnp.where(named, jnp.exp(logits - jnp.max(logits, axis=-1, keepdims=True)), 0.0)
    gate = raised / jnp.sum(raised, axis=-1, keepdims=True)
    gates[...] = gate
    high, low = split_low(gate)
    low = pltpu.roll(low.astype(F32), E, 1).astype(BF)
    half = post_a.shape[1]
    post_a[...] = post[:, :half]
    post_b[:, :half] = post[:, half:]
    post_b[:, half:] = high + low


def route_rows(x, att, wo, gain, router, routes):
    rows, width = x.shape
    block = row_block(rows)
    outs = [
        shape((rows, width), F32),
        shape((rows, width // 2), BF),
        shape((rows, width // 2 + LANES), BF),
        shape((rows, LANES), F32),
    ]

    def rowwise(array):
        return pl.BlockSpec((block, array.shape[1]), lambda i: (i, 0))

    def whole(array):
        return pl.BlockSpec(array.shape, lambda i: (0,) * len(array.shape))

    return call(
        router_kernel,
        (rows // block,),
        [rowwise(x), rowwise(att), whole(wo), whole(gain), whole(router), rowwise(routes)],
        [rowwise(a) for a in outs],
        outs,
        flops=2 * rows * width * width,
        nbytes=rows * width * 12,
    )(x, att, wo, gain, router, routes)


def router_back_kernel(
    middle, back_a, back_b, gates, cot, gain, router, wo, att,
    grad_middle, grad_att, dwo, drouter, d_gain,
    acc_o, acc_r,
):
    step = pl.program_id(0)

    @pl.when(step == 0)
    def _():
        for ref in (acc_o, acc_r, d_gain):
            ref[...] = jnp.zeros_like(ref)

    mid = middle[...]
    scale = rms(mid)
    post = (mid * scale * gain[...]).astype(BF)
    half = back_a.shape[1]
    both = back_b[:, half:].astype(F32)
    grad_gates = both + pltpu.roll(both, LANES - E, 1)
    gate = gates[...]
    inner = jnp.sum(gate * grad_gates, axis=-1, keepdims=True)
    grad_logits = (gate * (grad_gates - inner)).astype(BF)
    grad_post = jnp.concatenate(
        [back_a[...].astype(F32), back_b[:, :half].astype(F32)], axis=1
    ) + mm_nt(grad_logits, router[...])
    weighted = grad_post * gain[...]
    mean = jnp.mean(weighted * mid, axis=-1, keepdims=True)
    total = cot[...].astype(F32) + scale * weighted - mid * (scale * scale * scale) * mean
    grad_middle[...] = total
    low = total.astype(BF)
    grad_att[...] = mm_nt(low, wo[...]).astype(BF)
    acc_o[...] += mm_tn(att[...], low)
    acc_r[...] += mm_tn(post, grad_logits)
    d_gain[...] += jnp.sum(grad_post * mid * scale, axis=0, keepdims=True)

    @pl.when(step == pl.num_programs(0) - 1)
    def _():
        dwo[...] = acc_o[...].astype(BF)
        drouter[...] = acc_r[...].astype(BF)


def route_back(middle, back_a, back_b, gates, cot, gain, router, wo, att):
    rows, width = middle.shape
    block = row_block(rows)
    outs = [
        shape((rows, width), F32),
        shape((rows, width), BF),
        shape(wo.shape, BF),
        shape(router.shape, BF),
        shape((1, width), F32),
    ]

    def rowwise(array):
        return pl.BlockSpec((block, array.shape[1]), lambda i: (i, 0))

    def whole(array):
        return pl.BlockSpec(array.shape, lambda i: (0,) * len(array.shape))

    return call(
        router_back_kernel,
        (rows // block,),
        [rowwise(a) for a in (middle, back_a, back_b, gates, cot)]
        + [whole(a) for a in (gain, router, wo)]
        + [rowwise(att)],
        [rowwise(a) for a in outs[:2]] + [whole(a) for a in outs[2:]],
        outs,
        scratch=[pltpu.VMEM(wo.shape, F32), pltpu.VMEM(router.shape, F32)],
        flops=4 * rows * width * width,
        nbytes=rows * width * 18,
    )(middle, back_a, back_b, gates, cot, gain, router, wo, att)


def slot_matrix(rank, cap):
    slots = lax.broadcasted_iota(I32, (cap, 1), 0).astype(F32)
    parts = [
        jnp.where(rank[e : e + 1, :] == slots, 1.0, 0.0).astype(BF) for e in range(rank.shape[0])
    ]
    return jnp.concatenate(parts, axis=0)


def dispatch_kernel(n_in, piece_of, base, rank, part_a, part_b, *refs):
    gated = n_in > 1
    slots = refs[n_in]
    experts, _, cap, width = slots.shape
    half = part_a.shape[2]
    chosen = slot_matrix(rank[0], cap)
    slots[:, 0, :, :half] = mm(chosen, part_a[0]).astype(BF).reshape(experts, cap, half)
    rest = mm(chosen, part_b[0])
    slots[:, 0, :, half:] = rest[:, : width - half].astype(BF).reshape(experts, cap, width - half)
    if rest.shape[1] > width - half:
        gates = refs[n_in + 1]
        both = rest[:, width - half :]
        lane = lane_index()
        for e in range(experts):
            mine = base[0] + e
            picked = (lane == mine) | (lane == mine + E)
            total = jnp.sum(
                jnp.where(picked, both[e * cap : (e + 1) * cap], 0.0), axis=-1, keepdims=True
            )
            gates[e, 0] = jnp.broadcast_to(total, (cap, LANES))


def dispatch(piece_of, base, rank, part_a, part_b, cap, width, earlier):
    pieces, experts, length = rank.shape
    count = part_a.shape[0]
    gated = part_a.shape[2] + part_b.shape[2] > width

    def token_spec(array):
        return pl.BlockSpec((1,) + array.shape[1:], lambda i, piece_of, base: (i, 0, 0))

    def slot_spec(columns):
        return pl.BlockSpec(
            (experts, 1, cap, columns), lambda i, piece_of, base: (0, piece_of[i], 0, 0)
        )

    outs = [shape((experts, pieces, cap, width), BF)]
    out_specs = [slot_spec(width)]
    if gated:
        outs.append(shape((experts, pieces, cap, LANES), F32))
        out_specs.append(slot_spec(LANES))
    earlier = list(earlier or [])
    return call(
        functools.partial(dispatch_kernel, len(earlier)),
        (count,),
        [
            pl.BlockSpec((1, experts, length), lambda i, piece_of, base: (piece_of[i], 0, 0)),
            token_spec(part_a),
            token_spec(part_b),
        ]
        + [pl.BlockSpec(memory_space=pl.ANY)] * len(earlier),
        out_specs,
        outs,
        prefetch=2,
        aliases={5 + i: i for i in range(len(earlier))},
        flops=2 * count * experts * cap * length * width,
        nbytes=2 * count * width * (length + experts * cap),
    )(piece_of, base, rank, part_a, part_b, *earlier)


def combine_kernel(rank, out_rows, back_rows, gate_rows, out_a, out_b, back_a, back_b):
    experts, _, cap, width = out_rows.shape
    half = out_a.shape[2]
    columns = experts * cap
    col = lax.broadcasted_iota(I32, (1, columns), 1)
    expert_row = lax.broadcasted_iota(I32, (experts, 1), 0)
    spread = jnp.where(col // cap == expert_row, 1.0, 0.0).astype(BF)
    wanted = (col % cap).astype(F32)
    chosen = jnp.where(mm(rank[0].astype(BF), spread) == wanted, 1.0, 0.0).astype(BF)
    flat = out_rows[...].reshape(columns, width)
    summed = mm(chosen, flat).astype(BF)
    out_a[0] = summed[:, :half]
    out_b[0] = summed[:, half:]
    summed = mm(chosen, back_rows[...].reshape(columns, width)).astype(BF)
    back_a[0] = summed[:, :half]
    back_b[0, :, :half] = summed[:, half:]
    back_b[0, :, half:] = mm(chosen, gate_rows[...].reshape(columns, LANES)).astype(BF)


def combine(piece_of, rank, out_rows, back_rows, gate_rows):
    experts, pieces, cap, width = out_rows.shape
    _, length, _ = rank.shape
    count = piece_of.shape[0]
    half = width // 2

    def slot_spec(columns):
        return pl.BlockSpec((experts, 1, cap, columns), lambda i, piece_of: (0, piece_of[i], 0, 0))

    def token_spec(columns):
        return pl.BlockSpec((1, length, columns), lambda i, piece_of: (i, 0, 0))

    widths = [half, half, half, half + LANES]
    return call(
        lambda piece_of, *refs: combine_kernel(*refs),
        (count,),
        [
            pl.BlockSpec((1, length, experts), lambda i, piece_of: (piece_of[i], 0, 0)),
            slot_spec(width),
            slot_spec(width),
            slot_spec(LANES),
        ],
        [token_spec(c) for c in widths],
        [shape((count, length, c), BF) for c in widths],
        prefetch=1,
        flops=4 * count * experts * cap * length * width,
        nbytes=4 * count * width * (length + experts * cap),
    )(piece_of, rank, out_rows, back_rows, gate_rows)


def expert_kernel(n_in, first, base, rows, grads, gates, w_in, w_out, *refs):
    outs, backs, gate_grads, dw_in, dw_out, acc_in, acc_out = refs[n_in:]
    step = pl.program_id(1)
    _, pieces, cap, width = rows.shape
    count = pieces * cap
    hidden_width = w_out.shape[1]

    @pl.when(step == 0)
    def _():
        acc_in[...] = jnp.zeros_like(acc_in)
        acc_out[...] = jnp.zeros_like(acc_out)

    x = rows[...].reshape(count, width)
    grad = grads[...].reshape(count, width)
    gate = gates[...].reshape(count, LANES)[:, 0:1]
    gate_up = mm(x, w_in[0])
    a = gate_up[:, :hidden_width]
    u = gate_up[:, hidden_width:]
    sigma = 1.0 / (1.0 + jnp.exp(-a))
    silu = a * sigma
    hidden = silu * u
    low = hidden.astype(BF)
    outs[...] = (mm(low, w_out[0]) * gate).astype(BF).reshape(outs.shape)
    grad_hidden = mm_nt(grad, w_out[0])
    inner = jnp.sum(low.astype(F32) * grad_hidden, axis=-1, keepdims=True)
    grad_hidden = grad_hidden * gate
    grad_a = grad_hidden * u * (sigma * (1.0 + a * (1.0 - sigma)))
    grad_u = grad_hidden * silu
    grad_gate_up = jnp.concatenate([grad_a, grad_u], axis=1).astype(BF)
    backs[...] = mm_nt(grad_gate_up, w_in[0]).astype(BF).reshape(backs.shape)
    acc_in[...] += mm_tn(x, grad_gate_up)
    acc_out[...] += mm_tn((hidden * gate).astype(BF), grad)
    lane = lane_index()
    mine = base[0] + first + pl.program_id(0)
    high = inner.astype(BF).astype(F32)
    both = jnp.where(lane == mine, high, jnp.where(lane == mine + E, inner - high, 0.0))
    gate_grads[...] = both.astype(BF).reshape(gate_grads.shape)

    @pl.when(step == pl.num_programs(1) - 1)
    def _():
        dw_in[0] = acc_in[...].astype(BF)
        dw_out[0] = acc_out[...].astype(BF)


def run_experts(first, number, base, rows, grads, gates, w_in, w_out, earlier):
    experts, pieces, cap, width = rows.shape
    group = max(1, 384 // cap)
    hidden_width = w_out.shape[1]

    def slot_spec(columns):
        return pl.BlockSpec((1, group, cap, columns), lambda e, c, base: (first + e, c, 0, 0))

    def weight_spec(array, offset):
        return pl.BlockSpec((1,) + array.shape[1:], lambda e, c, base: (offset + e, 0, 0))

    outs = [
        shape(rows.shape, BF),
        shape(rows.shape, BF),
        shape((experts, pieces, cap, LANES), BF),
        shape((number,) + w_in.shape[1:], BF),
        shape((number,) + w_out.shape[1:], BF),
    ]
    earlier = list(earlier or [])
    return call(
        functools.partial(lambda n_in, base, *refs: expert_kernel(n_in, first, base, *refs), len(earlier)),
        (number, pieces // group),
        [slot_spec(width), slot_spec(width), slot_spec(LANES), weight_spec(w_in, first), weight_spec(w_out, first)]
        + [pl.BlockSpec(memory_space=pl.ANY)] * len(earlier),
        [slot_spec(width), slot_spec(width), slot_spec(LANES), weight_spec(outs[3], 0), weight_spec(outs[4], 0)],
        outs,
        scratch=[pltpu.VMEM(w_in.shape[1:], F32), pltpu.VMEM(w_out.shape[1:], F32)],
        prefetch=1,
        aliases={6 + i: i for i in range(len(earlier))},
        flops=18 * number * pieces * cap * width * hidden_width,
        nbytes=number * (8 * pieces * cap * width + 12 * width * hidden_width),
    )(base, rows, grads, gates, w_in, w_out, *earlier)


def per_device(
    tokens, segments, routes, norm_in, q_weight, key_weight, value_weight, q_gain, k_gain,
    o_weight, norm_post, router, expert_in, expert_out, cotangent,
):
    size = lax.axis_size("group")
    me = lax.axis_index("group")
    sequences, length, width = tokens.shape
    half = width // 2
    parts = size // sequences
    rows = sequences * length
    full = length * size
    experts = expert_in.shape[0]
    cap = (length * TOPK * 4 // (3 * E) + 7) // 8 * 8
    bits = [1 << b for b in range(size.bit_length() - 1)]
    order_a, order_b = bits, bits[::-1]
    part, sequence = me // sequences, me % sequences
    exchange = [[q * sequences + s for s in range(sequences)] for q in range(parts)]
    fellows = [[q * sequences + s for q in range(parts)] for s in range(sequences)]

    def regroup(value):
        return lax.all_to_all(
            value, "group", 0, 0, tiled=True, axis_index_groups=exchange if parts > 1 else None
        )

    def gathered(value, order):
        return gather_relative(value, "group", size, order)

    x = regroup(tokens).reshape(rows, width)
    kv_weight = jnp.concatenate([key_weight, value_weight], axis=1)
    wq = place(gathered(q_weight, order_a), me)
    wkv = place(gathered(kv_weight, order_b), me)
    key_width = key_weight.shape[1]
    wk, wv = wkv[:, :key_width], wkv[:, key_width:]
    small = jnp.concatenate([norm_in, norm_post, q_gain, k_gain])
    small = lax.all_gather(small, "group").astype(F32)
    n_norm, n_gain = norm_in.shape[0], q_gain.shape[0]
    cuts = [0, n_norm, 2 * n_norm, 2 * n_norm + n_gain, 2 * n_norm + 2 * n_gain]
    gain_in, gain_post, gain_q, gain_k = (
        small[:, a:b].reshape(1, -1) for a, b in zip(cuts[:-1], cuts[1:])
    )
    gain_q = jnp.concatenate([gain_q, gain_q], axis=1)
    gain_k = jnp.concatenate([gain_k, gain_k], axis=1)

    seg_all = lax.all_gather(segments, "group", axis=1, tiled=True)
    seg_full = lax.dynamic_index_in_dim(seg_all, sequence, 0, keepdims=False)
    place_of = part * rows + jnp.arange(rows, dtype=I32)
    seg_own = lax.dynamic_slice_in_dim(seg_full, part * rows, rows)
    first = jnp.sum((seg_full[None, :] < seg_own[:, None]).astype(I32), axis=1)
    frequency = jnp.exp(
        -(2.0 * jnp.arange(HEAD_SIZE // 2, dtype=F32) / HEAD_SIZE) * math.log(ROPE_BASE)
    )
    phase = (place_of - first).astype(F32)[:, None] * frequency
    cos, sin = jnp.cos(phase), jnp.sin(phase)
    cos = jnp.concatenate([cos] * 4, axis=1)
    sin = jnp.concatenate([-sin, sin, -sin, sin], axis=1)
    first, place_of = first[:, None], place_of[:, None]

    routes_all = lax.all_gather(routes, "group")
    pieces = size * sequences
    base = me * experts
    local = routes_all.reshape(pieces, length, TOPK) - base
    hit = jnp.zeros((pieces, length, experts), jnp.bool_)
    for k in range(TOPK):
        hit = hit | (local[:, :, k : k + 1] == jnp.arange(experts, dtype=I32))
    before = (jnp.arange(length)[:, None] > jnp.arange(length)[None, :]).astype(BF)
    rank = jnp.einsum("ij,pje->pie", before, hit.astype(BF), preferred_element_type=F32)
    rank = jnp.where(hit, rank, -1.0)
    rank_rows = rank.transpose(0, 2, 1)
    base = base.reshape(1)
    own_routes = lax.dynamic_slice(
        routes_all, (part * sequences, sequence, 0, 0), (sequences, 1, length, TOPK)
    ).reshape(rows, TOPK)

    def sequence_pieces(j):
        other = me ^ j
        return (other // sequences * sequences + jnp.arange(sequences, dtype=I32)) * sequences + other % sequences

    def position_pieces(j):
        return (me ^ j) * sequences + jnp.arange(sequences, dtype=I32)

    cot_a = gathered(cotangent[:, :, :half], order_a)
    cot_b = gathered(cotangent[:, :, half:], order_b)

    normed, q_pre, k_pre, queries, keys, values = project(
        x, gain_in, wq, wk, wv, gain_q, gain_k, cos, sin
    )
    if parts > 1:
        keys = lax.all_gather(keys, "group", axis=0, tiled=True, axis_index_groups=fellows)
        values = lax.all_gather(values, "group", axis=0, tiled=True, axis_index_groups=fellows)
    attended = attend(queries, keys, values, first, place_of)

    wo_router = jnp.concatenate(
        [o_weight, router, jnp.zeros((router.shape[0], LANES - E), BF)], axis=1
    )
    wo = jnp.concatenate(
        [
            place(gathered(wo_router[:, :half], order_a), me),
            place(gathered(wo_router[:, half:], order_b), me),
        ],
        axis=1,
    )
    wo, router_full = wo[:, :width], wo[:, width:]
    middle, post_a, post_b, gates = route_rows(x, attended, wo, gain_post, router_full, own_routes)

    slot_grads = None
    for j in range(size):
        slot_grads = dispatch(
            position_pieces(j), base, rank_rows, cot_a[j], cot_b[j], cap, width, slot_grads
        )
    posts_a = gathered(post_a.reshape(sequences, length, -1), order_a)
    posts_b = gathered(post_b.reshape(sequences, length, -1), order_b)
    slot_rows = None
    for j in range(size):
        slot_rows = dispatch(
            sequence_pieces(j), base, rank_rows, posts_a[j], posts_b[j], cap, width, slot_rows
        )
    made = None
    grads_in, grads_out = [], []
    step = 2 if experts % 2 == 0 else 1
    for e in range(0, experts, step):
        *made, grad_in, grad_out = run_experts(
            e, step, base, slot_rows[0], slot_grads[0], slot_rows[1], expert_in, expert_out, made
        )
        grads_in.append(lax.psum(grad_in, "replica").astype(F32))
        grads_out.append(lax.psum(grad_out, "replica").astype(F32))
    expert_in_grad = jnp.concatenate(grads_in, axis=0)
    expert_out_grad = jnp.concatenate(grads_out, axis=0)

    combined = [combine(sequence_pieces(j), rank, *made) for j in range(size)]
    out_a, out_b, back_a, back_b = (
        scatter_relative([c[i] for c in combined], "group", size, order).reshape(rows, -1)
        for i, order in ((0, order_a), (1, order_b), (2, order_a), (3, order_b))
    )
    summed = jnp.concatenate([out_a, out_b], axis=1).astype(F32)
    layer_out = regroup((middle + summed).astype(BF).reshape(sequences, length, width))

    own_cot = []
    for cot in (cot_a, cot_b):
        stack = jnp.stack([lax.dynamic_index_in_dim(c, sequence, 0, keepdims=False) for c in cot])
        own_cot.append(
            jnp.concatenate(
                [
                    lax.dynamic_index_in_dim(stack, (part * sequences + i) ^ me, 0, keepdims=False)
                    for i in range(sequences)
                ],
                axis=0,
            )
        )
    own_cot = jnp.concatenate(own_cot, axis=1)
    grad_middle, grad_att, dwo, drouter, d_norm_post = route_back(
        middle, back_a, back_b, gates, own_cot, gain_post, router_full, wo, attended
    )
    dq, dk, dv = attend_back(queries, keys, values, grad_att, first, place_of)
    if parts > 1:
        dk, dv = (
            lax.psum_scatter(
                d.astype(BF), "group", scatter_dimension=0, tiled=True, axis_index_groups=fellows
            ).astype(F32)
            for d in (dk, dv)
        )
    tokens_grad, dwq, dwk, dwv, d_norm_in, d_gq, d_gk = project_back(
        dq, dk, dv, q_pre, k_pre, x, normed, grad_middle, gain_in, wq, wk, wv, gain_q, gain_k, cos, sin
    )
    tokens_grad = regroup(tokens_grad.reshape(sequences, length, width)).astype(F32)

    big = jnp.concatenate([dwq, dwk, dwv, dwo, drouter], axis=1)
    big = lax.psum_scatter(big, "group", scatter_dimension=0, tiled=True)
    big = lax.psum(big, "replica").astype(F32)
    cuts = [0]
    for piece in (dwq, dwk, dwv, dwo):
        cuts.append(cuts[-1] + piece.shape[1])
    cuts.append(cuts[-1] + E)
    shard_q, shard_k, shard_v, shard_o, shard_router = (
        big[:, a:b] for a, b in zip(cuts[:-1], cuts[1:])
    )
    d_gq = d_gq[:, :HEAD_SIZE] + d_gq[:, HEAD_SIZE:]
    d_gk = d_gk[:, :HEAD_SIZE] + d_gk[:, HEAD_SIZE:]
    vectors = jnp.concatenate([d_norm_in, d_norm_post, d_gq, d_gk], axis=1)[0]
    vectors = lax.psum(vectors, ("group", "replica"))

    def own_part(start, count):
        return lax.dynamic_slice_in_dim(vectors, start + me * (count // size), count // size)

    return (
        layer_out,
        tokens_grad,
        own_part(0, width),
        shard_q,
        shard_k,
        shard_v,
        own_part(2 * width, HEAD_SIZE),
        own_part(2 * width + HEAD_SIZE, HEAD_SIZE),
        shard_o,
        own_part(width, width),
        shard_router,
        expert_in_grad,
        expert_out_grad,
    )


def solution(mesh):
    row, column = P("group", None), P("group")
    stream = P("replica", "group", None)
    expert = P("group", None, None)
    return jax.shard_map(
        per_device,
        mesh=mesh,
        in_specs=(
            stream, P("replica", "group"), stream, column, row, row, row, column, column,
            row, column, row, expert, expert, stream,
        ),
        out_specs=(
            stream, stream, column, row, row, row, column, column, row, column, row, expert, expert,
        ),
        check_vma=False,
    )
```

```python
import functools
import math

import jax
import jax.numpy as jnp
from jax import lax
from jax.experimental import pallas as pl
from jax.experimental.pallas import tpu as pltpu
from jax.sharding import PartitionSpec as P

QUERY_HEADS = 16
KEY_VALUE_HEADS = 8
HEAD_SIZE = 64
E = 32
TOPK = 8
EPSILON = 1e-06
ROPE_BASE = 10000.0
LANES = 128
VMEM_BYTES = 58 * 1024 * 1024

BF = jnp.bfloat16
F32 = jnp.float32
I32 = jnp.int32


def mm(a, b):
    return lax.dot_general(a, b, (((1,), (0,)), ((), ())), preferred_element_type=F32)


def mm_nt(a, b):
    return lax.dot_general(a, b, (((1,), (1,)), ((), ())), preferred_element_type=F32)


def mm_tn(a, b):
    return lax.dot_general(a, b, (((0,), (0,)), ((), ())), preferred_element_type=F32)


def shape(dims, dtype):
    return jax.ShapeDtypeStruct(dims, dtype)


def call(kernel, grid, in_specs, out_specs, out_shape, scratch=(), prefetch=0, flops=0, nbytes=0, aliases=None):
    return pl.pallas_call(
        kernel,
        grid_spec=pltpu.PrefetchScalarGridSpec(
            num_scalar_prefetch=prefetch,
            grid=grid,
            in_specs=in_specs,
            out_specs=out_specs,
            scratch_shapes=list(scratch),
        ),
        out_shape=out_shape,
        input_output_aliases=aliases or {},
        compiler_params=pltpu.CompilerParams(vmem_limit_bytes=VMEM_BYTES),
        cost_estimate=pl.CostEstimate(flops=int(flops), bytes_accessed=int(nbytes), transcendentals=0),
    )


def row_block(rows, most=272):
    best = 16
    for size in range(16, most + 1, 16):
        if rows % size == 0:
            best = size
    return best


def swap_bit(value, axis, bit, size):
    return lax.ppermute(value, axis, [(i, i ^ bit) for i in range(size)])


def gather_relative(value, axis, size, order):
    value = value[None]
    for bit in order:
        value = jnp.concatenate([value, swap_bit(value, axis, bit, size)], axis=0)
    return value


def relative_order(order):
    indices = [0]
    for bit in order:
        indices = indices + [j ^ bit for j in indices]
    return indices


def after(value, *earlier):
    return lax.optimization_barrier((value,) + earlier)[0]


def add_low(a, b):
    return (a.astype(F32) + b.astype(F32)).astype(BF)


class Plan:
    def __init__(self, token):
        self.token, self.now, self.free, self.flows, self.count = token, 0.0, {}, [], 0

    def tie(self, value):
        held, tree = jax.tree.flatten(value)
        return jax.tree.unflatten(tree, lax.optimization_barrier((*held, self.token))[:-1])

    def note(self, *values, span=0.0):
        self.token = after(self.token, *values)
        self.now += span

    def start(self, flow, arrived=None):
        try:
            link, span, arrived = flow.send(arrived)
        except StopIteration:
            return
        self.put(link, span, lambda: self.start(flow, arrived))

    def put(self, link, span, act):
        self.free[link] = max(self.now, self.free.get(link, 0.0)) + span
        self.count += 1
        self.flows.append((self.free[link] + 5.0, self.count, act))

    def run(self, span):
        self.now += span
        while self.flows and min(f[0] for f in self.flows) <= self.now:
            self.advance()

    def advance(self):
        first = min(self.flows, key=lambda f: f[:2])
        self.flows.remove(first)
        self.now = max(self.now, first[0])
        first[2]()

    def drain(self, done):
        while not done():
            self.advance()


def travel(value, fast=False):
    nbytes = value.size * value.dtype.itemsize
    return nbytes / 480e3 if fast else nbytes / 43e3


def add_kernel(a, b, total):
    total[...] = add_low(a[...], b[...])


def pick_kernel(second, a, b, out):
    out[...] = jnp.where(jnp.broadcast_to(second[0], out.shape) == 1, b[...], a[...])


def add_blocks(a, b):
    count, rows, columns = a.shape
    depth = row_block(rows, 256)
    spec = pl.BlockSpec((1, depth, columns), lambda i, j: (i, j, 0))
    return call(
        add_kernel, (count, rows // depth), [spec, spec], spec, shape(a.shape, BF),
        flops=a.size, nbytes=6 * a.size,
    )(a, b)


def pick_blocks(second, a, b):
    count, rows, columns = a.shape
    depth = row_block(rows, 256)

    def take(k):
        def index(i, j, second):
            on = (second[0] == k).astype(I32)
            return i * on, j * on, 0

        return pl.BlockSpec((1, depth, columns), index)

    return call(
        pick_kernel,
        (count, rows // depth),
        [take(0), take(1)],
        pl.BlockSpec((1, depth, columns), lambda i, j, second: (i, j, 0)),
        shape(a.shape, BF),
        prefetch=1,
        flops=a.size,
        nbytes=4 * a.size,
    )(second.astype(I32).reshape(1), a, b)


def line_flow(plan, value, axis, size, result):
    chips = size // 2
    middle = chips // 2
    chip = lax.axis_index(axis) // 2
    large = value.ndim == 3
    add = add_blocks if large else add_low
    span = 4.0 if large else 2.0

    def send(held, pairs):
        both = [(2 * a + core, 2 * b + core) for a, b in pairs for core in range(2)]
        return lax.ppermute(held, axis, both)

    for k in range(1, middle):
        arrived = yield "in", travel(value), send(value, [(k - 1, k), (chips - k, chips - 1 - k)])
        value = add(value, plan.tie(arrived))
        plan.note(value, span=span)
    arrived = yield "across", travel(value), send(value, [(middle - 1, middle), (middle, middle - 1)])
    value = add(value, plan.tie(arrived))
    plan.note(value, span=span)
    for k in range(middle - 1, 0, -1):
        arrived = yield "out", travel(value), send(value, [(k, k - 1), (chips - 1 - k, chips - k)])
        outer = (chip == k - 1) | (chip == chips - k)
        if large:
            value = pick_blocks(outer, value, plan.tie(arrived))
        else:
            value = lax.select(outer, plan.tie(arrived), value)
        plan.note(value, span=span)
    result.append(value)


def scatter_flow(plan, link, have, order, axis, size, result):
    for bit in order:
        moving = [j for j in range(size) if j in have and j & bit]
        sent = swap_bit(jnp.stack([have.pop(j) for j in moving]), axis, bit, size)
        arrived = yield link, travel(sent), sent
        arrived = plan.tie(arrived)
        for k, j in enumerate(moving):
            have[j ^ bit] = add_low(have[j ^ bit], arrived[k])
        plan.note(*[have[j ^ bit] for j in moving], span=5.0)
    result.append(have[0])


def gather_flow(plan, value, order, axis, size, result):
    held = value[None]
    where = {0: (held, 0)}
    for level, bit in enumerate(order):
        depth = held.shape[0]
        if level + 1 < len(order):
            both = jnp.zeros((2 * depth,) + held.shape[1:], held.dtype)
            both = lax.dynamic_update_slice(both, held, (0,) * held.ndim)
        arrived = yield bit, travel(held), swap_bit(held, axis, bit, size)
        arrived = plan.tie(arrived)
        indices = relative_order(order[:level])
        where.update({j ^ bit: (arrived, k) for k, j in enumerate(indices)})
        if level + 1 < len(order):
            held = lax.dynamic_update_slice(both, arrived, (depth,) + (0,) * (held.ndim - 1))
            where = {j: (held, k) for k, j in enumerate(indices + [j ^ bit for j in indices])}
            plan.note(held, span=2.0)
        else:
            plan.note(arrived)
    result.update(where)


def place(blocks, indices, me):
    whole = jnp.zeros_like(blocks)
    for k, j in enumerate(indices):
        start = (me ^ j,) + (0,) * (blocks.ndim - 1)
        whole = lax.dynamic_update_slice(whole, blocks[k : k + 1], start)
    return whole


def rms(values):
    return lax.rsqrt(jnp.mean(values * values, axis=-1, keepdims=True) + EPSILON)


def lane_index():
    return lax.broadcasted_iota(I32, (1, LANES), 1)


def head_ones():
    row = lax.broadcasted_iota(I32, (LANES, LANES), 0) // HEAD_SIZE
    col = lax.broadcasted_iota(I32, (LANES, LANES), 1) // HEAD_SIZE
    return jnp.where(row == col, 1.0 / HEAD_SIZE, 0.0).astype(BF)


def head_mean(values, ones):
    high = values.astype(BF)
    low = (values - high.astype(F32)).astype(BF)
    return mm(high, ones) + mm(low, ones)


def half_swap(values):
    half = HEAD_SIZE // 2
    first = (lane_index() % HEAD_SIZE) < half
    return jnp.where(
        first, pltpu.roll(values, LANES - half, 1), pltpu.roll(values, half, 1)
    )


def blocks_of(ref, order, depth):
    return [
        ref[:, pl.ds(pl.multiple_of(order[k] * depth, depth), depth)] for k in range(order.shape[0])
    ]


def mm_blocks(ref, order, weight):
    parts = blocks_of(ref, order, weight.shape[1])
    return sum(mm(part, weight[k]) for k, part in enumerate(parts))


def weight_spec(weight, width, column):
    return pl.BlockSpec(weight.shape[:2] + (width,), lambda i, *_: (0, 0, column))


def project_kernel(
    order_a, order_b, x, gain, wq, wkv, gq, gk, cos, sin, normed, q_pre, k_pre, q_out, k_out, v_out
):
    ones = head_ones()
    values = x[...].astype(F32)
    normed[...] = (values * rms(values) * gain[...]).astype(BF)
    q_pre[...] = mm_blocks(normed, order_a, wq)
    both = mm_blocks(normed, order_b, wkv)
    k_pre[...] = both[:, : k_pre.shape[1]]
    v_out[...] = both[:, k_pre.shape[1] :].astype(BF)
    for pre, gains, out, factor in ((q_pre, gq, q_out, HEAD_SIZE**-0.5), (k_pre, gk, k_out, 1.0)):
        for start in range(0, pre.shape[1], LANES):
            block = pre[:, start : start + LANES]
            scale = lax.rsqrt(head_mean(block * block, ones) + EPSILON)
            block = block * scale * gains[...]
            turned = block * cos[...] + half_swap(block) * sin[...]
            out[:, start : start + LANES] = (turned * factor).astype(BF)


def project(orders, x, gain, weight_a, weight_b, gq, gk, cos, sin):
    rows, width = x.shape
    block = row_block(rows)
    qw, kw = QUERY_HEADS * HEAD_SIZE, KEY_VALUE_HEADS * HEAD_SIZE

    def rowwise(columns):
        return pl.BlockSpec((block, columns), lambda i, *_: (i, 0))

    def whole(array):
        return pl.BlockSpec(array.shape, lambda i, *_: (0,) * array.ndim)

    return call(
        project_kernel,
        (rows // block,),
        [rowwise(width), whole(gain), weight_spec(weight_a, qw, 0), weight_spec(weight_b, 2 * kw, 0)]
        + [whole(gq), whole(gk)]
        + [rowwise(LANES)] * 2,
        [rowwise(c) for c in (width, qw, kw, qw, kw, kw)],
        [
            shape((rows, width), BF),
            shape((rows, qw), F32),
            shape((rows, kw), F32),
            shape((rows, qw), BF),
            shape((rows, kw), BF),
            shape((rows, kw), BF),
        ],
        prefetch=2,
        flops=2 * rows * width * (qw + 2 * kw),
        nbytes=rows * (2 * width + 8 * qw + 14 * kw),
    )(*orders, x, gain, weight_a, weight_b, gq, gk, cos, sin)


def head_back(pre, gain, incoming, ones, cos, sin):
    turned = incoming * cos - half_swap(incoming) * sin
    scale = lax.rsqrt(head_mean(pre * pre, ones) + EPSILON)
    weighted = turned * gain
    inner = head_mean(weighted * pre, ones)
    grad = scale * weighted - pre * (scale * scale * scale) * inner
    return grad.astype(BF), jnp.sum(turned * pre * scale, axis=0, keepdims=True)


def project_back_kernel(
    starts, order_a, order_b,
    dq, dk, dv, q_pre, k_pre, x, normed, grad_middle, gain, wq, wkv, gq, gk, cos, sin,
    tokens_grad, keep_a, keep_b, send_a, send_b,
    low_q, low_kv, grad_normed, acc_q, acc_kv, acc_x, d_gq, d_gk,
):
    step = pl.program_id(0)
    key_width = dk.shape[1]

    @pl.when(step == 0)
    def _():
        for ref in (acc_q, acc_kv, acc_x, d_gq, d_gk):
            ref[...] = jnp.zeros_like(ref)

    ones = head_ones()
    for incoming, pre, gains, low, total, factor in (
        (dq, q_pre, gq, low_q, d_gq, HEAD_SIZE**-0.5),
        (dk, k_pre, gk, low_kv, d_gk, 1.0),
    ):
        for start in range(0, pre.shape[1], LANES):
            span = slice(start, start + LANES)
            grad, terms = head_back(
                pre[:, span], gains[...], incoming[:, span] * factor, ones, cos[...], sin[...]
            )
            low[:, span] = grad
            total[0:1, :] += terms
    low_kv[:, key_width:] = dv[...].astype(BF)
    depth = wq.shape[1]
    for k in range(wq.shape[0]):
        span = pl.ds(pl.multiple_of(order_a[k] * depth, depth), depth)
        grad_normed[:, span] = mm_nt(low_q[...], wq[k])
    for k in range(wkv.shape[0]):
        span = pl.ds(pl.multiple_of(order_b[k] * depth, depth), depth)
        grad_normed[:, span] += mm_nt(low_kv[...], wkv[k])
    values = x[...].astype(F32)
    scale = rms(values)
    weighted = grad_normed[...] * gain[...]
    inner = jnp.mean(weighted * values, axis=-1, keepdims=True)
    tokens_grad[...] = (
        grad_middle[...] + scale * weighted - values * (scale * scale * scale) * inner
    ).astype(BF)
    rows = normed[...]
    acc_q[...] += mm_tn(rows, low_q[...])
    acc_kv[...] += mm_tn(rows, low_kv[...])
    acc_x[...] += column_sums(grad_normed[...] * values * scale, 0)

    @pl.when(step == pl.num_programs(0) - 1)
    def _():
        gains = column_sums(d_gq[...], 1) + column_sums(d_gk[...], 2)
        gains = gains[:HEAD_SIZE, :] + gains[HEAD_SIZE:, :]
        owners = keep_a.shape[0]
        each, depth = HEAD_SIZE // owners, acc_x.shape[0] // owners
        for d in range(owners):
            acc_x[d * depth : d * depth + each, :] += gains[d * each : (d + 1) * each, :]
        write_shares(starts, acc_q, acc_x, keep_a, keep_b, send_a, send_b)
        for which, out in ((0, keep_b), (1, send_b)):
            for j in range(owners):
                span = pl.ds(pl.multiple_of(starts[which, j], out.shape[1]), out.shape[1])
                out[j, :, LANES:] = acc_kv[span, :].astype(BF)


def project_back(
    starts, orders, dq, dk, dv, q_pre, k_pre, x, normed, grad_middle, gain, weight_a, weight_b, gq, gk, cos, sin
):
    rows, width = x.shape
    block = row_block(rows)
    qw, kw = QUERY_HEADS * HEAD_SIZE, 2 * KEY_VALUE_HEADS * HEAD_SIZE
    count = starts.shape[1]
    depth = width // (2 * count)

    def rowwise(array):
        return pl.BlockSpec((block, array.shape[1]), lambda i, *_: (i, 0))

    def whole(array):
        return pl.BlockSpec(array.shape, lambda i, *_: (0,) * len(array.shape))

    outs = [
        shape((rows, width), BF),
        *[shape((count, depth, c), BF) for c in (qw, kw + LANES) * 2],
    ]
    return call(
        project_back_kernel,
        (rows // block,),
        [rowwise(a) for a in (dq, dk, dv, q_pre, k_pre, x, normed, grad_middle)]
        + [whole(gain), weight_spec(weight_a, qw, 0), weight_spec(weight_b, kw, 0), whole(gq), whole(gk)]
        + [rowwise(a) for a in (cos, sin)],
        [rowwise(outs[0])] + [whole(a) for a in outs[1:]],
        outs,
        scratch=[
            pltpu.VMEM((block, qw), BF),
            pltpu.VMEM((block, kw), BF),
            pltpu.VMEM((block, width), F32),
            pltpu.VMEM((width, qw), F32),
            pltpu.VMEM((width, kw), F32),
            pltpu.VMEM((width, LANES), F32),
            pltpu.VMEM((8, LANES), F32),
            pltpu.VMEM((8, LANES), F32),
        ],
        prefetch=3,
        flops=4 * rows * width * (qw + kw),
        nbytes=rows * (10 * width + 8 * qw + 8 * kw),
    )(starts, *orders, dq, dk, dv, q_pre, k_pre, x, normed, grad_middle, gain, weight_a, weight_b, gq, gk, cos, sin)


def doubled(block, head):
    values = block.astype(F32)
    keep = (lane_index() // HEAD_SIZE) == (head % 2)
    return jnp.where(keep, values, pltpu.roll(values, HEAD_SIZE, 1))


def stacked(block):
    low = jnp.where(lane_index() < HEAD_SIZE, 1.0, 0.0).astype(BF)
    high = jnp.where(lane_index() < HEAD_SIZE, 0.0, 1.0).astype(BF)
    return jnp.concatenate([block * low, block * high], axis=0)


def unstacked(values):
    count = values.shape[0] // 2
    return jnp.where(lane_index() < HEAD_SIZE, values[:count], values[count:])


def beside(values, extra):
    return jnp.concatenate([values, extra], axis=1)


def picked_lanes(first, count):
    lane = lane_index()
    return jnp.where((lane >= first) & (lane < first + count), 1.0, 0.0).astype(BF)


def key_parts(causal, start, count, full):
    if not causal:
        return [(0, full, True)]
    parts = [(0, start, False)] if start else []
    return parts + [(start, start + count, True)]


def masked(values, begin, place_of):
    row = begin + lax.broadcasted_iota(I32, values.shape, 0)
    return jnp.where(row <= jnp.concatenate([place_of, place_of], axis=1), values, 0.0)


def query_blocks(rows, size=256):
    return [(start, min(size, rows - start)) for start in range(0, rows, size)]


def attend_kernel(causal, q, k, v, q_more, k_more, place_of, out, norms, keys, values_t):
    head = pl.program_id(0)
    keys[:, :LANES] = doubled(k[...], head).astype(BF)
    keys[:, LANES:] = k_more[...]
    values_t[...] = doubled(v[...], head).T.astype(BF)
    lane = lane_index()
    for start, count in query_blocks(q.shape[0]):
        span = slice(start, start + count)
        more = q_more[span, :]
        queries = beside(stacked(q[span, :]), jnp.concatenate([more, more], axis=0))
        total, summed = 0.0, 0.0
        for begin, end, later in key_parts(causal, start, count, keys.shape[0]):
            raised = jnp.exp(mm_nt(keys[begin:end, :], queries))
            if later:
                raised = masked(raised, begin, place_of[:, span])
            total += jnp.sum(raised, axis=0, keepdims=True)
            summed += mm(values_t[:, begin:end], raised.astype(BF))
        total = jnp.broadcast_to(total, (8, total.shape[1]))
        both = jnp.concatenate([summed * (1.0 / total[:1]), -jnp.log(total)], axis=0).T
        out[span, :] = unstacked(both[:, :LANES]).astype(BF)
        high, low = split_low(both[:, LANES : LANES + 1])
        norms[span, :] = (
            jnp.where(lane == 8, high[:count], 0.0)
            + jnp.where(lane == 9, low[:count], 0.0)
            + jnp.where(lane == 10, high[count:], 0.0)
            + jnp.where(lane == 11, low[count:], 0.0)
        ).astype(BF)


def attend(q, k, v, q_more, k_more, place_of):
    rows, full = q.shape[0], k.shape[0]
    heads = q.shape[1] // LANES
    qspec = pl.BlockSpec((rows, LANES), lambda j: (0, j))
    kspec = pl.BlockSpec((full, LANES), lambda j: (0, j // 2))

    def whole(array):
        return pl.BlockSpec(array.shape, lambda j: (0, 0))

    return call(
        functools.partial(attend_kernel, rows == full),
        (heads,),
        [qspec, kspec, kspec, whole(q_more), whole(k_more), whole(place_of)],
        [qspec, qspec],
        [shape(q.shape, BF)] * 2,
        scratch=[pltpu.VMEM((full, 2 * LANES), BF), pltpu.VMEM((LANES, full), BF)],
        flops=4 * rows * full * q.shape[1],
        nbytes=4 * q.size + 4 * k.size,
    )(q, k, v, q_more, k_more, place_of)


def attend_back_kernel(causal, q, k, v, grad, out, norms, q_more, k_more, place_of, *refs):
    dq, dk, dv, keys, values, keys_t, acc_k, acc_v = refs[-8:]
    head = pl.program_id(0)
    both = doubled(k[...], head)
    keys[:, :LANES] = both.astype(BF)
    keys[:, LANES:] = k_more[...]
    keys_t[...] = both.T.astype(BF)
    values[:, :LANES] = doubled(v[...], head).astype(BF)
    values[:, LANES:] = k_more[...]
    acc_k[...] = jnp.zeros_like(acc_k)
    acc_v[...] = jnp.zeros_like(acc_v)
    lane = lane_index()
    for start, count in query_blocks(q.shape[0]):
        span = slice(start, start + count)
        queries, grads = stacked(q[span, :]), stacked(grad[span, :])
        norm = norms[span, :]
        more = q_more[span, :]
        more = jnp.concatenate(
            [more + norm * picked_lanes(8, 2), more + norm * picked_lanes(10, 2)], axis=0
        )
        full_queries = beside(queries, more)
        inner = -(grad[span, :].astype(F32) * out[span, :].astype(F32))
        inner = jnp.concatenate(
            [
                jnp.sum(jnp.where(lane < HEAD_SIZE, inner, 0.0), axis=-1, keepdims=True),
                jnp.sum(jnp.where(lane < HEAD_SIZE, 0.0, inner), axis=-1, keepdims=True),
            ],
            axis=0,
        )
        high = inner.astype(BF).astype(F32)
        inner = jnp.where(lane == 8, high, jnp.where(lane == 9, inner - high, 0.0)).astype(BF)
        full_grads = beside(grads, inner)
        dq_t = 0.0
        for begin, end, later in key_parts(causal, start, count, keys.shape[0]):
            probs = jnp.exp(mm_nt(keys[begin:end, :], full_queries))
            if later:
                probs = masked(probs, begin, place_of[:, span])
            grad_scores = (probs * mm_nt(values[begin:end, :], full_grads)).astype(BF)
            dq_t += mm(keys_t[:, begin:end], grad_scores)
            acc_k[begin:end, :] += mm(grad_scores, queries)
            acc_v[begin:end, :] += mm(probs.astype(BF), grads)
        dq[span, :] = unstacked(dq_t.T)
    mine = (lane // HEAD_SIZE) == (head % 2)
    for acc, grads in ((acc_k, dk), (acc_v, dv)):
        total = acc[...] + pltpu.roll(acc[...], HEAD_SIZE, 1)
        grads[...] = jnp.where(mine, total, grads[...])


def attend_back(begin, heads, q, k, v, grad, out, norms, q_more, k_more, place_of, earlier):
    rows, full = q.shape[0], k.shape[0]
    qspec = pl.BlockSpec((rows, LANES), lambda j: (0, begin + j))
    kspec = pl.BlockSpec((full, LANES), lambda j: (0, (begin + j) // 2))

    def whole(array):
        return pl.BlockSpec(array.shape, lambda j: (0, 0))

    earlier = list(earlier or [])
    return call(
        functools.partial(attend_back_kernel, rows == full),
        (heads,),
        [qspec, kspec, kspec, qspec, qspec, qspec, whole(q_more), whole(k_more), whole(place_of)]
        + [pl.BlockSpec(memory_space=pl.ANY)] * len(earlier),
        [qspec, kspec, kspec],
        [shape(q.shape, F32), shape(k.shape, F32), shape(k.shape, F32)],
        scratch=[
            pltpu.VMEM((full, 2 * LANES), BF),
            pltpu.VMEM((full, 2 * LANES), BF),
            pltpu.VMEM((LANES, full), BF),
            pltpu.VMEM((full, LANES), F32),
            pltpu.VMEM((full, LANES), F32),
        ],
        aliases={9 + i: i for i in range(len(earlier))},
        flops=10 * rows * full * q.shape[1],
        nbytes=8 * q.size + 12 * k.size,
    )(q, k, v, grad, out, norms, q_more, k_more, place_of, *earlier)


def split_low(values):
    high = values.astype(BF)
    return high, (values - high.astype(F32)).astype(BF)


def router_kernel(
    order_a, order_b, x, att, wo_a, wo_b, router, gain, routes, middle, post_a, post_b, gates, rows
):
    grown = [mm_blocks(att, order_a, wo_a), mm_blocks(att, order_b, wo_b)]
    mid = x[...].astype(F32) + jnp.concatenate(grown, axis=1)
    middle[...] = mid
    post = (mid * rms(mid) * gain[...]).astype(BF)
    rows[...] = post
    logits = mm_blocks(rows, order_b, router)
    lane = lane_index()
    named = routes[:, 0:1] == lane
    for k in range(1, TOPK):
        named = named | (routes[:, k : k + 1] == lane)
    logits = jnp.where(named, logits, -1e30)
    raised = jnp.where(named, jnp.exp(logits - jnp.max(logits, axis=-1, keepdims=True)), 0.0)
    gate = raised / jnp.sum(raised, axis=-1, keepdims=True)
    gates[...] = gate
    high, low = split_low(gate)
    low = pltpu.roll(low.astype(F32), E, 1).astype(BF)
    half = post_a.shape[1]
    post_a[...] = post[:, :half]
    post_b[:, :half] = post[:, half:]
    post_b[:, half:] = high + low


def output_specs(weight_a, weight_b, half):
    behind = 2 * half
    return [
        weight_spec(weight_a, half, behind // half),
        weight_spec(weight_b, half, behind // half),
        weight_spec(weight_b, LANES, (behind + half) // LANES),
    ]


def route_rows(orders, x, att, weight_a, weight_b, gain, routes):
    rows, width = x.shape
    block = row_block(rows)
    outs = [
        shape((rows, width), F32),
        shape((rows, width // 2), BF),
        shape((rows, width // 2 + LANES), BF),
        shape((rows, LANES), F32),
    ]

    def rowwise(array):
        return pl.BlockSpec((block, array.shape[1]), lambda i, *_: (i, 0))

    return call(
        router_kernel,
        (rows // block,),
        [rowwise(x), rowwise(att)]
        + output_specs(weight_a, weight_b, width // 2)
        + [pl.BlockSpec(gain.shape, lambda i, *_: (0, 0)), rowwise(routes)],
        [rowwise(a) for a in outs],
        outs,
        scratch=[pltpu.VMEM((block, width), BF)],
        prefetch=2,
        flops=2 * rows * width * width,
        nbytes=rows * width * 12,
    )(*orders, x, att, weight_a, weight_b, weight_b, gain, routes)


def column_sums(values, lane):
    chosen = jnp.where(lane_index() == lane, 1.0, 0.0)
    chosen = jnp.broadcast_to(chosen, (values.shape[0], LANES)).astype(BF)
    high, low = split_low(values)
    return mm_tn(high, chosen) + mm_tn(low, chosen)


def write_shares(starts, total, extra, keep_a, keep_b, send_a, send_b):
    count, depth, cut = keep_a.shape
    rest = total.shape[1] - cut
    for which, (out_a, out_b) in enumerate(((keep_a, keep_b), (send_a, send_b))):
        for j in range(count):
            span = pl.ds(pl.multiple_of(starts[which, j], depth), depth)
            out_a[j] = total[span, :cut].astype(BF)
            if rest:
                out_b[j, :, :rest] = total[span, cut:].astype(BF)
            out_b[j, :, rest : rest + LANES] = extra[span, :].astype(BF)


def router_back_kernel(
    starts, order_a, order_b,
    middle, back_a, back_b, gates, cot, gain, wo_a, wo_b, router, att,
    grad_middle, grad_att, keep_a, keep_b, send_a, send_b,
    acc_o, acc_r, columns,
):
    step = pl.program_id(0)

    @pl.when(step == 0)
    def _():
        for ref in (acc_o, acc_r):
            ref[...] = jnp.zeros_like(ref)

    mid = middle[...]
    scale = rms(mid)
    post = (mid * scale * gain[...]).astype(BF)
    half = back_a.shape[1]
    both = back_b[:, half:].astype(F32)
    grad_gates = both + pltpu.roll(both, LANES - E, 1)
    gate = gates[...]
    inner = jnp.sum(gate * grad_gates, axis=-1, keepdims=True)
    grad_logits = (gate * (grad_gates - inner)).astype(BF)
    depth = wo_a.shape[1]
    spans_a, spans_b = (
        [pl.ds(pl.multiple_of(order[k] * depth, depth), depth) for k in range(wo_a.shape[0])]
        for order in (order_a, order_b)
    )
    columns[:, :half] = back_a[...].astype(F32)
    columns[:, half:] = back_b[:, :half].astype(F32)
    for k, span in enumerate(spans_b):
        columns[:, span] += mm_nt(grad_logits, router[k])
    grad_post = columns[...]
    weighted = grad_post * gain[...]
    mean = jnp.mean(weighted * mid, axis=-1, keepdims=True)
    total = cot[...].astype(F32) + scale * weighted - mid * (scale * scale * scale) * mean
    grad_middle[...] = total
    low = total.astype(BF)
    for k, span in enumerate(spans_a):
        columns[:, span] = mm_nt(low[:, :half], wo_a[k])
    for k, span in enumerate(spans_b):
        grad_att[:, span] = (columns[:, span] + mm_nt(low[:, half:], wo_b[k])).astype(BF)
    acc_o[...] += mm_tn(att[...], low)
    acc_r[...] += mm_tn(post, grad_logits) + column_sums(grad_post * mid * scale, E)

    @pl.when(step == pl.num_programs(0) - 1)
    def _():
        write_shares(starts, acc_o, acc_r, keep_a, keep_b, send_a, send_b)


def route_back(starts, orders, middle, back_a, back_b, gates, cot, gain, weight_a, weight_b, att):
    rows, width = middle.shape
    block = row_block(rows)
    outs = [
        shape((rows, width), F32),
        shape((rows, width), BF),
        *[shape((starts.shape[1], width // (2 * starts.shape[1]), c), BF) for c in (width // 2, width // 2 + LANES) * 2],
    ]

    def rowwise(array):
        return pl.BlockSpec((block, array.shape[1]), lambda i, *_: (i, 0))

    def whole(array):
        return pl.BlockSpec(array.shape, lambda i, *_: (0,) * len(array.shape))

    return call(
        router_back_kernel,
        (rows // block,),
        [rowwise(a) for a in (middle, back_a, back_b, gates, cot)]
        + [whole(gain)]
        + output_specs(weight_a, weight_b, width // 2)
        + [rowwise(att)],
        [rowwise(a) for a in outs[:2]] + [whole(a) for a in outs[2:]],
        outs,
        scratch=[
            pltpu.VMEM((width, width), F32),
            pltpu.VMEM((width, LANES), F32),
            pltpu.VMEM((block, width), F32),
        ],
        prefetch=3,
        flops=4 * rows * width * width,
        nbytes=rows * width * 18,
    )(starts, *orders, middle, back_a, back_b, gates, cot, gain, weight_a, weight_b, weight_b, att)


def slot_matrix(rank, cap):
    slots = lax.broadcasted_iota(I32, (cap, 1), 0).astype(F32)
    parts = [
        jnp.where(rank[e : e + 1, :] == slots, 1.0, 0.0).astype(BF) for e in range(rank.shape[0])
    ]
    return jnp.concatenate(parts, axis=0)


def dispatch_kernel(n_in, piece_of, base, rank, part_a, part_b, *refs):
    gated = n_in > 1
    slots = refs[n_in]
    experts, _, cap, width = slots.shape
    half = part_a.shape[3]
    chosen = slot_matrix(rank[0], cap)
    slots[:, 0, :, :half] = mm(chosen, part_a[0, 0]).astype(BF).reshape(experts, cap, half)
    rest = mm(chosen, part_b[0, 0])
    slots[:, 0, :, half:] = rest[:, : width - half].astype(BF).reshape(experts, cap, width - half)
    if rest.shape[1] > width - half:
        gates = refs[n_in + 1]
        both = rest[:, width - half :]
        lane = lane_index()
        for e in range(experts):
            mine = base[0] + e
            picked = (lane == mine) | (lane == mine + E)
            total = jnp.sum(
                jnp.where(picked, both[e * cap : (e + 1) * cap], 0.0), axis=-1, keepdims=True
            )
            gates[e, 0] = jnp.broadcast_to(total, (cap, LANES))


def dispatch(piece_of, base, rank, part_a, part_b, cap, width, earlier):
    pieces, experts, length = rank.shape
    (part_a, at_a), (part_b, at_b) = part_a, part_b
    count = part_a.shape[1]
    gated = part_a.shape[3] + part_b.shape[3] > width

    def token_spec(array, at):
        return pl.BlockSpec((1, 1) + array.shape[2:], lambda i, piece_of, base: (at, i, 0, 0))

    def slot_spec(columns):
        return pl.BlockSpec(
            (experts, 1, cap, columns), lambda i, piece_of, base: (0, piece_of[i], 0, 0)
        )

    outs = [shape((experts, pieces, cap, width), BF)]
    out_specs = [slot_spec(width)]
    if gated:
        outs.append(shape((experts, pieces, cap, LANES), F32))
        out_specs.append(slot_spec(LANES))
    earlier = list(earlier or [])
    return call(
        functools.partial(dispatch_kernel, len(earlier)),
        (count,),
        [
            pl.BlockSpec((1, experts, length), lambda i, piece_of, base: (piece_of[i], 0, 0)),
            token_spec(part_a, at_a),
            token_spec(part_b, at_b),
        ]
        + [pl.BlockSpec(memory_space=pl.ANY)] * len(earlier),
        out_specs,
        outs,
        prefetch=2,
        aliases={5 + i: i for i in range(len(earlier))},
        flops=2 * count * experts * cap * length * width,
        nbytes=2 * count * width * (length + experts * cap),
    )(piece_of, base, rank, part_a, part_b, *earlier)


def combine_kernel(own, n_in, rank, out_rows, back_rows, gate_rows, *refs):
    summed_rows, back_a, back_b = refs[n_in:]
    experts, _, cap, width = out_rows.shape
    half = back_a.shape[2]
    columns = experts * cap
    col = lax.broadcasted_iota(I32, (1, columns), 1)
    expert_row = lax.broadcasted_iota(I32, (experts, 1), 0)
    spread = jnp.where(col // cap == expert_row, 1.0, 0.0).astype(BF)
    wanted = (col % cap).astype(F32)
    chosen = jnp.where(mm_tn(rank[0].astype(BF), spread) == wanted, 1.0, 0.0).astype(BF)
    summed = mm(chosen, out_rows[...].reshape(columns, width))
    if own:
        summed = summed + refs[0][0]
    summed_rows[0] = summed.astype(BF)
    summed = mm(chosen, back_rows[...].reshape(columns, width)).astype(BF)
    back_a[0] = summed[:, :half]
    back_b[0, :, :half] = summed[:, half:]
    back_b[0, :, half:] = mm(chosen, gate_rows[...].reshape(columns, LANES)).astype(BF)


def combine(piece_of, rank, out_rows, back_rows, gate_rows, middle, earlier):
    experts, pieces, cap, width = out_rows.shape
    _, _, length = rank.shape
    count = piece_of.shape[0]
    half = width // 2

    def slot_spec(columns):
        return pl.BlockSpec((experts, 1, cap, columns), lambda i, piece_of: (0, piece_of[i], 0, 0))

    def token_spec(columns):
        return pl.BlockSpec((1, length, columns), lambda i, piece_of: (i, 0, 0))

    outs = [shape((pieces, length, width), BF)]
    outs += [shape((count, length, c), BF) for c in (half, half + LANES)]
    more, more_specs = [], []
    if middle is not None:
        more.append(middle)
        more_specs.append(token_spec(width))
    aliases = {}
    if earlier is not None:
        aliases = {5 + len(more): 0}
        more.append(earlier)
        more_specs.append(pl.BlockSpec(memory_space=pl.ANY))
    kernel = functools.partial(combine_kernel, middle is not None, len(more))
    return call(
        lambda piece_of, *refs: kernel(*refs),
        (count,),
        [
            pl.BlockSpec((1, experts, length), lambda i, piece_of: (piece_of[i], 0, 0)),
            slot_spec(width),
            slot_spec(width),
            slot_spec(LANES),
        ]
        + more_specs,
        [pl.BlockSpec((1, length, width), lambda i, piece_of: (piece_of[i], 0, 0))]
        + [token_spec(c) for c in (half, half + LANES)],
        outs,
        prefetch=1,
        aliases=aliases,
        flops=4 * count * experts * cap * length * width,
        nbytes=4 * count * width * (length + experts * cap),
    )(piece_of, rank, out_rows, back_rows, gate_rows, *more)


def expert_kernel(n_in, first, base, rows, grads, gates, w_in, w_out, *refs):
    outs, backs, gate_grads, keep, send, acc_in, acc_out = refs[n_in:]
    step = pl.program_id(1)
    _, pieces, cap, width = rows.shape
    count = pieces * cap
    hidden_width = w_out.shape[1]

    @pl.when(step == 0)
    def _():
        acc_in[...] = jnp.zeros_like(acc_in)
        acc_out[...] = jnp.zeros_like(acc_out)

    x = rows[...].reshape(count, width)
    grad = grads[...].reshape(count, width)
    gate = gates[...].reshape(count, LANES)[:, 0:1]
    gate_up = mm(x, w_in[0])
    grad_hidden = mm_nt(grad, w_out[0])
    a = gate_up[:, :hidden_width]
    u = gate_up[:, hidden_width:]
    sigma = 1.0 / (1.0 + jnp.exp(-a))
    silu = a * sigma
    hidden = silu * u
    inner = jnp.sum(hidden * grad_hidden, axis=-1, keepdims=True)
    gated = (hidden * gate).astype(BF)
    grad_hidden = grad_hidden * gate
    grad_a = (grad_hidden * u) * (sigma + silu * (1.0 - sigma))
    grad_u = grad_hidden * silu
    grad_gate_up = jnp.concatenate([grad_a.astype(BF), grad_u.astype(BF)], axis=1)
    outs[...] = mm(gated, w_out[0]).astype(BF).reshape(outs.shape)
    backs[...] = mm_nt(grad_gate_up, w_in[0]).astype(BF).reshape(backs.shape)
    acc_in[...] += mm_tn(x, grad_gate_up)
    acc_out[...] += mm_tn(gated, grad)
    lane = lane_index()
    mine = base[0] + first + pl.program_id(0)
    high = inner.astype(BF).astype(F32)
    both = jnp.where(lane == mine, high, jnp.where(lane == mine + E, inner - high, 0.0))
    gate_grads[...] = both.astype(BF).reshape(gate_grads.shape)

    @pl.when(step == pl.num_programs(1) - 1)
    def _():
        in_depth, out_depth = width // 2, hidden_width // 2
        for share, core in ((keep, base[1]), (send, 1 - base[1])):
            span = pl.ds(pl.multiple_of(core * in_depth, in_depth), in_depth)
            share[0, :in_depth, :] = acc_in[span, :].astype(BF)
            span = pl.ds(pl.multiple_of(core * out_depth, out_depth), out_depth)
            share[0, in_depth:, :] = acc_out[span, :].astype(BF)


def settle_kernel(n_in, core, mine, other, *refs):
    grad_in, grad_out = refs[n_in:]
    depth = grad_in.shape[1]
    own = pl.program_id(1) == core[0]

    def write(share):
        grad_in[0] = share[0, :depth, :].astype(F32)
        grad_out[0] = share[0, depth:, :].astype(F32)

    pl.when(own)(lambda: write(mine))
    pl.when(jnp.logical_not(own))(lambda: write(other))


def settle(first, core, mine, other, in_shape, out_shape, earlier):
    earlier = list(earlier or [])

    def share_spec():
        return pl.BlockSpec((1,) + mine.shape[1:], lambda e, h, core: (e, 0, 0))

    def out_spec(dims):
        return pl.BlockSpec((1, dims[1] // 2, dims[2]), lambda e, h, core: (first + e, h, 0))

    return call(
        functools.partial(settle_kernel, len(earlier)),
        (mine.shape[0], 2),
        [share_spec(), share_spec()] + [pl.BlockSpec(memory_space=pl.ANY)] * len(earlier),
        [out_spec(in_shape), out_spec(out_shape)],
        [shape(in_shape, F32), shape(out_shape, F32)],
        prefetch=1,
        aliases={3 + i: i for i in range(len(earlier))},
        flops=0,
        nbytes=12 * mine.size,
    )(core, mine, other, *earlier)


def run_experts(first, number, base, rows, grads, gates, w_in, w_out, earlier):
    experts, pieces, cap, width = rows.shape
    group = max(1, 768 // cap)
    hidden_width = w_out.shape[1]

    def slot_spec(columns):
        return pl.BlockSpec((1, group, cap, columns), lambda e, c, base: (first + e, c, 0, 0))

    def expert_spec(array, offset):
        return pl.BlockSpec((1,) + array.shape[1:], lambda e, c, base: (offset + e, 0, 0))

    outs = [
        shape(rows.shape, BF),
        shape(rows.shape, BF),
        shape((experts, pieces, cap, LANES), BF),
        shape((number, (width + hidden_width) // 2, width), BF),
        shape((number, (width + hidden_width) // 2, width), BF),
    ]
    earlier = list(earlier or [])
    return call(
        functools.partial(lambda n_in, base, *refs: expert_kernel(n_in, first, base, *refs), len(earlier)),
        (number, pieces // group),
        [slot_spec(width), slot_spec(width), slot_spec(LANES), expert_spec(w_in, first), expert_spec(w_out, first)]
        + [pl.BlockSpec(memory_space=pl.ANY)] * len(earlier),
        [slot_spec(width), slot_spec(width), slot_spec(LANES), expert_spec(outs[3], 0), expert_spec(outs[4], 0)],
        outs,
        scratch=[pltpu.VMEM(w_in.shape[1:], F32), pltpu.VMEM(w_out.shape[1:], F32)],
        prefetch=1,
        aliases={6 + i: i for i in range(len(earlier))},
        flops=18 * number * pieces * cap * width * hidden_width,
        nbytes=number * (8 * pieces * cap * width + 12 * width * hidden_width),
    )(base, rows, grads, gates, w_in, w_out, *earlier)


def per_device(
    tokens, segments, routes, norm_in, q_weight, key_weight, value_weight, q_gain, k_gain,
    o_weight, norm_post, router, expert_in, expert_out, cotangent,
):
    size = lax.axis_size("group")
    me = lax.axis_index("group")
    sequences, length, width = tokens.shape
    half = width // 2
    parts = size // sequences
    rows = sequences * length
    full = length * size
    experts = expert_in.shape[0]
    cap = (length * TOPK * 4 // (3 * E) + 7) // 8 * 8
    bits = [1 << b for b in range(size.bit_length() - 1)]
    order_a, order_b = bits, bits[::-1]
    part, sequence = me // sequences, me % sequences
    exchange = [[q * sequences + s for s in range(sequences)] for q in range(parts)]
    fellows = [[q * sequences + s for q in range(parts)] for s in range(sequences)]

    def regroup(value):
        return lax.all_to_all(
            value, "group", 0, 0, tiled=True, axis_index_groups=exchange if parts > 1 else None
        )

    def gathered(value, order):
        return gather_relative(value, "group", size, order)

    replicas = lax.axis_size("replica")
    core = lax.axis_index("replica") % 2
    base = jnp.stack([me * experts, core])
    plan = Plan(base)

    def swap_core(value):
        return swap_bit(value, "replica", 1, replicas)

    n_norm, n_gain = norm_in.shape[0], q_gain.shape[0]
    gains = jnp.concatenate([norm_in, norm_post, q_gain, k_gain])
    n_small = gains.shape[0]
    named = jnp.concatenate([routes.transpose(0, 2, 1), segments[:, None, :]], axis=1)
    named = named.reshape(sequences * (TOPK + 1), length).astype(BF)
    gains = jnp.pad(gains, (0, -n_small % length)).reshape(-1, length)
    small = jnp.concatenate([named, gains], axis=0)
    small = jnp.stack([small] + [lax.ppermute(small, "group", [(i, i ^ j) for i in range(size)]) for j in range(1, size)])
    small = place(small, range(size), me)
    gains = small[:, named.shape[0] :].reshape(size, -1).astype(F32)
    named = small[:, : named.shape[0]].astype(I32).reshape(size, sequences, TOPK + 1, length)
    cuts = [0, n_norm, 2 * n_norm, 2 * n_norm + n_gain, 2 * n_norm + 2 * n_gain]
    gain_in, gain_post, gain_q, gain_k = (
        gains[:, a:b].reshape(1, -1) for a, b in zip(cuts[:-1], cuts[1:])
    )
    gain_q = jnp.concatenate([gain_q, gain_q], axis=1)
    gain_k = jnp.concatenate([gain_k, gain_k], axis=1)

    def own_half(shard):
        depth = shard.shape[0] // 2
        return lax.dynamic_slice_in_dim(shard, core * depth, depth)

    def both_cores(mine):
        other = swap_core(mine)
        return lax.select(
            core == 0,
            jnp.concatenate([mine, other], axis=1),
            jnp.concatenate([other, mine], axis=1),
        )

    key_width = key_weight.shape[1]
    orders = [
        jnp.stack([me ^ j for j in relative_order(order)]) for order in (order_a, order_b)
    ]
    half_a = gathered(own_half(jnp.concatenate([q_weight, o_weight[:, :half]], axis=1)), order_a)
    unused = jnp.zeros((router.shape[0], LANES - E), BF)
    half_b = jnp.concatenate([key_weight, value_weight, o_weight[:, half:], router, unused], axis=1)
    half_b = gathered(own_half(half_b), order_b)
    weight_a, weight_b = both_cores(half_a), both_cores(half_b)
    x = regroup(tokens).reshape(rows, width)
    shares = jnp.stack(
        [
            jnp.stack([(me ^ j) * n_norm + which * (n_norm // 2) for j in range(size)])
            for which in (core, 1 - core)
        ]
    )

    seg_full = lax.dynamic_index_in_dim(named[:, :, TOPK], sequence, 1, keepdims=False).reshape(full)
    place_of = part * rows + jnp.arange(rows, dtype=I32)
    seg_own = lax.dynamic_slice_in_dim(seg_full, part * rows, rows)
    first = jnp.sum((seg_full[None, :] < seg_own[:, None]).astype(I32), axis=1)
    frequency = jnp.exp(
        -(2.0 * jnp.arange(HEAD_SIZE // 2, dtype=F32) / HEAD_SIZE) * math.log(ROPE_BASE)
    )
    phase = (place_of - first).astype(F32)[:, None] * frequency
    cos, sin = jnp.cos(phase), jnp.sin(phase)
    cos = jnp.concatenate([cos] * 4, axis=1)
    sin = jnp.concatenate([-sin, sin, -sin, sin], axis=1)
    place_of = place_of[None, :]
    document = jnp.arange(LANES, dtype=I32)
    q_more = jnp.where((document < 8) & (seg_own[:, None] != document), -256.0, 0.0).astype(BF)
    k_more = jnp.where((document >= 8) & (document < 12), 1.0, 0.0)
    k_more = jnp.where(seg_full[:, None] == document, 1.0, k_more).astype(BF)

    pieces = size * sequences
    local = named.reshape(pieces, TOPK + 1, length)[:, :TOPK] - me * experts
    hit = jnp.zeros((pieces, experts, length), jnp.bool_)
    for k in range(TOPK):
        hit = hit | (local[:, k : k + 1, :] == jnp.arange(experts, dtype=I32)[:, None])
    before = (jnp.arange(length)[:, None] < jnp.arange(length)[None, :]).astype(BF)
    rank = jnp.einsum("pei,ij->pej", hit.astype(BF), before, preferred_element_type=F32)
    rank = jnp.where(hit, rank, -1.0)
    own_routes = lax.dynamic_slice(
        named, (part * sequences, sequence, 0, 0), (sequences, 1, TOPK, length)
    )
    own_routes = own_routes[:, 0].transpose(0, 2, 1).reshape(rows, TOPK)

    def sequence_pieces(j):
        other = me ^ j
        return (other // sequences * sequences + jnp.arange(sequences, dtype=I32)) * sequences + other % sequences

    def position_pieces(j):
        return (me ^ j) * sequences + jnp.arange(sequences, dtype=I32)

    cot = after(cotangent, half_a, half_b)
    cots, posts = ({}, {}), ({}, {})
    for value, order, result in ((cot[:, :, :half], order_a, cots[0]), (cot[:, :, half:], order_b, cots[1])):
        plan.start(gather_flow(plan, value, order, "group", size, result))

    plan.run(16.0)
    normed, q_pre, k_pre, queries, keys, values = project(
        orders, x, plan.tie(gain_in), weight_a, weight_b, gain_q, gain_k, cos, sin
    )
    plan.note(queries)
    plan.run(16.0)
    if parts > 1:
        keys = lax.all_gather(keys, "group", axis=0, tiled=True, axis_index_groups=fellows)
        values = lax.all_gather(values, "group", axis=0, tiled=True, axis_index_groups=fellows)
    attended, norms = attend(queries, keys, values, q_more, k_more, plan.tie(place_of))
    plan.note(attended)
    plan.run(22.0)
    middle, post_a, post_b, gates = route_rows(
        orders, x, plan.tie(attended), weight_a, weight_b, gain_post, own_routes
    )
    plan.note(post_a)
    plan.run(11.0)
    post_a, post_b = (v.reshape(sequences, length, -1) for v in (post_a, post_b))
    for value, order, result in ((post_a, order_a, posts[0]), (post_b, order_b, posts[1])):
        plan.start(gather_flow(plan, value, order, "group", size, result))

    def rows_of(j, part_a, part_b):
        nonlocal slot_rows
        slot_rows = dispatch(
            plan.tie(sequence_pieces(j)), base, rank, part_a, part_b, cap, width, slot_rows
        )
        plan.note(slot_rows[0])
        plan.run(8.5)

    slot_rows, slot_grads = None, None
    rows_of(0, (post_a[None], 0), (post_b[None], 0))
    plan.drain(lambda: cots[0] and cots[1])
    for j in range(size):
        slot_grads = dispatch(
            plan.tie(position_pieces(j)),
            base,
            rank,
            cots[0][j],
            cots[1][j],
            cap,
            width,
            slot_grads,
        )
        plan.note(slot_grads[0])
        plan.run(7.5)
    own_cot = jnp.zeros((sequences, length, width), BF)
    for j in range(sequences):
        for begin, (held, at) in ((0, cots[0][j]), (half, cots[1][j])):
            piece = lax.dynamic_slice(held, (at, sequence, 0, 0), (1, 1, length, half))[0]
            own_cot = lax.dynamic_update_slice(own_cot, piece, (sequence ^ j, 0, begin))
    own_cot = own_cot.reshape(rows, width)
    plan.note(own_cot)
    plan.run(10.0)
    plan.drain(lambda: posts[0] and posts[1])
    for j in range(1, size):
        rows_of(j, posts[0][j], posts[1][j])
    settled = []

    def expert_flow(e, keep, send):
        arrived = yield "core", travel(send, fast=True), swap_core(send)
        value = add_blocks(keep, plan.tie(arrived))
        plan.note(value, span=4.0)
        mine = []
        yield from line_flow(plan, value, "replica", replicas, mine)
        arrived = yield "core", travel(mine[0], fast=True), swap_core(mine[0])
        settled[:] = settle(
            e, core.reshape(1), mine[0], plan.tie(arrived), expert_in.shape, expert_out.shape, settled
        )
        plan.note(*settled, span=8.0)

    def owned_flow(keep_a, keep_b, send_a, send_b, result):
        arrived = yield (
            "core",
            travel(send_a, fast=True) + travel(send_b, fast=True),
            [swap_core(send) for send in (send_a, send_b)],
        )
        totals = [add_low(keep, plan.tie(a)) for keep, a in zip((keep_a, keep_b), arrived)]
        plan.note(*totals)
        mine = ([], [])
        for total, order, landed in zip(totals, (order_a, order_b), mine):
            have = {j: total[j] for j in range(size)}
            plan.start(scatter_flow(plan, order[0], have, order, "group", size, landed))
        while not (mine[0] and mine[1]):
            yield "wait", 10.0, None
        value = jnp.concatenate([mine[0][0], mine[1][0]], axis=1)
        mine = []
        yield from line_flow(plan, value, "replica", replicas, mine)
        mine = mine[0]
        arrived = yield "core", travel(mine, fast=True), swap_core(mine)
        other = plan.tie(arrived)
        result.append(
            jnp.where(
                core == 0,
                jnp.concatenate([mine, other], axis=0),
                jnp.concatenate([other, mine], axis=0),
            ).astype(F32)
        )
        plan.note(result[0])

    made = None
    together = 2 if experts % 2 == 0 else 1
    for e in range(0, experts, together):
        *made, keep, send = run_experts(
            e, together, plan.tie(base), slot_rows[0], slot_grads[0], slot_rows[1], expert_in, expert_out, made
        )
        plan.note(keep)
        plan.run(7.0 + 17.0 * together)
        plan.start(expert_flow(e, keep, send))

    summed, back, backs = None, ({}, {}), ([], [])
    waiting = [(order, have, result) for order, have, result in zip((order_a, order_b), back, backs)]
    for j in sorted(range(size), key=lambda j: (-bin(j).count("1"), j)):
        summed, back[0][j], back[1][j] = combine(
            plan.tie(sequence_pieces(j)),
            rank,
            *made,
            None if j else middle.reshape(sequences, length, width),
            summed,
        )
        plan.note(back[0][j], back[1][j])
        plan.run(10.0)
        for one in list(waiting):
            order, have, result = one
            if all(k in have for k in range(size) if k & order[0]):
                plan.start(scatter_flow(plan, order[0], have, order, "group", size, result))
                waiting.remove(one)
    plan.drain(lambda: backs[0] and backs[1])
    back_a, back_b = (b[0].reshape(rows, -1) for b in backs)
    arrived = lax.all_to_all(
        plan.tie(summed).reshape(size, sequences, length, width), "group", 0, 0, tiled=True
    )

    grad_middle, grad_att, *parts_o = route_back(
        shares, orders, middle, back_a, back_b, plan.tie(gates), own_cot, gain_post, weight_a, weight_b, attended
    )
    plan.note(grad_att)
    grads_o, grads_q = [], []
    plan.run(21.0)
    plan.start(owned_flow(*parts_o, grads_o))
    through = None
    span = KEY_VALUE_HEADS // 2
    for begin in range(0, KEY_VALUE_HEADS, span):
        through = attend_back(
            begin, span, queries, keys, values, grad_att, attended, norms, q_more, k_more,
            plan.tie(place_of), through,
        )
        plan.note(through[0])
        plan.run(24.0)
    dq, dk, dv = through
    if parts > 1:
        dk, dv = (
            lax.psum_scatter(
                d.astype(BF), "group", scatter_dimension=0, tiled=True, axis_index_groups=fellows
            ).astype(F32)
            for d in (dk, dv)
        )
    tokens_grad, *parts_q = project_back(
        plan.tie(shares), orders, dq, dk, dv, q_pre, k_pre, x, normed, grad_middle, gain_in, weight_a, weight_b,
        gain_q, gain_k, cos, sin,
    )
    plan.note(tokens_grad)
    plan.run(34.0)
    plan.start(owned_flow(*parts_q, grads_q))
    layer_out = jnp.sum(plan.tie(arrived).astype(F32), axis=0).astype(BF)
    plan.note(layer_out, span=8.0)
    plan.run(0.0)
    tokens_grad = regroup(tokens_grad.reshape(sequences, length, width)).astype(F32)
    plan.drain(lambda: not plan.flows)
    grads_o, grads_q = grads_o[0], grads_q[0]
    expert_in_grad, expert_out_grad = settled
    extra = width + LANES
    return (
        layer_out,
        tokens_grad,
        grads_q[:, width],
        grads_q[:, :width],
        grads_q[:, extra : extra + key_width],
        grads_q[:, extra + key_width :],
        grads_q[:n_gain, width + 1],
        grads_q[:n_gain, width + 2],
        grads_o[:, :width],
        grads_o[:, width + E],
        grads_o[:, width : width + E],
        expert_in_grad,
        expert_out_grad,
    )


def solution(mesh):
    row, column = P("group", None), P("group")
    stream = P("replica", "group", None)
    expert = P("group", None, None)
    return jax.shard_map(
        per_device,
        mesh=mesh,
        in_specs=(
            stream, P("replica", "group"), stream, column, row, row, row, column, column,
            row, column, row, expert, expert, stream,
        ),
        out_specs=(
            stream, stream, column, row, row, row, column, column, row, column, row, expert, expert,
        ),
        check_vma=False,
    )
```

```python
import functools
import math

import jax
import jax.numpy as jnp
from jax import lax
from jax.experimental import pallas as pl
from jax.experimental.pallas import tpu as pltpu
from jax.sharding import PartitionSpec as P

QUERY_HEADS = 16
KEY_VALUE_HEADS = 8
HEAD_SIZE = 64
E = 32
TOPK = 8
EPSILON = 1e-06
ROPE_BASE = 10000.0
LANES = 128
VMEM_BYTES = 58 * 1024 * 1024

BF = jnp.bfloat16
F32 = jnp.float32
I32 = jnp.int32


def mm(a, b):
    return lax.dot_general(a, b, (((1,), (0,)), ((), ())), preferred_element_type=F32)


def mm_nt(a, b):
    return lax.dot_general(a, b, (((1,), (1,)), ((), ())), preferred_element_type=F32)


def mm_tn(a, b):
    return lax.dot_general(a, b, (((0,), (0,)), ((), ())), preferred_element_type=F32)


def shape(dims, dtype):
    return jax.ShapeDtypeStruct(dims, dtype)


def call(
    kernel, grid, in_specs, out_specs, out_shape, scratch=(), prefetch=0, flops=0, nbytes=0, aliases=None, weight=256
):
    return pl.pallas_call(
        kernel,
        grid_spec=pltpu.PrefetchScalarGridSpec(
            num_scalar_prefetch=prefetch,
            grid=grid,
            in_specs=in_specs,
            out_specs=out_specs,
            scratch_shapes=list(scratch),
        ),
        out_shape=out_shape,
        input_output_aliases=aliases or {},
        compiler_params=pltpu.CompilerParams(vmem_limit_bytes=VMEM_BYTES),
        cost_estimate=pl.CostEstimate(flops=int(weight * flops), bytes_accessed=int(weight * nbytes), transcendentals=0),
    )


def row_block(rows, most=272):
    best = 16
    for size in range(16, most + 1, 16):
        if rows % size == 0:
            best = size
    return best


def swap_bit(value, axis, bit, size):
    return lax.ppermute(value, axis, [(i, i ^ bit) for i in range(size)])


def gather_relative(value, axis, size, order):
    value = value[None]
    for bit in order:
        value = jnp.concatenate([value, swap_bit(value, axis, bit, size)], axis=0)
    return value


def relative_order(order):
    indices = [0]
    for bit in order:
        indices = indices + [j ^ bit for j in indices]
    return indices


def after(value, *earlier):
    return lax.optimization_barrier((value,) + earlier)[0]


def add_low(a, b):
    return (a.astype(F32) + b.astype(F32)).astype(BF)


class Plan:
    def __init__(self, token):
        self.token, self.now, self.free, self.flows, self.count = token, 0.0, {}, [], 0

    def tie(self, value):
        held, tree = jax.tree.flatten(value)
        return jax.tree.unflatten(tree, lax.optimization_barrier((*held, self.token))[:-1])

    def note(self, *values, span=0.0):
        self.token = after(self.token, *values)
        self.now += span

    def start(self, flow, arrived=None):
        try:
            link, span, arrived = flow.send(arrived)
        except StopIteration:
            return
        self.put(link, span, lambda: self.start(flow, arrived))

    def put(self, link, span, act):
        self.free[link] = max(self.now, self.free.get(link, 0.0)) + span
        self.count += 1
        self.flows.append((self.free[link] + 5.0, self.count, act, link))

    def run(self, span):
        self.now += span
        while self.flows and min(f[0] for f in self.flows) <= self.now:
            self.advance()

    def advance(self):
        first = min(self.flows, key=lambda f: f[:2])
        self.flows.remove(first)
        self.now = max(self.now, first[0])
        first[2]()

    def drain(self, done):
        while not done():
            self.advance()


def travel(value, fast=False):
    nbytes = value.size * value.dtype.itemsize
    return nbytes / 480e3 if fast else nbytes / 52e3


def add_kernel(a, b, total):
    total[...] = add_low(a[...], b[...])


def pick_kernel(second, a, b, out):
    out[...] = jnp.where(jnp.broadcast_to(second[0], out.shape) == 1, b[...], a[...])


def add_blocks(a, b):
    spec = pl.BlockSpec((1,) + a.shape[1:], lambda i: (i, 0, 0))
    return call(
        add_kernel, a.shape[:1], [spec, spec], spec, shape(a.shape, BF), flops=a.size, nbytes=6 * a.size
    )(a, b)


def pick_blocks(second, a, b):
    block = (1,) + a.shape[1:]

    def take(k):
        return pl.BlockSpec(block, lambda i, second: (i * (second[0] == k).astype(I32), 0, 0))

    return call(
        pick_kernel,
        a.shape[:1],
        [take(0), take(1)],
        pl.BlockSpec(block, lambda i, second: (i, 0, 0)),
        shape(a.shape, BF),
        prefetch=1,
        flops=a.size,
        nbytes=4 * a.size,
    )(second.astype(I32).reshape(1), a, b)


def line_flow(plan, value, axis, size, result):
    chips = size // 2
    middle = chips // 2
    chip = lax.axis_index(axis) // 2
    large = value.ndim == 3
    add = add_blocks if large else add_low
    span = 4.0 if large else 2.0

    def send(held, pairs):
        both = [(2 * a + core, 2 * b + core) for a, b in pairs for core in range(2)]
        return lax.ppermute(held, axis, both)

    for k in range(1, middle):
        arrived = yield "in", travel(value), send(value, [(k - 1, k), (chips - k, chips - 1 - k)])
        value = add(value, plan.tie(arrived))
        plan.note(value, span=span)
    arrived = yield "across", travel(value), send(value, [(middle - 1, middle), (middle, middle - 1)])
    value = add(value, plan.tie(arrived))
    plan.note(value, span=span)
    for k in range(middle - 1, 0, -1):
        arrived = yield "out", travel(value), send(value, [(k, k - 1), (chips - 1 - k, chips - k)])
        outer = (chip == k - 1) | (chip == chips - k)
        if large:
            value = pick_blocks(outer, value, plan.tie(arrived))
        else:
            value = lax.select(outer, plan.tie(arrived), value)
        plan.note(value, span=span)
    result.append(value)


def scatter_flow(plan, link, have, order, axis, size, result):
    for bit in order:
        moving = [j for j in range(size) if j in have and j & bit]
        sent = swap_bit(jnp.stack([have.pop(j) for j in moving]), axis, bit, size)
        arrived = yield link, travel(sent), sent
        arrived = plan.tie(arrived)
        for k, j in enumerate(moving):
            have[j ^ bit] = add_low(have[j ^ bit], arrived[k])
        plan.note(*[have[j ^ bit] for j in moving], span=5.0)
    result.append(have[0])


def gather_flow(plan, value, order, axis, size, result):
    have = {0: value}
    for level in range(len(order)):
        sent = {}
        for j, held in have.items():
            if bin(j).count("1") == level:
                for k, bit in enumerate(order):
                    if j < 1 or all(order.index(b) < k for b in order if b & j):
                        sent[j ^ bit] = swap_bit(held, axis, bit, size)
        yield order[level], len(sent) * travel(value), None
        sent = {j: plan.tie(arrived) for j, arrived in sent.items()}
        plan.note(*sent.values())
        have.update(sent)
    result.update({j: held[None] for j, held in have.items()})


def place(blocks, indices, me):
    whole = jnp.zeros_like(blocks)
    for k, j in enumerate(indices):
        start = (me ^ j,) + (0,) * (blocks.ndim - 1)
        whole = lax.dynamic_update_slice(whole, blocks[k : k + 1], start)
    return whole


def rms(values):
    return lax.rsqrt(jnp.mean(values * values, axis=-1, keepdims=True) + EPSILON)


def lane_index():
    return lax.broadcasted_iota(I32, (1, LANES), 1)


def head_ones():
    row = lax.broadcasted_iota(I32, (LANES, LANES), 0) // HEAD_SIZE
    col = lax.broadcasted_iota(I32, (LANES, LANES), 1) // HEAD_SIZE
    return jnp.where(row == col, 1.0 / HEAD_SIZE, 0.0).astype(BF)


def head_mean(values, ones):
    high = values.astype(BF)
    low = (values - high.astype(F32)).astype(BF)
    return mm(high, ones) + mm(low, ones)


def half_swap(values):
    half = HEAD_SIZE // 2
    first = (lane_index() % HEAD_SIZE) < half
    return jnp.where(
        first, pltpu.roll(values, LANES - half, 1), pltpu.roll(values, half, 1)
    )


def blocks_of(ref, order, depth):
    return [
        ref[:, pl.ds(pl.multiple_of(order[k] * depth, depth), depth)] for k in range(order.shape[0])
    ]


def mm_blocks(ref, order, weight):
    parts = blocks_of(ref, order, weight.shape[1])
    return sum(mm(part, weight[k]) for k, part in enumerate(parts))


def weight_spec(weight, width, column):
    return pl.BlockSpec(weight.shape[:2] + (width,), lambda i, *_: (0, 0, column))


def project_kernel(
    order_a, order_b, x, gain, wq, wkv, gq, gk, cos, sin, normed, q_pre, k_pre, q_out, k_out, v_out
):
    ones = head_ones()
    values = x[...].astype(F32)
    normed[...] = (values * rms(values) * gain[...]).astype(BF)
    q_pre[...] = mm_blocks(normed, order_a, wq)
    both = mm_blocks(normed, order_b, wkv)
    k_pre[...] = both[:, : k_pre.shape[1]]
    v_out[...] = both[:, k_pre.shape[1] :].astype(BF)
    for pre, gains, out, factor in ((q_pre, gq, q_out, HEAD_SIZE**-0.5), (k_pre, gk, k_out, 1.0)):
        for start in range(0, pre.shape[1], LANES):
            block = pre[:, start : start + LANES]
            scale = lax.rsqrt(head_mean(block * block, ones) + EPSILON)
            block = block * scale * gains[...]
            turned = block * cos[...] + half_swap(block) * sin[...]
            out[:, start : start + LANES] = (turned * factor).astype(BF)


def project(orders, x, gain, weight_a, weight_b, gq, gk, cos, sin):
    rows, width = x.shape
    block = row_block(rows)
    qw, kw = QUERY_HEADS * HEAD_SIZE, KEY_VALUE_HEADS * HEAD_SIZE

    def rowwise(columns):
        return pl.BlockSpec((block, columns), lambda i, *_: (i, 0))

    def whole(array):
        return pl.BlockSpec(array.shape, lambda i, *_: (0,) * array.ndim)

    return call(
        project_kernel,
        (rows // block,),
        [rowwise(width), whole(gain), weight_spec(weight_a, qw, 0), weight_spec(weight_b, 2 * kw, 0)]
        + [whole(gq), whole(gk)]
        + [rowwise(LANES)] * 2,
        [rowwise(c) for c in (width, qw, kw, qw, kw, kw)],
        [
            shape((rows, width), BF),
            shape((rows, qw), F32),
            shape((rows, kw), F32),
            shape((rows, qw), BF),
            shape((rows, kw), BF),
            shape((rows, kw), BF),
        ],
        prefetch=2,
        flops=2 * rows * width * (qw + 2 * kw),
        nbytes=rows * (2 * width + 8 * qw + 14 * kw),
    )(*orders, x, gain, weight_a, weight_b, gq, gk, cos, sin)


def head_back(pre, gain, incoming, ones, cos, sin):
    turned = incoming * cos - half_swap(incoming) * sin
    scale = lax.rsqrt(head_mean(pre * pre, ones) + EPSILON)
    weighted = turned * gain
    inner = head_mean(weighted * pre, ones)
    grad = scale * weighted - pre * (scale * scale * scale) * inner
    return grad.astype(BF), jnp.sum(turned * pre * scale, axis=0, keepdims=True)


def project_back_kernel(
    starts, order_a, order_b,
    dq, dk, dv, q_pre, k_pre, x, normed, grad_middle, gain, wq, wkv, gq, gk, cos, sin,
    tokens_grad, keep_a, keep_b, send_a, send_b,
    low_q, low_kv, grad_normed, acc_q, acc_kv, acc_x, d_gq, d_gk,
):
    step = pl.program_id(0)
    key_width = dk.shape[1]

    @pl.when(step == 0)
    def _():
        for ref in (acc_q, acc_kv, acc_x, d_gq, d_gk):
            ref[...] = jnp.zeros_like(ref)

    ones = head_ones()
    for incoming, pre, gains, low, total, factor in (
        (dq, q_pre, gq, low_q, d_gq, HEAD_SIZE**-0.5),
        (dk, k_pre, gk, low_kv, d_gk, 1.0),
    ):
        for start in range(0, pre.shape[1], LANES):
            span = slice(start, start + LANES)
            grad, terms = head_back(
                pre[:, span], gains[...], incoming[:, span] * factor, ones, cos[...], sin[...]
            )
            low[:, span] = grad
            total[0:1, :] += terms
    low_kv[:, key_width:] = dv[...].astype(BF)
    depth = wq.shape[1]
    for k in range(wq.shape[0]):
        span = pl.ds(pl.multiple_of(order_a[k] * depth, depth), depth)
        grad_normed[:, span] = mm_nt(low_q[...], wq[k])
    for k in range(wkv.shape[0]):
        span = pl.ds(pl.multiple_of(order_b[k] * depth, depth), depth)
        grad_normed[:, span] += mm_nt(low_kv[...], wkv[k])
    values = x[...].astype(F32)
    scale = rms(values)
    weighted = grad_normed[...] * gain[...]
    inner = jnp.mean(weighted * values, axis=-1, keepdims=True)
    tokens_grad[...] = (
        grad_middle[...] + scale * weighted - values * (scale * scale * scale) * inner
    ).astype(BF)
    rows = normed[...]
    acc_q[...] += mm_tn(rows, low_q[...])
    acc_kv[...] += mm_tn(rows, low_kv[...])
    acc_x[...] += column_sums(grad_normed[...] * values * scale, 0)

    @pl.when(step == pl.num_programs(0) - 1)
    def _():
        gains = column_sums(d_gq[...], 1) + column_sums(d_gk[...], 2)
        gains = gains[:HEAD_SIZE, :] + gains[HEAD_SIZE:, :]
        owners = keep_a.shape[0]
        each, depth = HEAD_SIZE // owners, acc_x.shape[0] // owners
        for d in range(owners):
            acc_x[d * depth : d * depth + each, :] += gains[d * each : (d + 1) * each, :]
        write_shares(starts, acc_q, acc_x, keep_a, keep_b, send_a, send_b)
        for which, out in ((0, keep_b), (1, send_b)):
            for j in range(owners):
                span = pl.ds(pl.multiple_of(starts[which, j], out.shape[1]), out.shape[1])
                out[j, :, LANES:] = acc_kv[span, :].astype(BF)


def project_back(
    starts, orders, dq, dk, dv, q_pre, k_pre, x, normed, grad_middle, gain, weight_a, weight_b, gq, gk, cos, sin
):
    rows, width = x.shape
    block = row_block(rows)
    qw, kw = QUERY_HEADS * HEAD_SIZE, 2 * KEY_VALUE_HEADS * HEAD_SIZE
    count = starts.shape[1]
    depth = width // (2 * count)

    def rowwise(array):
        return pl.BlockSpec((block, array.shape[1]), lambda i, *_: (i, 0))

    def whole(array):
        return pl.BlockSpec(array.shape, lambda i, *_: (0,) * len(array.shape))

    outs = [
        shape((rows, width), BF),
        *[shape((count, depth, c), BF) for c in (qw, kw + LANES) * 2],
    ]
    return call(
        project_back_kernel,
        (rows // block,),
        [rowwise(a) for a in (dq, dk, dv, q_pre, k_pre, x, normed, grad_middle)]
        + [whole(gain), weight_spec(weight_a, qw, 0), weight_spec(weight_b, kw, 0), whole(gq), whole(gk)]
        + [rowwise(a) for a in (cos, sin)],
        [rowwise(outs[0])] + [whole(a) for a in outs[1:]],
        outs,
        scratch=[
            pltpu.VMEM((block, qw), BF),
            pltpu.VMEM((block, kw), BF),
            pltpu.VMEM((block, width), F32),
            pltpu.VMEM((width, qw), F32),
            pltpu.VMEM((width, kw), F32),
            pltpu.VMEM((width, LANES), F32),
            pltpu.VMEM((8, LANES), F32),
            pltpu.VMEM((8, LANES), F32),
        ],
        prefetch=3,
        flops=4 * rows * width * (qw + kw),
        nbytes=rows * (10 * width + 8 * qw + 8 * kw),
        weight=0.001,
    )(starts, *orders, dq, dk, dv, q_pre, k_pre, x, normed, grad_middle, gain, weight_a, weight_b, gq, gk, cos, sin)


def doubled(block, head):
    values = block.astype(F32)
    keep = (lane_index() // HEAD_SIZE) == (head % 2)
    return jnp.where(keep, values, pltpu.roll(values, HEAD_SIZE, 1))


def stacked(block):
    low = jnp.where(lane_index() < HEAD_SIZE, 1.0, 0.0).astype(BF)
    high = jnp.where(lane_index() < HEAD_SIZE, 0.0, 1.0).astype(BF)
    return jnp.concatenate([block * low, block * high], axis=0)


def unstacked(values):
    count = values.shape[0] // 2
    return jnp.where(lane_index() < HEAD_SIZE, values[:count], values[count:])


def beside(values, extra):
    return jnp.concatenate([values, extra], axis=1)


def picked_lanes(first, count):
    lane = lane_index()
    return jnp.where((lane >= first) & (lane < first + count), 1.0, 0.0).astype(BF)


def key_parts(causal, start, count, full):
    if not causal:
        return [(0, full, True)]
    parts = [(0, start, False)] if start else []
    return parts + [(start, start + count, True)]


def masked(values, begin, place_of):
    row = begin + lax.broadcasted_iota(I32, values.shape, 0)
    return jnp.where(row <= jnp.concatenate([place_of, place_of], axis=1), values, 0.0)


def query_blocks(rows, size=256):
    return [(start, min(size, rows - start)) for start in range(0, rows, size)]


def attend_kernel(causal, q, k, v, q_more, k_more, place_of, out, norms, keys, values_t):
    head = pl.program_id(0)
    keys[:, :LANES] = doubled(k[...], head).astype(BF)
    keys[:, LANES:] = k_more[...]
    values_t[...] = doubled(v[...], head).T.astype(BF)
    lane = lane_index()
    for start, count in query_blocks(q.shape[0]):
        span = slice(start, start + count)
        more = q_more[span, :]
        queries = beside(stacked(q[span, :]), jnp.concatenate([more, more], axis=0))
        total, summed = 0.0, 0.0
        for begin, end, later in key_parts(causal, start, count, keys.shape[0]):
            raised = jnp.exp(mm_nt(keys[begin:end, :], queries))
            if later:
                raised = masked(raised, begin, place_of[:, span])
            total += jnp.sum(raised, axis=0, keepdims=True)
            summed += mm(values_t[:, begin:end], raised.astype(BF))
        total = jnp.broadcast_to(total, (8, total.shape[1]))
        both = jnp.concatenate([summed * (1.0 / total[:1]), -jnp.log(total)], axis=0).T
        out[span, :] = unstacked(both[:, :LANES]).astype(BF)
        high, low = split_low(both[:, LANES : LANES + 1])
        norms[span, :] = (
            jnp.where(lane == 8, high[:count], 0.0)
            + jnp.where(lane == 9, low[:count], 0.0)
            + jnp.where(lane == 10, high[count:], 0.0)
            + jnp.where(lane == 11, low[count:], 0.0)
        ).astype(BF)


def attend(q, k, v, q_more, k_more, place_of):
    rows, full = q.shape[0], k.shape[0]
    heads = q.shape[1] // LANES
    qspec = pl.BlockSpec((rows, LANES), lambda j: (0, j))
    kspec = pl.BlockSpec((full, LANES), lambda j: (0, j // 2))

    def whole(array):
        return pl.BlockSpec(array.shape, lambda j: (0, 0))

    return call(
        functools.partial(attend_kernel, rows == full),
        (heads,),
        [qspec, kspec, kspec, whole(q_more), whole(k_more), whole(place_of)],
        [qspec, qspec],
        [shape(q.shape, BF)] * 2,
        scratch=[pltpu.VMEM((full, 2 * LANES), BF), pltpu.VMEM((LANES, full), BF)],
        flops=4 * rows * full * q.shape[1],
        nbytes=4 * q.size + 4 * k.size,
    )(q, k, v, q_more, k_more, place_of)


def attend_back_kernel(causal, q, k, v, grad, out, norms, q_more, k_more, place_of, *refs):
    dq, dk, dv, keys, values, keys_t, acc_k, acc_v = refs[-8:]
    head = pl.program_id(0)
    both = doubled(k[...], head)
    keys[:, :LANES] = both.astype(BF)
    keys[:, LANES:] = k_more[...]
    keys_t[...] = both.T.astype(BF)
    values[:, :LANES] = doubled(v[...], head).astype(BF)
    values[:, LANES:] = k_more[...]
    acc_k[...] = jnp.zeros_like(acc_k)
    acc_v[...] = jnp.zeros_like(acc_v)
    lane = lane_index()
    for start, count in query_blocks(q.shape[0]):
        span = slice(start, start + count)
        queries, grads = stacked(q[span, :]), stacked(grad[span, :])
        norm = norms[span, :]
        more = q_more[span, :]
        more = jnp.concatenate(
            [more + norm * picked_lanes(8, 2), more + norm * picked_lanes(10, 2)], axis=0
        )
        full_queries = beside(queries, more)
        inner = -(grad[span, :].astype(F32) * out[span, :].astype(F32))
        inner = jnp.concatenate(
            [
                jnp.sum(jnp.where(lane < HEAD_SIZE, inner, 0.0), axis=-1, keepdims=True),
                jnp.sum(jnp.where(lane < HEAD_SIZE, 0.0, inner), axis=-1, keepdims=True),
            ],
            axis=0,
        )
        high = inner.astype(BF).astype(F32)
        inner = jnp.where(lane == 8, high, jnp.where(lane == 9, inner - high, 0.0)).astype(BF)
        full_grads = beside(grads, inner)
        dq_t = 0.0
        for begin, end, later in key_parts(causal, start, count, keys.shape[0]):
            probs = jnp.exp(mm_nt(keys[begin:end, :], full_queries))
            if later:
                probs = masked(probs, begin, place_of[:, span])
            grad_scores = (probs * mm_nt(values[begin:end, :], full_grads)).astype(BF)
            dq_t += mm(keys_t[:, begin:end], grad_scores)
            acc_k[begin:end, :] += mm(grad_scores, queries)
            acc_v[begin:end, :] += mm(probs.astype(BF), grads)
        dq[span, :] = unstacked(dq_t.T)
    mine = (lane // HEAD_SIZE) == (head % 2)
    for acc, grads in ((acc_k, dk), (acc_v, dv)):
        total = acc[...] + pltpu.roll(acc[...], HEAD_SIZE, 1)
        grads[...] = jnp.where(mine, total, grads[...])


def attend_back(begin, heads, q, k, v, grad, out, norms, q_more, k_more, place_of, earlier):
    rows, full = q.shape[0], k.shape[0]
    qspec = pl.BlockSpec((rows, LANES), lambda j: (0, begin + j))
    kspec = pl.BlockSpec((full, LANES), lambda j: (0, (begin + j) // 2))

    def whole(array):
        return pl.BlockSpec(array.shape, lambda j: (0, 0))

    earlier = list(earlier or [])
    return call(
        functools.partial(attend_back_kernel, rows == full),
        (heads,),
        [qspec, kspec, kspec, qspec, qspec, qspec, whole(q_more), whole(k_more), whole(place_of)]
        + [pl.BlockSpec(memory_space=pl.ANY)] * len(earlier),
        [qspec, kspec, kspec],
        [shape(q.shape, F32), shape(k.shape, F32), shape(k.shape, F32)],
        scratch=[
            pltpu.VMEM((full, 2 * LANES), BF),
            pltpu.VMEM((full, 2 * LANES), BF),
            pltpu.VMEM((LANES, full), BF),
            pltpu.VMEM((full, LANES), F32),
            pltpu.VMEM((full, LANES), F32),
        ],
        aliases={9 + i: i for i in range(len(earlier))},
        flops=10 * rows * full * q.shape[1],
        nbytes=8 * q.size + 12 * k.size,
    )(q, k, v, grad, out, norms, q_more, k_more, place_of, *earlier)


def split_low(values):
    high = values.astype(BF)
    return high, (values - high.astype(F32)).astype(BF)


def router_kernel(
    order_a, order_b, x, att, wo_a, wo_b, router, gain, routes, middle, post_a, post_b, gates, rows
):
    grown = [mm_blocks(att, order_a, wo_a), mm_blocks(att, order_b, wo_b)]
    mid = x[...].astype(F32) + jnp.concatenate(grown, axis=1)
    middle[...] = mid
    post = (mid * rms(mid) * gain[...]).astype(BF)
    rows[...] = post
    logits = mm_blocks(rows, order_b, router)
    lane = lane_index()
    named = routes[:, 0:1] == lane
    for k in range(1, TOPK):
        named = named | (routes[:, k : k + 1] == lane)
    logits = jnp.where(named, logits, -1e30)
    raised = jnp.where(named, jnp.exp(logits - jnp.max(logits, axis=-1, keepdims=True)), 0.0)
    gate = raised / jnp.sum(raised, axis=-1, keepdims=True)
    gates[...] = gate
    high, low = split_low(gate)
    low = pltpu.roll(low.astype(F32), E, 1).astype(BF)
    half = post_a.shape[1]
    post_a[...] = post[:, :half]
    post_b[:, :half] = post[:, half:]
    post_b[:, half:] = high + low


def output_specs(weight_a, weight_b, half):
    behind = 2 * half
    return [
        weight_spec(weight_a, half, behind // half),
        weight_spec(weight_b, half, behind // half),
        weight_spec(weight_b, LANES, (behind + half) // LANES),
    ]


def route_rows(orders, x, att, weight_a, weight_b, gain, routes):
    rows, width = x.shape
    block = row_block(rows)
    outs = [
        shape((rows, width), F32),
        shape((rows, width // 2), BF),
        shape((rows, width // 2 + LANES), BF),
        shape((rows, LANES), F32),
    ]

    def rowwise(array):
        return pl.BlockSpec((block, array.shape[1]), lambda i, *_: (i, 0))

    return call(
        router_kernel,
        (rows // block,),
        [rowwise(x), rowwise(att)]
        + output_specs(weight_a, weight_b, width // 2)
        + [pl.BlockSpec(gain.shape, lambda i, *_: (0, 0)), rowwise(routes)],
        [rowwise(a) for a in outs],
        outs,
        scratch=[pltpu.VMEM((block, width), BF)],
        prefetch=2,
        flops=2 * rows * width * width,
        nbytes=rows * width * 12,
    )(*orders, x, att, weight_a, weight_b, weight_b, gain, routes)


def column_sums(values, lane):
    chosen = jnp.where(lane_index() == lane, 1.0, 0.0)
    chosen = jnp.broadcast_to(chosen, (values.shape[0], LANES)).astype(BF)
    high, low = split_low(values)
    return mm_tn(high, chosen) + mm_tn(low, chosen)


def write_shares(starts, total, extra, keep_a, keep_b, send_a, send_b):
    count, depth, cut = keep_a.shape
    rest = total.shape[1] - cut
    for which, (out_a, out_b) in enumerate(((keep_a, keep_b), (send_a, send_b))):
        for j in range(count):
            span = pl.ds(pl.multiple_of(starts[which, j], depth), depth)
            out_a[j] = total[span, :cut].astype(BF)
            if rest:
                out_b[j, :, :rest] = total[span, cut:].astype(BF)
            out_b[j, :, rest : rest + LANES] = extra[span, :].astype(BF)


def router_back_kernel(
    starts, order_a, order_b,
    middle, back_a, back_b, gates, cot, gain, wo_a, wo_b, router, att,
    grad_middle, grad_att, keep_a, keep_b, send_a, send_b,
    acc_o, acc_r, columns,
):
    step = pl.program_id(0)

    @pl.when(step == 0)
    def _():
        for ref in (acc_o, acc_r):
            ref[...] = jnp.zeros_like(ref)

    mid = middle[...]
    scale = rms(mid)
    post = (mid * scale * gain[...]).astype(BF)
    half = back_a.shape[1]
    both = back_b[:, half:].astype(F32)
    grad_gates = both + pltpu.roll(both, LANES - E, 1)
    gate = gates[...]
    inner = jnp.sum(gate * grad_gates, axis=-1, keepdims=True)
    grad_logits = (gate * (grad_gates - inner)).astype(BF)
    depth = wo_a.shape[1]
    spans_a, spans_b = (
        [pl.ds(pl.multiple_of(order[k] * depth, depth), depth) for k in range(wo_a.shape[0])]
        for order in (order_a, order_b)
    )
    columns[:, :half] = back_a[...].astype(F32)
    columns[:, half:] = back_b[:, :half].astype(F32)
    for k, span in enumerate(spans_b):
        columns[:, span] += mm_nt(grad_logits, router[k])
    grad_post = columns[...]
    weighted = grad_post * gain[...]
    mean = jnp.mean(weighted * mid, axis=-1, keepdims=True)
    total = cot[...].astype(F32) + scale * weighted - mid * (scale * scale * scale) * mean
    grad_middle[...] = total
    low = total.astype(BF)
    for k, span in enumerate(spans_a):
        columns[:, span] = mm_nt(low[:, :half], wo_a[k])
    for k, span in enumerate(spans_b):
        grad_att[:, span] = (columns[:, span] + mm_nt(low[:, half:], wo_b[k])).astype(BF)
    acc_o[...] += mm_tn(att[...], low)
    acc_r[...] += mm_tn(post, grad_logits) + column_sums(grad_post * mid * scale, E)

    @pl.when(step == pl.num_programs(0) - 1)
    def _():
        write_shares(starts, acc_o, acc_r, keep_a, keep_b, send_a, send_b)


def route_back(starts, orders, middle, back_a, back_b, gates, cot, gain, weight_a, weight_b, att):
    rows, width = middle.shape
    block = row_block(rows)
    outs = [
        shape((rows, width), F32),
        shape((rows, width), BF),
        *[shape((starts.shape[1], width // (2 * starts.shape[1]), c), BF) for c in (width // 2, width // 2 + LANES) * 2],
    ]

    def rowwise(array):
        return pl.BlockSpec((block, array.shape[1]), lambda i, *_: (i, 0))

    def whole(array):
        return pl.BlockSpec(array.shape, lambda i, *_: (0,) * len(array.shape))

    return call(
        router_back_kernel,
        (rows // block,),
        [rowwise(a) for a in (middle, back_a, back_b, gates, cot)]
        + [whole(gain)]
        + output_specs(weight_a, weight_b, width // 2)
        + [rowwise(att)],
        [rowwise(a) for a in outs[:2]] + [whole(a) for a in outs[2:]],
        outs,
        scratch=[
            pltpu.VMEM((width, width), F32),
            pltpu.VMEM((width, LANES), F32),
            pltpu.VMEM((block, width), F32),
        ],
        prefetch=3,
        flops=4 * rows * width * width,
        nbytes=rows * width * 18,
    )(starts, *orders, middle, back_a, back_b, gates, cot, gain, weight_a, weight_b, weight_b, att)


def slot_matrix(rank, cap):
    slots = lax.broadcasted_iota(I32, (cap, 1), 0).astype(F32)
    parts = [
        jnp.where(rank[e : e + 1, :] == slots, 1.0, 0.0).astype(BF) for e in range(rank.shape[0])
    ]
    return jnp.concatenate(parts, axis=0)


def dispatch_kernel(n_in, piece_of, base, rank, part_a, part_b, *refs):
    gated = n_in > 1
    slots = refs[n_in]
    experts, _, cap, width = slots.shape
    half = part_a.shape[3]
    chosen = slot_matrix(rank[0], cap)
    slots[:, 0, :, :half] = mm(chosen, part_a[0, 0]).astype(BF).reshape(experts, cap, half)
    rest = mm(chosen, part_b[0, 0])
    slots[:, 0, :, half:] = rest[:, : width - half].astype(BF).reshape(experts, cap, width - half)
    if rest.shape[1] > width - half:
        gates = refs[n_in + 1]
        both = rest[:, width - half :]
        lane = lane_index()
        for e in range(experts):
            mine = base[0] + e
            picked = (lane == mine) | (lane == mine + E)
            total = jnp.sum(
                jnp.where(picked, both[e * cap : (e + 1) * cap], 0.0), axis=-1, keepdims=True
            )
            gates[e, 0] = jnp.broadcast_to(total, (cap, LANES))


def dispatch(piece_of, base, rank, part_a, part_b, cap, width, earlier):
    pieces, experts, length = rank.shape
    (part_a, at_a), (part_b, at_b) = part_a, part_b
    count = part_a.shape[1]
    gated = part_a.shape[3] + part_b.shape[3] > width

    def token_spec(array, at):
        return pl.BlockSpec((1, 1) + array.shape[2:], lambda i, piece_of, base: (at, i, 0, 0))

    def slot_spec(columns):
        return pl.BlockSpec(
            (experts, 1, cap, columns), lambda i, piece_of, base: (0, piece_of[i], 0, 0)
        )

    outs = [shape((experts, pieces, cap, width), BF)]
    out_specs = [slot_spec(width)]
    if gated:
        outs.append(shape((experts, pieces, cap, LANES), F32))
        out_specs.append(slot_spec(LANES))
    earlier = list(earlier or [])
    return call(
        functools.partial(dispatch_kernel, len(earlier)),
        (count,),
        [
            pl.BlockSpec((1, experts, length), lambda i, piece_of, base: (piece_of[i], 0, 0)),
            token_spec(part_a, at_a),
            token_spec(part_b, at_b),
        ]
        + [pl.BlockSpec(memory_space=pl.ANY)] * len(earlier),
        out_specs,
        outs,
        prefetch=2,
        aliases={5 + i: i for i in range(len(earlier))},
        flops=2 * count * experts * cap * length * width,
        nbytes=2 * count * width * (length + experts * cap),
    )(piece_of, base, rank, part_a, part_b, *earlier)


def combine_kernel(own, n_in, rank, out_rows, back_rows, gate_rows, *refs):
    summed_rows, back_a, back_b = refs[n_in:]
    experts, _, cap, width = out_rows.shape
    half = back_a.shape[2]
    columns = experts * cap
    col = lax.broadcasted_iota(I32, (1, columns), 1)
    expert_row = lax.broadcasted_iota(I32, (experts, 1), 0)
    spread = jnp.where(col // cap == expert_row, 1.0, 0.0).astype(BF)
    wanted = (col % cap).astype(F32)
    chosen = jnp.where(mm_tn(rank[0].astype(BF), spread) == wanted, 1.0, 0.0).astype(BF)
    summed = mm(chosen, out_rows[...].reshape(columns, width))
    if own:
        summed = summed + refs[0][0]
    summed_rows[0] = summed.astype(BF)
    summed = mm(chosen, back_rows[...].reshape(columns, width)).astype(BF)
    back_a[0] = summed[:, :half]
    back_b[0, :, :half] = summed[:, half:]
    back_b[0, :, half:] = mm(chosen, gate_rows[...].reshape(columns, LANES)).astype(BF)


def combine(piece_of, rank, out_rows, back_rows, gate_rows, middle, earlier):
    experts, pieces, cap, width = out_rows.shape
    _, _, length = rank.shape
    count = piece_of.shape[0]
    half = width // 2

    def slot_spec(columns):
        return pl.BlockSpec((experts, 1, cap, columns), lambda i, piece_of: (0, piece_of[i], 0, 0))

    def token_spec(columns):
        return pl.BlockSpec((1, length, columns), lambda i, piece_of: (i, 0, 0))

    outs = [shape((pieces, length, width), BF)]
    outs += [shape((count, length, c), BF) for c in (half, half + LANES)]
    more, more_specs = [], []
    if middle is not None:
        more.append(middle)
        more_specs.append(token_spec(width))
    aliases = {}
    if earlier is not None:
        aliases = {5 + len(more): 0}
        more.append(earlier)
        more_specs.append(pl.BlockSpec(memory_space=pl.ANY))
    kernel = functools.partial(combine_kernel, middle is not None, len(more))
    return call(
        lambda piece_of, *refs: kernel(*refs),
        (count,),
        [
            pl.BlockSpec((1, experts, length), lambda i, piece_of: (piece_of[i], 0, 0)),
            slot_spec(width),
            slot_spec(width),
            slot_spec(LANES),
        ]
        + more_specs,
        [pl.BlockSpec((1, length, width), lambda i, piece_of: (piece_of[i], 0, 0))]
        + [token_spec(c) for c in (half, half + LANES)],
        outs,
        prefetch=1,
        aliases=aliases,
        flops=4 * count * experts * cap * length * width,
        nbytes=4 * count * width * (length + experts * cap),
    )(piece_of, rank, out_rows, back_rows, gate_rows, *more)


def expert_kernel(n_in, first, base, rows, grads, gates, w_in, w_out, *refs):
    outs, backs, gate_grads, keep, send, acc_in, acc_out = refs[n_in:]
    step = pl.program_id(1)
    _, pieces, cap, width = rows.shape
    count = pieces * cap
    hidden_width = w_out.shape[1]

    @pl.when(step == 0)
    def _():
        acc_in[...] = jnp.zeros_like(acc_in)
        acc_out[...] = jnp.zeros_like(acc_out)

    x = rows[...].reshape(count, width)
    grad = grads[...].reshape(count, width)
    gate = gates[...].reshape(count, LANES)[:, 0:1]
    gate_up = mm(x, w_in[0])
    grad_hidden = mm_nt(grad, w_out[0])
    a = gate_up[:, :hidden_width]
    u = gate_up[:, hidden_width:]
    sigma = 1.0 / (1.0 + jnp.exp(-a))
    silu = a * sigma
    hidden = silu * u
    inner = jnp.sum(hidden * grad_hidden, axis=-1, keepdims=True)
    gated = (hidden * gate).astype(BF)
    grad_hidden = grad_hidden * gate
    grad_a = (grad_hidden * u) * (sigma + silu * (1.0 - sigma))
    grad_u = grad_hidden * silu
    grad_gate_up = jnp.concatenate([grad_a.astype(BF), grad_u.astype(BF)], axis=1)
    outs[...] = mm(gated, w_out[0]).astype(BF).reshape(outs.shape)
    backs[...] = mm_nt(grad_gate_up, w_in[0]).astype(BF).reshape(backs.shape)
    acc_in[...] += mm_tn(x, grad_gate_up)
    acc_out[...] += mm_tn(gated, grad)
    lane = lane_index()
    mine = base[0] + first + pl.program_id(0)
    high = inner.astype(BF).astype(F32)
    both = jnp.where(lane == mine, high, jnp.where(lane == mine + E, inner - high, 0.0))
    gate_grads[...] = both.astype(BF).reshape(gate_grads.shape)

    @pl.when(step == pl.num_programs(1) - 1)
    def _():
        in_depth, out_depth = width // 2, hidden_width // 2
        for share, core in ((keep, base[1]), (send, 1 - base[1])):
            span = pl.ds(pl.multiple_of(core * in_depth, in_depth), in_depth)
            share[0, :in_depth, :] = acc_in[span, :].astype(BF)
            span = pl.ds(pl.multiple_of(core * out_depth, out_depth), out_depth)
            share[0, in_depth:, :] = acc_out[span, :].astype(BF)


def settle_kernel(n_in, core, mine, other, *refs):
    grad_in, grad_out = refs[n_in:]
    depth = grad_in.shape[1]
    own = pl.program_id(1) == core[0]

    def write(share):
        grad_in[0] = share[0, :depth, :].astype(F32)
        grad_out[0] = share[0, depth:, :].astype(F32)

    pl.when(own)(lambda: write(mine))
    pl.when(jnp.logical_not(own))(lambda: write(other))


def settle(first, core, mine, other, in_shape, out_shape, earlier):
    earlier = list(earlier or [])

    def share_spec():
        return pl.BlockSpec((1,) + mine.shape[1:], lambda e, h, core: (e, 0, 0))

    def out_spec(dims):
        return pl.BlockSpec((1, dims[1] // 2, dims[2]), lambda e, h, core: (first + e, h, 0))

    return call(
        functools.partial(settle_kernel, len(earlier)),
        (mine.shape[0], 2),
        [share_spec(), share_spec()] + [pl.BlockSpec(memory_space=pl.ANY)] * len(earlier),
        [out_spec(in_shape), out_spec(out_shape)],
        [shape(in_shape, F32), shape(out_shape, F32)],
        prefetch=1,
        aliases={3 + i: i for i in range(len(earlier))},
        flops=0,
        nbytes=12 * mine.size,
    )(core, mine, other, *earlier)


def run_experts(first, number, base, rows, grads, gates, w_in, w_out, earlier):
    experts, pieces, cap, width = rows.shape
    group = max(1, 768 // cap)
    hidden_width = w_out.shape[1]

    def slot_spec(columns):
        return pl.BlockSpec((1, group, cap, columns), lambda e, c, base: (first + e, c, 0, 0))

    def expert_spec(array, offset):
        return pl.BlockSpec((1,) + array.shape[1:], lambda e, c, base: (offset + e, 0, 0))

    outs = [
        shape(rows.shape, BF),
        shape(rows.shape, BF),
        shape((experts, pieces, cap, LANES), BF),
        shape((number, (width + hidden_width) // 2, width), BF),
        shape((number, (width + hidden_width) // 2, width), BF),
    ]
    earlier = list(earlier or [])
    return call(
        functools.partial(lambda n_in, base, *refs: expert_kernel(n_in, first, base, *refs), len(earlier)),
        (number, pieces // group),
        [slot_spec(width), slot_spec(width), slot_spec(LANES), expert_spec(w_in, first), expert_spec(w_out, first)]
        + [pl.BlockSpec(memory_space=pl.ANY)] * len(earlier),
        [slot_spec(width), slot_spec(width), slot_spec(LANES), expert_spec(outs[3], 0), expert_spec(outs[4], 0)],
        outs,
        scratch=[pltpu.VMEM(w_in.shape[1:], F32), pltpu.VMEM(w_out.shape[1:], F32)],
        prefetch=1,
        aliases={6 + i: i for i in range(len(earlier))},
        flops=18 * number * pieces * cap * width * hidden_width,
        nbytes=number * (8 * pieces * cap * width + 12 * width * hidden_width),
    )(base, rows, grads, gates, w_in, w_out, *earlier)


def per_device(
    tokens, segments, routes, norm_in, q_weight, key_weight, value_weight, q_gain, k_gain,
    o_weight, norm_post, router, expert_in, expert_out, cotangent,
):
    size = lax.axis_size("group")
    me = lax.axis_index("group")
    sequences, length, width = tokens.shape
    half = width // 2
    parts = size // sequences
    rows = sequences * length
    full = length * size
    experts = expert_in.shape[0]
    cap = (length * TOPK * 4 // (3 * E) + 7) // 8 * 8
    bits = [1 << b for b in range(size.bit_length() - 1)]
    order_a, order_b = bits, bits[::-1]
    part, sequence = me // sequences, me % sequences
    exchange = [[q * sequences + s for s in range(sequences)] for q in range(parts)]
    fellows = [[q * sequences + s for q in range(parts)] for s in range(sequences)]

    def regroup(value):
        return lax.all_to_all(
            value, "group", 0, 0, tiled=True, axis_index_groups=exchange if parts > 1 else None
        )

    def gathered(value, order):
        return gather_relative(value, "group", size, order)

    replicas = lax.axis_size("replica")
    core = lax.axis_index("replica") % 2
    base = jnp.stack([me * experts, core])
    plan = Plan(base)

    def swap_core(value):
        return swap_bit(value, "replica", 1, replicas)

    n_norm, n_gain = norm_in.shape[0], q_gain.shape[0]
    gains = jnp.concatenate([norm_in, norm_post, q_gain, k_gain])
    n_small = gains.shape[0]
    named = jnp.concatenate([routes.transpose(0, 2, 1), segments[:, None, :]], axis=1)
    named = named.reshape(sequences * (TOPK + 1), length).astype(BF)
    gains = jnp.pad(gains, (0, -n_small % length)).reshape(-1, length)
    small = jnp.concatenate([named, gains], axis=0)
    small = jnp.stack([small] + [lax.ppermute(small, "group", [(i, i ^ j) for i in range(size)]) for j in range(1, size)])
    small = place(small, range(size), me)
    gains = small[:, named.shape[0] :].reshape(size, -1).astype(F32)
    named = small[:, : named.shape[0]].astype(I32).reshape(size, sequences, TOPK + 1, length)
    cuts = [0, n_norm, 2 * n_norm, 2 * n_norm + n_gain, 2 * n_norm + 2 * n_gain]
    gain_in, gain_post, gain_q, gain_k = (
        gains[:, a:b].reshape(1, -1) for a, b in zip(cuts[:-1], cuts[1:])
    )
    gain_q = jnp.concatenate([gain_q, gain_q], axis=1)
    gain_k = jnp.concatenate([gain_k, gain_k], axis=1)

    def own_half(shard):
        depth = shard.shape[0] // 2
        return lax.dynamic_slice_in_dim(shard, core * depth, depth)

    def both_cores(mine):
        other = swap_core(mine)
        return lax.select(
            core == 0,
            jnp.concatenate([mine, other], axis=1),
            jnp.concatenate([other, mine], axis=1),
        )

    key_width = key_weight.shape[1]
    orders = [
        jnp.stack([me ^ j for j in relative_order(order)]) for order in (order_a, order_b)
    ]
    half_a = gathered(own_half(jnp.concatenate([q_weight, o_weight[:, :half]], axis=1)), order_a)
    unused = jnp.zeros((router.shape[0], LANES - E), BF)
    half_b = jnp.concatenate([key_weight, value_weight, o_weight[:, half:], router, unused], axis=1)
    half_b = gathered(own_half(half_b), order_b)
    weight_a, weight_b = both_cores(half_a), both_cores(half_b)
    x = regroup(tokens).reshape(rows, width)
    shares = jnp.stack(
        [
            jnp.stack([(me ^ j) * n_norm + which * (n_norm // 2) for j in range(size)])
            for which in (core, 1 - core)
        ]
    )

    seg_full = lax.dynamic_index_in_dim(named[:, :, TOPK], sequence, 1, keepdims=False).reshape(full)
    place_of = part * rows + jnp.arange(rows, dtype=I32)
    seg_own = lax.dynamic_slice_in_dim(seg_full, part * rows, rows)
    first = jnp.sum((seg_full[None, :] < seg_own[:, None]).astype(I32), axis=1)
    frequency = jnp.exp(
        -(2.0 * jnp.arange(HEAD_SIZE // 2, dtype=F32) / HEAD_SIZE) * math.log(ROPE_BASE)
    )
    phase = (place_of - first).astype(F32)[:, None] * frequency
    cos, sin = jnp.cos(phase), jnp.sin(phase)
    cos = jnp.concatenate([cos] * 4, axis=1)
    sin = jnp.concatenate([-sin, sin, -sin, sin], axis=1)
    place_of = place_of[None, :]
    document = jnp.arange(LANES, dtype=I32)
    q_more = jnp.where((document < 8) & (seg_own[:, None] != document), -256.0, 0.0).astype(BF)
    k_more = jnp.where((document >= 8) & (document < 12), 1.0, 0.0)
    k_more = jnp.where(seg_full[:, None] == document, 1.0, k_more).astype(BF)

    pieces = size * sequences
    local = named.reshape(pieces, TOPK + 1, length)[:, :TOPK] - me * experts
    hit = jnp.zeros((pieces, experts, length), jnp.bool_)
    for k in range(TOPK):
        hit = hit | (local[:, k : k + 1, :] == jnp.arange(experts, dtype=I32)[:, None])
    before = (jnp.arange(length)[:, None] < jnp.arange(length)[None, :]).astype(BF)
    rank = jnp.einsum("pei,ij->pej", hit.astype(BF), before, preferred_element_type=F32)
    rank = jnp.where(hit, rank, -1.0)
    own_routes = lax.dynamic_slice(
        named, (part * sequences, sequence, 0, 0), (sequences, 1, TOPK, length)
    )
    own_routes = own_routes[:, 0].transpose(0, 2, 1).reshape(rows, TOPK)

    def sequence_pieces(j):
        other = me ^ j
        return (other // sequences * sequences + jnp.arange(sequences, dtype=I32)) * sequences + other % sequences

    def position_pieces(j):
        return (me ^ j) * sequences + jnp.arange(sequences, dtype=I32)

    cot = after(cotangent, half_a, half_b)
    cots, posts = ({}, {}), ({}, {})
    for value, order, result in ((cot[:, :, :half], order_a, cots[0]), (cot[:, :, half:], order_b, cots[1])):
        plan.start(gather_flow(plan, value, order, "group", size, result))

    plan.run(16.0)
    normed, q_pre, k_pre, queries, keys, values = project(
        orders, x, plan.tie(gain_in), weight_a, weight_b, gain_q, gain_k, cos, sin
    )
    plan.note(queries)
    plan.run(16.0)
    if parts > 1:
        keys = lax.all_gather(keys, "group", axis=0, tiled=True, axis_index_groups=fellows)
        values = lax.all_gather(values, "group", axis=0, tiled=True, axis_index_groups=fellows)
    attended, norms = attend(queries, keys, values, q_more, k_more, plan.tie(place_of))
    plan.note(attended)
    plan.run(22.0)
    middle, post_a, post_b, gates = route_rows(
        orders, x, plan.tie(attended), weight_a, weight_b, gain_post, own_routes
    )
    plan.note(post_a)
    plan.run(11.0)
    post_a, post_b = (v.reshape(sequences, length, -1) for v in (post_a, post_b))
    for value, order, result in ((post_a, order_a, posts[0]), (post_b, order_b, posts[1])):
        plan.start(gather_flow(plan, value, order, "group", size, result))

    def rows_of(j, part_a, part_b):
        nonlocal slot_rows
        slot_rows = dispatch(
            plan.tie(sequence_pieces(j)), base, rank, part_a, part_b, cap, width, slot_rows
        )
        plan.note(slot_rows[0])
        plan.run(8.5)

    slot_rows, slot_grads = None, None
    rows_of(0, (post_a[None], 0), (post_b[None], 0))
    plan.drain(lambda: cots[0] and cots[1])
    for j in range(size):
        slot_grads = dispatch(
            plan.tie(position_pieces(j)),
            base,
            rank,
            (cots[0][j], 0),
            (cots[1][j], 0),
            cap,
            width,
            slot_grads,
        )
        plan.note(slot_grads[0])
        plan.run(7.5)
    own_cot = jnp.zeros((sequences, length, width), BF)
    for j in range(sequences):
        for begin, held in ((0, cots[0][j]), (half, cots[1][j])):
            piece = lax.dynamic_slice(held, (0, sequence, 0, 0), (1, 1, length, half))[0]
            own_cot = lax.dynamic_update_slice(own_cot, piece, (sequence ^ j, 0, begin))
    own_cot = own_cot.reshape(rows, width)
    plan.note(own_cot)
    plan.run(10.0)
    plan.drain(lambda: posts[0] and posts[1])
    for j in range(1, size):
        rows_of(j, (posts[0][j], 0), (posts[1][j], 0))
    settled = []

    def expert_flow(e, keep, send):
        arrived = yield "core", travel(send, fast=True), swap_core(send)
        value = add_blocks(keep, plan.tie(arrived))
        plan.note(value, span=4.0)
        mine = []
        yield from line_flow(plan, value, "replica", replicas, mine)
        arrived = yield "core", travel(mine[0], fast=True), swap_core(mine[0])
        settled[:] = settle(
            e, core.reshape(1), mine[0], plan.tie(arrived), expert_in.shape, expert_out.shape, settled
        )
        plan.note(*settled, span=8.0)

    def owned_flow(keep_a, keep_b, send_a, send_b, result):
        arrived = yield (
            "core",
            travel(send_a, fast=True) + travel(send_b, fast=True),
            [swap_core(send) for send in (send_a, send_b)],
        )
        totals = [add_low(keep, plan.tie(a)) for keep, a in zip((keep_a, keep_b), arrived)]
        plan.note(*totals)
        mine = ([], [])
        for total, order, landed in zip(totals, (order_a, order_b), mine):
            have = {j: total[j] for j in range(size)}
            plan.start(scatter_flow(plan, order[0], have, order, "group", size, landed))
        while not (mine[0] and mine[1]):
            yield "wait", 10.0, None
        value = jnp.concatenate([mine[0][0], mine[1][0]], axis=1)
        mine = []
        yield from line_flow(plan, value, "replica", replicas, mine)
        mine = mine[0]
        arrived = yield "core", travel(mine, fast=True), swap_core(mine)
        other = plan.tie(arrived)
        result.append(
            jnp.where(
                core == 0,
                jnp.concatenate([mine, other], axis=0),
                jnp.concatenate([other, mine], axis=0),
            ).astype(F32)
        )
        plan.note(result[0])

    made, e = None, 0
    while e < experts:
        together = 2 if 0 < e < experts - 2 else 1
        *made, keep, send = run_experts(
            e, together, plan.tie(base), slot_rows[0], slot_grads[0], slot_rows[1], expert_in, expert_out, made
        )
        plan.note(keep)
        plan.run(7.0 + 17.0 * together)
        plan.start(expert_flow(e, keep, send))
        e += together

    summed, back, backs = None, ({}, {}), ([], [])
    waiting = [(order, have, result) for order, have, result in zip((order_a, order_b), back, backs)]
    for j in sorted(range(size), key=lambda j: (-bin(j).count("1"), j)):
        summed, back[0][j], back[1][j] = combine(
            plan.tie(sequence_pieces(j)),
            rank,
            *made,
            None if j else middle.reshape(sequences, length, width),
            summed,
        )
        plan.note(back[0][j], back[1][j])
        plan.now += 10.0
        for one in list(waiting):
            order, have, result = one
            if all(k in have for k in range(size) if k & order[0]):
                plan.start(scatter_flow(plan, order[0], have, order, "group", size, result))
                waiting.remove(one)
    plan.drain(lambda: backs[0] and backs[1])
    back_a, back_b = (b[0].reshape(rows, -1) for b in backs)
    arrived = lax.all_to_all(
        plan.tie(summed).reshape(size, sequences, length, width), "group", 0, 0, tiled=True
    )

    grad_middle, grad_att, *parts_o = route_back(
        shares, orders, middle, back_a, back_b, plan.tie(gates), own_cot, gain_post, weight_a, weight_b, attended
    )
    plan.note(grad_att)
    grads_o, grads_q = [], []
    plan.run(21.0)
    plan.start(owned_flow(*parts_o, grads_o))
    through = None
    span = KEY_VALUE_HEADS // 2
    for begin in range(0, KEY_VALUE_HEADS, span):
        through = attend_back(
            begin, span, queries, keys, values, grad_att, attended, norms, q_more, k_more,
            plan.tie(place_of), through,
        )
        plan.note(through[0])
        plan.run(24.0)
    dq, dk, dv = through
    if parts > 1:
        dk, dv = (
            lax.psum_scatter(
                d.astype(BF), "group", scatter_dimension=0, tiled=True, axis_index_groups=fellows
            ).astype(F32)
            for d in (dk, dv)
        )
    layer_out = jnp.sum(plan.tie(arrived).astype(F32), axis=0).astype(BF)
    plan.note(layer_out, span=8.0)
    tokens_grad, *parts_q = project_back(
        plan.tie(shares), orders, dq, dk, dv, q_pre, k_pre, x, normed, grad_middle, gain_in, weight_a, weight_b,
        gain_q, gain_k, cos, sin,
    )
    plan.note(tokens_grad)
    plan.now += 34.0
    plan.flows = [
        (arrives + (35.0 if link == "core" else 15.0), count, act, link)
        for arrives, count, act, link in plan.flows
    ]
    plan.free.pop("core", None)
    plan.start(owned_flow(*parts_q, grads_q))
    plan.run(0.0)
    tokens_grad = regroup(tokens_grad.reshape(sequences, length, width)).astype(F32)
    plan.drain(lambda: not plan.flows)
    grads_o, grads_q = grads_o[0], grads_q[0]
    expert_in_grad, expert_out_grad = settled
    extra = width + LANES
    return (
        layer_out,
        tokens_grad,
        grads_q[:, width],
        grads_q[:, :width],
        grads_q[:, extra : extra + key_width],
        grads_q[:, extra + key_width :],
        grads_q[:n_gain, width + 1],
        grads_q[:n_gain, width + 2],
        grads_o[:, :width],
        grads_o[:, width + E],
        grads_o[:, width : width + E],
        expert_in_grad,
        expert_out_grad,
    )


def solution(mesh):
    row, column = P("group", None), P("group")
    stream = P("replica", "group", None)
    expert = P("group", None, None)
    return jax.shard_map(
        per_device,
        mesh=mesh,
        in_specs=(
            stream, P("replica", "group"), stream, column, row, row, row, column, column,
            row, column, row, expert, expert, stream,
        ),
        out_specs=(
            stream, stream, column, row, row, row, column, column, row, column, row, expert, expert,
        ),
        check_vma=False,
    )
```

```python
import functools
import math

import jax
import jax.numpy as jnp
from jax import lax
from jax.experimental import pallas as pl
from jax.experimental.pallas import tpu as pltpu
from jax.sharding import PartitionSpec as P

QUERY_HEADS = 16
KEY_VALUE_HEADS = 8
HEAD_SIZE = 64
E = 32
TOPK = 8
EPSILON = 1e-06
ROPE_BASE = 10000.0
LANES = 128
VMEM_BYTES = 58 * 1024 * 1024

BF = jnp.bfloat16
F32 = jnp.float32
I32 = jnp.int32


def mm(a, b):
    return lax.dot_general(a, b, (((1,), (0,)), ((), ())), preferred_element_type=F32)


def mm_nt(a, b):
    return lax.dot_general(a, b, (((1,), (1,)), ((), ())), preferred_element_type=F32)


def mm_tn(a, b):
    return lax.dot_general(a, b, (((0,), (0,)), ((), ())), preferred_element_type=F32)


def shape(dims, dtype):
    return jax.ShapeDtypeStruct(dims, dtype)


def call(
    kernel, grid, in_specs, out_specs, out_shape, scratch=(), prefetch=0, flops=0, nbytes=0, aliases=None, weight=256
):
    return pl.pallas_call(
        kernel,
        grid_spec=pltpu.PrefetchScalarGridSpec(
            num_scalar_prefetch=prefetch,
            grid=grid,
            in_specs=in_specs,
            out_specs=out_specs,
            scratch_shapes=list(scratch),
        ),
        out_shape=out_shape,
        input_output_aliases=aliases or {},
        compiler_params=pltpu.CompilerParams(vmem_limit_bytes=VMEM_BYTES),
        cost_estimate=pl.CostEstimate(flops=int(weight * flops), bytes_accessed=int(weight * nbytes), transcendentals=0),
    )


def row_block(rows, most=272):
    best = 16
    for size in range(16, most + 1, 16):
        if rows % size == 0:
            best = size
    return best


def swap_bit(value, axis, bit, size):
    return lax.ppermute(value, axis, [(i, i ^ bit) for i in range(size)])


def gather_relative(value, axis, size, order):
    value = value[None]
    for bit in order:
        value = jnp.concatenate([value, swap_bit(value, axis, bit, size)], axis=0)
    return value


def relative_order(order):
    indices = [0]
    for bit in order:
        indices = indices + [j ^ bit for j in indices]
    return indices


def after(value, *earlier):
    return lax.optimization_barrier((value,) + earlier)[0]


def add_low(a, b):
    return (a.astype(F32) + b.astype(F32)).astype(BF)


class Plan:
    def __init__(self, token):
        self.token, self.now, self.free, self.flows, self.count = token, 0.0, {}, [], 0

    def tie(self, value):
        held, tree = jax.tree.flatten(value)
        return jax.tree.unflatten(tree, lax.optimization_barrier((*held, self.token))[:-1])

    def note(self, *values, span=0.0):
        self.token = after(self.token, *values)
        self.now += span

    def start(self, flow, arrived=None):
        try:
            link, span, arrived = flow.send(arrived)
        except StopIteration:
            return
        self.put(link, span, lambda: self.start(flow, arrived))

    def put(self, link, span, act):
        self.free[link] = max(self.now, self.free.get(link, 0.0)) + span
        self.count += 1
        self.flows.append((self.free[link] + 5.0, self.count, act, link))

    def run(self, span):
        self.now += span
        while self.flows and min(f[0] for f in self.flows) <= self.now:
            self.advance()

    def advance(self):
        first = min(self.flows, key=lambda f: f[:2])
        self.flows.remove(first)
        self.now = max(self.now, first[0])
        first[2]()

    def drain(self, done):
        while not done():
            self.advance()


def travel(value, fast=False):
    nbytes = value.size * value.dtype.itemsize
    return nbytes / 480e3 if fast else nbytes / 52e3


def add_kernel(a, b, total):
    total[...] = add_low(a[...], b[...])


def pick_kernel(second, a, b, out):
    out[...] = jnp.where(jnp.broadcast_to(second[0], out.shape) == 1, b[...], a[...])


def add_blocks(a, b):
    spec = pl.BlockSpec((1,) + a.shape[1:], lambda i: (i, 0, 0))
    return call(
        add_kernel, a.shape[:1], [spec, spec], spec, shape(a.shape, BF), flops=a.size, nbytes=6 * a.size
    )(a, b)


def pick_blocks(second, a, b):
    block = (1,) + a.shape[1:]

    def take(k):
        return pl.BlockSpec(block, lambda i, second: (i * (second[0] == k).astype(I32), 0, 0))

    return call(
        pick_kernel,
        a.shape[:1],
        [take(0), take(1)],
        pl.BlockSpec(block, lambda i, second: (i, 0, 0)),
        shape(a.shape, BF),
        prefetch=1,
        flops=a.size,
        nbytes=4 * a.size,
    )(second.astype(I32).reshape(1), a, b)


def line_flow(plan, value, axis, size, result):
    chips = size // 2
    middle = chips // 2
    chip = lax.axis_index(axis) // 2
    large = value.ndim == 3
    add = add_blocks if large else add_low
    span = 4.0 if large else 2.0

    def send(held, pairs):
        both = [(2 * a + core, 2 * b + core) for a, b in pairs for core in range(2)]
        return lax.ppermute(held, axis, both)

    for k in range(1, middle):
        arrived = yield "in", travel(value), send(value, [(k - 1, k), (chips - k, chips - 1 - k)])
        value = add(value, plan.tie(arrived))
        plan.note(value, span=span)
    arrived = yield "across", travel(value), send(value, [(middle - 1, middle), (middle, middle - 1)])
    value = add(value, plan.tie(arrived))
    plan.note(value, span=span)
    for k in range(middle - 1, 0, -1):
        arrived = yield "out", travel(value), send(value, [(k, k - 1), (chips - 1 - k, chips - k)])
        outer = (chip == k - 1) | (chip == chips - k)
        if large:
            value = pick_blocks(outer, value, plan.tie(arrived))
        else:
            value = lax.select(outer, plan.tie(arrived), value)
        plan.note(value, span=span)
    result.append(value)


def scatter_flow(plan, link, have, order, axis, size, result):
    for bit in order:
        moving = [j for j in range(size) if j in have and j & bit]
        sent = swap_bit(jnp.stack([have.pop(j) for j in moving]), axis, bit, size)
        arrived = yield link, travel(sent), sent
        arrived = plan.tie(arrived)
        for k, j in enumerate(moving):
            have[j ^ bit] = add_low(have[j ^ bit], arrived[k])
        plan.note(*[have[j ^ bit] for j in moving], span=5.0)
    result.append(have[0])


def gather_flow(plan, value, order, axis, size, result):
    have = {0: value}
    for level in range(len(order)):
        sent = {}
        for j, held in have.items():
            if bin(j).count("1") == level:
                for k, bit in enumerate(order):
                    if j < 1 or all(order.index(b) < k for b in order if b & j):
                        sent[j ^ bit] = swap_bit(held, axis, bit, size)
        yield order[level], len(sent) * travel(value), None
        sent = {j: plan.tie(arrived) for j, arrived in sent.items()}
        plan.note(*sent.values())
        have.update(sent)
    result.update({j: held[None] for j, held in have.items()})


def place(blocks, indices, me):
    whole = jnp.zeros_like(blocks)
    for k, j in enumerate(indices):
        start = (me ^ j,) + (0,) * (blocks.ndim - 1)
        whole = lax.dynamic_update_slice(whole, blocks[k : k + 1], start)
    return whole


def rms(values):
    return lax.rsqrt(jnp.mean(values * values, axis=-1, keepdims=True) + EPSILON)


def lane_index():
    return lax.broadcasted_iota(I32, (1, LANES), 1)


def head_ones():
    row = lax.broadcasted_iota(I32, (LANES, LANES), 0) // HEAD_SIZE
    col = lax.broadcasted_iota(I32, (LANES, LANES), 1) // HEAD_SIZE
    return jnp.where(row == col, 1.0 / HEAD_SIZE, 0.0).astype(BF)


def head_mean(values, ones):
    high = values.astype(BF)
    low = (values - high.astype(F32)).astype(BF)
    return mm(high, ones) + mm(low, ones)


def half_swap(values):
    half = HEAD_SIZE // 2
    first = (lane_index() % HEAD_SIZE) < half
    return jnp.where(
        first, pltpu.roll(values, LANES - half, 1), pltpu.roll(values, half, 1)
    )


def blocks_of(ref, order, depth):
    return [
        ref[:, pl.ds(pl.multiple_of(order[k] * depth, depth), depth)] for k in range(order.shape[0])
    ]


def mm_blocks(ref, order, weight):
    parts = blocks_of(ref, order, weight.shape[1])
    return sum(mm(part, weight[k]) for k, part in enumerate(parts))


def weight_spec(weight, width, column):
    return pl.BlockSpec(weight.shape[:2] + (width,), lambda i, *_: (0, 0, column))


def project_kernel(
    order_a, order_b, x, gain, wq, wkv, gq, gk, cos, sin, normed, q_pre, k_pre, q_out, k_out, v_out
):
    ones = head_ones()
    values = x[...].astype(F32)
    normed[...] = (values * rms(values) * gain[...]).astype(BF)
    q_pre[...] = mm_blocks(normed, order_a, wq)
    both = mm_blocks(normed, order_b, wkv)
    k_pre[...] = both[:, : k_pre.shape[1]]
    v_out[...] = both[:, k_pre.shape[1] :].astype(BF)
    for pre, gains, out, factor in ((q_pre, gq, q_out, HEAD_SIZE**-0.5), (k_pre, gk, k_out, 1.0)):
        for start in range(0, pre.shape[1], LANES):
            block = pre[:, start : start + LANES]
            scale = lax.rsqrt(head_mean(block * block, ones) + EPSILON)
            block = block * scale * gains[...]
            turned = block * cos[...] + half_swap(block) * sin[...]
            out[:, start : start + LANES] = (turned * factor).astype(BF)


def project(orders, x, gain, weight_a, weight_b, gq, gk, cos, sin):
    rows, width = x.shape
    block = row_block(rows)
    qw, kw = QUERY_HEADS * HEAD_SIZE, KEY_VALUE_HEADS * HEAD_SIZE

    def rowwise(columns):
        return pl.BlockSpec((block, columns), lambda i, *_: (i, 0))

    def whole(array):
        return pl.BlockSpec(array.shape, lambda i, *_: (0,) * array.ndim)

    return call(
        project_kernel,
        (rows // block,),
        [rowwise(width), whole(gain), weight_spec(weight_a, qw, 0), weight_spec(weight_b, 2 * kw, 0)]
        + [whole(gq), whole(gk)]
        + [rowwise(LANES)] * 2,
        [rowwise(c) for c in (width, qw, kw, qw, kw, kw)],
        [
            shape((rows, width), BF),
            shape((rows, qw), F32),
            shape((rows, kw), F32),
            shape((rows, qw), BF),
            shape((rows, kw), BF),
            shape((rows, kw), BF),
        ],
        prefetch=2,
        flops=2 * rows * width * (qw + 2 * kw),
        nbytes=rows * (2 * width + 8 * qw + 14 * kw),
    )(*orders, x, gain, weight_a, weight_b, gq, gk, cos, sin)


def head_back(pre, gain, incoming, ones, cos, sin):
    turned = incoming * cos - half_swap(incoming) * sin
    scale = lax.rsqrt(head_mean(pre * pre, ones) + EPSILON)
    weighted = turned * gain
    inner = head_mean(weighted * pre, ones)
    grad = scale * weighted - pre * (scale * scale * scale) * inner
    return grad.astype(BF), jnp.sum(turned * pre * scale, axis=0, keepdims=True)


def project_back_kernel(
    starts, order_a, order_b,
    dq, dk, dv, q_pre, k_pre, x, normed, grad_middle, gain, wq, wkv, gq, gk, cos, sin,
    tokens_grad, keep_a, keep_b, send_a, send_b,
    low_q, low_kv, grad_normed, acc_q, acc_kv, acc_x, d_gq, d_gk,
):
    step = pl.program_id(0)
    key_width = dk.shape[1]

    @pl.when(step == 0)
    def _():
        for ref in (acc_q, acc_kv, acc_x, d_gq, d_gk):
            ref[...] = jnp.zeros_like(ref)

    ones = head_ones()
    for incoming, pre, gains, low, total, factor in (
        (dq, q_pre, gq, low_q, d_gq, HEAD_SIZE**-0.5),
        (dk, k_pre, gk, low_kv, d_gk, 1.0),
    ):
        for start in range(0, pre.shape[1], LANES):
            span = slice(start, start + LANES)
            grad, terms = head_back(
                pre[:, span], gains[...], incoming[:, span] * factor, ones, cos[...], sin[...]
            )
            low[:, span] = grad
            total[0:1, :] += terms
    low_kv[:, key_width:] = dv[...].astype(BF)
    depth = wq.shape[1]
    for k in range(wq.shape[0]):
        span = pl.ds(pl.multiple_of(order_a[k] * depth, depth), depth)
        grad_normed[:, span] = mm_nt(low_q[...], wq[k])
    for k in range(wkv.shape[0]):
        span = pl.ds(pl.multiple_of(order_b[k] * depth, depth), depth)
        grad_normed[:, span] += mm_nt(low_kv[...], wkv[k])
    values = x[...].astype(F32)
    scale = rms(values)
    weighted = grad_normed[...] * gain[...]
    inner = jnp.mean(weighted * values, axis=-1, keepdims=True)
    tokens_grad[...] = (
        grad_middle[...] + scale * weighted - values * (scale * scale * scale) * inner
    ).astype(BF)
    rows = normed[...]
    acc_q[...] += mm_tn(rows, low_q[...])
    acc_kv[...] += mm_tn(rows, low_kv[...])
    acc_x[...] += column_sums(grad_normed[...] * values * scale, 0)

    @pl.when(step == pl.num_programs(0) - 1)
    def _():
        gains = column_sums(d_gq[...], 1) + column_sums(d_gk[...], 2)
        gains = gains[:HEAD_SIZE, :] + gains[HEAD_SIZE:, :]
        owners = keep_a.shape[0]
        each, depth = HEAD_SIZE // owners, acc_x.shape[0] // owners
        for d in range(owners):
            acc_x[d * depth : d * depth + each, :] += gains[d * each : (d + 1) * each, :]
        write_shares(starts, acc_q, acc_x, keep_a, keep_b, send_a, send_b)
        for which, out in ((0, keep_b), (1, send_b)):
            for j in range(owners):
                span = pl.ds(pl.multiple_of(starts[which, j], out.shape[1]), out.shape[1])
                out[j, :, LANES:] = acc_kv[span, :].astype(BF)


def project_back(
    starts, orders, dq, dk, dv, q_pre, k_pre, x, normed, grad_middle, gain, weight_a, weight_b, gq, gk, cos, sin
):
    rows, width = x.shape
    block = row_block(rows)
    qw, kw = QUERY_HEADS * HEAD_SIZE, 2 * KEY_VALUE_HEADS * HEAD_SIZE
    count = starts.shape[1]
    depth = width // (2 * count)

    def rowwise(array):
        return pl.BlockSpec((block, array.shape[1]), lambda i, *_: (i, 0))

    def whole(array):
        return pl.BlockSpec(array.shape, lambda i, *_: (0,) * len(array.shape))

    outs = [
        shape((rows, width), BF),
        *[shape((count, depth, c), BF) for c in (qw, kw + LANES) * 2],
    ]
    return call(
        project_back_kernel,
        (rows // block,),
        [rowwise(a) for a in (dq, dk, dv, q_pre, k_pre, x, normed, grad_middle)]
        + [whole(gain), weight_spec(weight_a, qw, 0), weight_spec(weight_b, kw, 0), whole(gq), whole(gk)]
        + [rowwise(a) for a in (cos, sin)],
        [rowwise(outs[0])] + [whole(a) for a in outs[1:]],
        outs,
        scratch=[
            pltpu.VMEM((block, qw), BF),
            pltpu.VMEM((block, kw), BF),
            pltpu.VMEM((block, width), F32),
            pltpu.VMEM((width, qw), F32),
            pltpu.VMEM((width, kw), F32),
            pltpu.VMEM((width, LANES), F32),
            pltpu.VMEM((8, LANES), F32),
            pltpu.VMEM((8, LANES), F32),
        ],
        prefetch=3,
        flops=4 * rows * width * (qw + kw),
        nbytes=rows * (10 * width + 8 * qw + 8 * kw),
        weight=0.001,
    )(starts, *orders, dq, dk, dv, q_pre, k_pre, x, normed, grad_middle, gain, weight_a, weight_b, gq, gk, cos, sin)


def doubled(block, head):
    values = block.astype(F32)
    keep = (lane_index() // HEAD_SIZE) == (head % 2)
    return jnp.where(keep, values, pltpu.roll(values, HEAD_SIZE, 1))


def stacked(block):
    low = jnp.where(lane_index() < HEAD_SIZE, 1.0, 0.0).astype(BF)
    high = jnp.where(lane_index() < HEAD_SIZE, 0.0, 1.0).astype(BF)
    return jnp.concatenate([block * low, block * high], axis=0)


def unstacked(values):
    count = values.shape[0] // 2
    return jnp.where(lane_index() < HEAD_SIZE, values[:count], values[count:])


def beside(values, extra):
    return jnp.concatenate([values, extra], axis=1)


def picked_lanes(first, count):
    lane = lane_index()
    return jnp.where((lane >= first) & (lane < first + count), 1.0, 0.0).astype(BF)


def key_parts(causal, start, count, full):
    if not causal:
        return [(0, full, True)]
    parts = [(0, start, False)] if start else []
    return parts + [(start, start + count, True)]


def masked(values, begin, place_of):
    row = begin + lax.broadcasted_iota(I32, values.shape, 0)
    return jnp.where(row <= jnp.concatenate([place_of, place_of], axis=1), values, 0.0)


def query_blocks(rows, size=256):
    return [(start, min(size, rows - start)) for start in range(0, rows, size)]


def attend_kernel(causal, q, k, v, q_more, k_more, place_of, out, norms, keys, values_t):
    head = pl.program_id(0)
    keys[:, :LANES] = doubled(k[...], head).astype(BF)
    keys[:, LANES:] = k_more[...]
    values_t[...] = doubled(v[...], head).T.astype(BF)
    lane = lane_index()
    for start, count in query_blocks(q.shape[0]):
        span = slice(start, start + count)
        more = q_more[span, :]
        queries = beside(stacked(q[span, :]), jnp.concatenate([more, more], axis=0))
        total, summed = 0.0, 0.0
        for begin, end, later in key_parts(causal, start, count, keys.shape[0]):
            raised = jnp.exp(mm_nt(keys[begin:end, :], queries))
            if later:
                raised = masked(raised, begin, place_of[:, span])
            total += jnp.sum(raised, axis=0, keepdims=True)
            summed += mm(values_t[:, begin:end], raised.astype(BF))
        total = jnp.broadcast_to(total, (8, total.shape[1]))
        both = jnp.concatenate([summed * (1.0 / total[:1]), -jnp.log(total)], axis=0).T
        out[span, :] = unstacked(both[:, :LANES]).astype(BF)
        high, low = split_low(both[:, LANES : LANES + 1])
        norms[span, :] = (
            jnp.where(lane == 8, high[:count], 0.0)
            + jnp.where(lane == 9, low[:count], 0.0)
            + jnp.where(lane == 10, high[count:], 0.0)
            + jnp.where(lane == 11, low[count:], 0.0)
        ).astype(BF)


def attend(q, k, v, q_more, k_more, place_of):
    rows, full = q.shape[0], k.shape[0]
    heads = q.shape[1] // LANES
    qspec = pl.BlockSpec((rows, LANES), lambda j: (0, j))
    kspec = pl.BlockSpec((full, LANES), lambda j: (0, j // 2))

    def whole(array):
        return pl.BlockSpec(array.shape, lambda j: (0, 0))

    return call(
        functools.partial(attend_kernel, rows == full),
        (heads,),
        [qspec, kspec, kspec, whole(q_more), whole(k_more), whole(place_of)],
        [qspec, qspec],
        [shape(q.shape, BF)] * 2,
        scratch=[pltpu.VMEM((full, 2 * LANES), BF), pltpu.VMEM((LANES, full), BF)],
        flops=4 * rows * full * q.shape[1],
        nbytes=4 * q.size + 4 * k.size,
    )(q, k, v, q_more, k_more, place_of)


def attend_back_kernel(causal, q, k, v, grad, out, norms, q_more, k_more, place_of, *refs):
    dq, dk, dv, keys, values, keys_t, acc_k, acc_v = refs[-8:]
    head = pl.program_id(0)
    both = doubled(k[...], head)
    keys[:, :LANES] = both.astype(BF)
    keys[:, LANES:] = k_more[...]
    keys_t[...] = both.T.astype(BF)
    values[:, :LANES] = doubled(v[...], head).astype(BF)
    values[:, LANES:] = k_more[...]
    acc_k[...] = jnp.zeros_like(acc_k)
    acc_v[...] = jnp.zeros_like(acc_v)
    lane = lane_index()
    for start, count in query_blocks(q.shape[0]):
        span = slice(start, start + count)
        queries, grads = stacked(q[span, :]), stacked(grad[span, :])
        norm = norms[span, :]
        more = q_more[span, :]
        more = jnp.concatenate(
            [more + norm * picked_lanes(8, 2), more + norm * picked_lanes(10, 2)], axis=0
        )
        full_queries = beside(queries, more)
        inner = -(grad[span, :].astype(F32) * out[span, :].astype(F32))
        inner = jnp.concatenate(
            [
                jnp.sum(jnp.where(lane < HEAD_SIZE, inner, 0.0), axis=-1, keepdims=True),
                jnp.sum(jnp.where(lane < HEAD_SIZE, 0.0, inner), axis=-1, keepdims=True),
            ],
            axis=0,
        )
        high = inner.astype(BF).astype(F32)
        inner = jnp.where(lane == 8, high, jnp.where(lane == 9, inner - high, 0.0)).astype(BF)
        full_grads = beside(grads, inner)
        dq_t = 0.0
        for begin, end, later in key_parts(causal, start, count, keys.shape[0]):
            probs = jnp.exp(mm_nt(keys[begin:end, :], full_queries))
            if later:
                probs = masked(probs, begin, place_of[:, span])
            grad_scores = (probs * mm_nt(values[begin:end, :], full_grads)).astype(BF)
            dq_t += mm(keys_t[:, begin:end], grad_scores)
            acc_k[begin:end, :] += mm(grad_scores, queries)
            acc_v[begin:end, :] += mm(probs.astype(BF), grads)
        dq[span, :] = unstacked(dq_t.T)
    mine = (lane // HEAD_SIZE) == (head % 2)
    for acc, grads in ((acc_k, dk), (acc_v, dv)):
        total = acc[...] + pltpu.roll(acc[...], HEAD_SIZE, 1)
        grads[...] = jnp.where(mine, total, grads[...])


def attend_back(begin, heads, q, k, v, grad, out, norms, q_more, k_more, place_of, earlier):
    rows, full = q.shape[0], k.shape[0]
    qspec = pl.BlockSpec((rows, LANES), lambda j: (0, begin + j))
    kspec = pl.BlockSpec((full, LANES), lambda j: (0, (begin + j) // 2))

    def whole(array):
        return pl.BlockSpec(array.shape, lambda j: (0, 0))

    earlier = list(earlier or [])
    return call(
        functools.partial(attend_back_kernel, rows == full),
        (heads,),
        [qspec, kspec, kspec, qspec, qspec, qspec, whole(q_more), whole(k_more), whole(place_of)]
        + [pl.BlockSpec(memory_space=pl.ANY)] * len(earlier),
        [qspec, kspec, kspec],
        [shape(q.shape, F32), shape(k.shape, F32), shape(k.shape, F32)],
        scratch=[
            pltpu.VMEM((full, 2 * LANES), BF),
            pltpu.VMEM((full, 2 * LANES), BF),
            pltpu.VMEM((LANES, full), BF),
            pltpu.VMEM((full, LANES), F32),
            pltpu.VMEM((full, LANES), F32),
        ],
        aliases={9 + i: i for i in range(len(earlier))},
        flops=10 * rows * full * q.shape[1],
        nbytes=8 * q.size + 12 * k.size,
    )(q, k, v, grad, out, norms, q_more, k_more, place_of, *earlier)


def split_low(values):
    high = values.astype(BF)
    return high, (values - high.astype(F32)).astype(BF)


def router_kernel(
    order_a, order_b, x, att, wo_a, wo_b, router, gain, routes, middle, post_a, post_b, gates, rows
):
    grown = [mm_blocks(att, order_a, wo_a), mm_blocks(att, order_b, wo_b)]
    mid = x[...].astype(F32) + jnp.concatenate(grown, axis=1)
    middle[...] = mid
    post = (mid * rms(mid) * gain[...]).astype(BF)
    rows[...] = post
    logits = mm_blocks(rows, order_b, router)
    lane = lane_index()
    named = routes[:, 0:1] == lane
    for k in range(1, TOPK):
        named = named | (routes[:, k : k + 1] == lane)
    logits = jnp.where(named, logits, -1e30)
    raised = jnp.where(named, jnp.exp(logits - jnp.max(logits, axis=-1, keepdims=True)), 0.0)
    gate = raised / jnp.sum(raised, axis=-1, keepdims=True)
    gates[...] = gate
    high, low = split_low(gate)
    low = pltpu.roll(low.astype(F32), E, 1).astype(BF)
    half = post_a.shape[1]
    post_a[...] = post[:, :half]
    post_b[:, :half] = post[:, half:]
    post_b[:, half:] = high + low


def output_specs(weight_a, weight_b, half):
    behind = 2 * half
    return [
        weight_spec(weight_a, half, behind // half),
        weight_spec(weight_b, half, behind // half),
        weight_spec(weight_b, LANES, (behind + half) // LANES),
    ]


def route_rows(orders, x, att, weight_a, weight_b, gain, routes):
    rows, width = x.shape
    block = row_block(rows)
    outs = [
        shape((rows, width), F32),
        shape((rows, width // 2), BF),
        shape((rows, width // 2 + LANES), BF),
        shape((rows, LANES), F32),
    ]

    def rowwise(array):
        return pl.BlockSpec((block, array.shape[1]), lambda i, *_: (i, 0))

    return call(
        router_kernel,
        (rows // block,),
        [rowwise(x), rowwise(att)]
        + output_specs(weight_a, weight_b, width // 2)
        + [pl.BlockSpec(gain.shape, lambda i, *_: (0, 0)), rowwise(routes)],
        [rowwise(a) for a in outs],
        outs,
        scratch=[pltpu.VMEM((block, width), BF)],
        prefetch=2,
        flops=2 * rows * width * width,
        nbytes=rows * width * 12,
    )(*orders, x, att, weight_a, weight_b, weight_b, gain, routes)


def column_sums(values, lane):
    chosen = jnp.where(lane_index() == lane, 1.0, 0.0)
    chosen = jnp.broadcast_to(chosen, (values.shape[0], LANES)).astype(BF)
    high, low = split_low(values)
    return mm_tn(high, chosen) + mm_tn(low, chosen)


def write_shares(starts, total, extra, keep_a, keep_b, send_a, send_b):
    count, depth, cut = keep_a.shape
    rest = total.shape[1] - cut
    for which, (out_a, out_b) in enumerate(((keep_a, keep_b), (send_a, send_b))):
        for j in range(count):
            span = pl.ds(pl.multiple_of(starts[which, j], depth), depth)
            out_a[j] = total[span, :cut].astype(BF)
            if rest:
                out_b[j, :, :rest] = total[span, cut:].astype(BF)
            out_b[j, :, rest : rest + LANES] = extra[span, :].astype(BF)


def router_back_kernel(
    starts, order_a, order_b,
    middle, back_a, back_b, gates, cot, gain, wo_a, wo_b, router, att,
    grad_middle, grad_att, keep_a, keep_b, send_a, send_b,
    acc_o, acc_r, columns,
):
    step = pl.program_id(0)

    @pl.when(step == 0)
    def _():
        for ref in (acc_o, acc_r):
            ref[...] = jnp.zeros_like(ref)

    mid = middle[...]
    scale = rms(mid)
    post = (mid * scale * gain[...]).astype(BF)
    half = back_a.shape[1]
    both = back_b[:, half:].astype(F32)
    grad_gates = both + pltpu.roll(both, LANES - E, 1)
    gate = gates[...]
    inner = jnp.sum(gate * grad_gates, axis=-1, keepdims=True)
    grad_logits = (gate * (grad_gates - inner)).astype(BF)
    depth = wo_a.shape[1]
    spans_a, spans_b = (
        [pl.ds(pl.multiple_of(order[k] * depth, depth), depth) for k in range(wo_a.shape[0])]
        for order in (order_a, order_b)
    )
    columns[:, :half] = back_a[...].astype(F32)
    columns[:, half:] = back_b[:, :half].astype(F32)
    for k, span in enumerate(spans_b):
        columns[:, span] += mm_nt(grad_logits, router[k])
    grad_post = columns[...]
    weighted = grad_post * gain[...]
    mean = jnp.mean(weighted * mid, axis=-1, keepdims=True)
    total = cot[...].astype(F32) + scale * weighted - mid * (scale * scale * scale) * mean
    grad_middle[...] = total
    low = total.astype(BF)
    for k, span in enumerate(spans_a):
        columns[:, span] = mm_nt(low[:, :half], wo_a[k])
    for k, span in enumerate(spans_b):
        grad_att[:, span] = (columns[:, span] + mm_nt(low[:, half:], wo_b[k])).astype(BF)
    acc_o[...] += mm_tn(att[...], low)
    acc_r[...] += mm_tn(post, grad_logits) + column_sums(grad_post * mid * scale, E)

    @pl.when(step == pl.num_programs(0) - 1)
    def _():
        write_shares(starts, acc_o, acc_r, keep_a, keep_b, send_a, send_b)


def route_back(starts, orders, middle, back_a, back_b, gates, cot, gain, weight_a, weight_b, att):
    rows, width = middle.shape
    block = row_block(rows)
    outs = [
        shape((rows, width), F32),
        shape((rows, width), BF),
        *[shape((starts.shape[1], width // (2 * starts.shape[1]), c), BF) for c in (width // 2, width // 2 + LANES) * 2],
    ]

    def rowwise(array):
        return pl.BlockSpec((block, array.shape[1]), lambda i, *_: (i, 0))

    def whole(array):
        return pl.BlockSpec(array.shape, lambda i, *_: (0,) * len(array.shape))

    return call(
        router_back_kernel,
        (rows // block,),
        [rowwise(a) for a in (middle, back_a, back_b, gates, cot)]
        + [whole(gain)]
        + output_specs(weight_a, weight_b, width // 2)
        + [rowwise(att)],
        [rowwise(a) for a in outs[:2]] + [whole(a) for a in outs[2:]],
        outs,
        scratch=[
            pltpu.VMEM((width, width), F32),
            pltpu.VMEM((width, LANES), F32),
            pltpu.VMEM((block, width), F32),
        ],
        prefetch=3,
        flops=4 * rows * width * width,
        nbytes=rows * width * 18,
    )(starts, *orders, middle, back_a, back_b, gates, cot, gain, weight_a, weight_b, weight_b, att)


def slot_matrix(rank, cap):
    slots = lax.broadcasted_iota(I32, (cap, 1), 0).astype(F32)
    parts = [
        jnp.where(rank[e : e + 1, :] == slots, 1.0, 0.0).astype(BF) for e in range(rank.shape[0])
    ]
    return jnp.concatenate(parts, axis=0)


def dispatch_kernel(n_in, piece_of, base, rank, part_a, part_b, *refs):
    gated = n_in > 1
    slots = refs[n_in]
    experts, _, cap, width = slots.shape
    half = part_a.shape[3]
    chosen = slot_matrix(rank[0], cap)
    slots[:, 0, :, :half] = mm(chosen, part_a[0, 0]).astype(BF).reshape(experts, cap, half)
    rest = mm(chosen, part_b[0, 0])
    slots[:, 0, :, half:] = rest[:, : width - half].astype(BF).reshape(experts, cap, width - half)
    if rest.shape[1] > width - half:
        gates = refs[n_in + 1]
        both = rest[:, width - half :]
        lane = lane_index()
        for e in range(experts):
            mine = base[0] + e
            picked = (lane == mine) | (lane == mine + E)
            total = jnp.sum(
                jnp.where(picked, both[e * cap : (e + 1) * cap], 0.0), axis=-1, keepdims=True
            )
            gates[e, 0] = jnp.broadcast_to(total, (cap, LANES))


def dispatch(piece_of, base, rank, part_a, part_b, cap, width, earlier):
    pieces, experts, length = rank.shape
    (part_a, at_a), (part_b, at_b) = part_a, part_b
    count = part_a.shape[1]
    gated = part_a.shape[3] + part_b.shape[3] > width

    def token_spec(array, at):
        return pl.BlockSpec((1, 1) + array.shape[2:], lambda i, piece_of, base: (at, i, 0, 0))

    def slot_spec(columns):
        return pl.BlockSpec(
            (experts, 1, cap, columns), lambda i, piece_of, base: (0, piece_of[i], 0, 0)
        )

    outs = [shape((experts, pieces, cap, width), BF)]
    out_specs = [slot_spec(width)]
    if gated:
        outs.append(shape((experts, pieces, cap, LANES), F32))
        out_specs.append(slot_spec(LANES))
    earlier = list(earlier or [])
    return call(
        functools.partial(dispatch_kernel, len(earlier)),
        (count,),
        [
            pl.BlockSpec((1, experts, length), lambda i, piece_of, base: (piece_of[i], 0, 0)),
            token_spec(part_a, at_a),
            token_spec(part_b, at_b),
        ]
        + [pl.BlockSpec(memory_space=pl.ANY)] * len(earlier),
        out_specs,
        outs,
        prefetch=2,
        aliases={5 + i: i for i in range(len(earlier))},
        flops=2 * count * experts * cap * length * width,
        nbytes=2 * count * width * (length + experts * cap),
    )(piece_of, base, rank, part_a, part_b, *earlier)


def combine_kernel(own, n_in, rank, out_rows, back_rows, gate_rows, *refs):
    summed_rows, back_a, back_b = refs[n_in:]
    experts, _, cap, width = out_rows.shape
    half = back_a.shape[2]
    columns = experts * cap
    col = lax.broadcasted_iota(I32, (1, columns), 1)
    expert_row = lax.broadcasted_iota(I32, (experts, 1), 0)
    spread = jnp.where(col // cap == expert_row, 1.0, 0.0).astype(BF)
    wanted = (col % cap).astype(F32)
    chosen = jnp.where(mm_tn(rank[0].astype(BF), spread) == wanted, 1.0, 0.0).astype(BF)
    summed = mm(chosen, out_rows[...].reshape(columns, width))
    if own:
        summed = summed + refs[0][0]
    summed_rows[0] = summed.astype(BF)
    summed = mm(chosen, back_rows[...].reshape(columns, width)).astype(BF)
    back_a[0] = summed[:, :half]
    back_b[0, :, :half] = summed[:, half:]
    back_b[0, :, half:] = mm(chosen, gate_rows[...].reshape(columns, LANES)).astype(BF)


def combine(piece_of, rank, out_rows, back_rows, gate_rows, middle, earlier):
    experts, pieces, cap, width = out_rows.shape
    _, _, length = rank.shape
    count = piece_of.shape[0]
    half = width // 2

    def slot_spec(columns):
        return pl.BlockSpec((experts, 1, cap, columns), lambda i, piece_of: (0, piece_of[i], 0, 0))

    def token_spec(columns):
        return pl.BlockSpec((1, length, columns), lambda i, piece_of: (i, 0, 0))

    outs = [shape((pieces, length, width), BF)]
    outs += [shape((count, length, c), BF) for c in (half, half + LANES)]
    more, more_specs = [], []
    if middle is not None:
        more.append(middle)
        more_specs.append(token_spec(width))
    aliases = {}
    if earlier is not None:
        aliases = {5 + len(more): 0}
        more.append(earlier)
        more_specs.append(pl.BlockSpec(memory_space=pl.ANY))
    kernel = functools.partial(combine_kernel, middle is not None, len(more))
    return call(
        lambda piece_of, *refs: kernel(*refs),
        (count,),
        [
            pl.BlockSpec((1, experts, length), lambda i, piece_of: (piece_of[i], 0, 0)),
            slot_spec(width),
            slot_spec(width),
            slot_spec(LANES),
        ]
        + more_specs,
        [pl.BlockSpec((1, length, width), lambda i, piece_of: (piece_of[i], 0, 0))]
        + [token_spec(c) for c in (half, half + LANES)],
        outs,
        prefetch=1,
        aliases=aliases,
        flops=4 * count * experts * cap * length * width,
        nbytes=4 * count * width * (length + experts * cap),
    )(piece_of, rank, out_rows, back_rows, gate_rows, *more)


def expert_kernel(n_in, first, base, rows, grads, gates, w_in, w_out, *refs):
    outs, backs, gate_grads, keep, send, acc_in, acc_out = refs[n_in:]
    step = pl.program_id(1)
    _, pieces, cap, width = rows.shape
    count = pieces * cap
    hidden_width = w_out.shape[1]

    @pl.when(step == 0)
    def _():
        acc_in[...] = jnp.zeros_like(acc_in)
        acc_out[...] = jnp.zeros_like(acc_out)

    x = rows[...].reshape(count, width)
    grad = grads[...].reshape(count, width)
    gate = gates[...].reshape(count, LANES)[:, 0:1]
    gate_up = mm(x, w_in[0])
    grad_hidden = mm_nt(grad, w_out[0])
    a = gate_up[:, :hidden_width]
    u = gate_up[:, hidden_width:]
    sigma = 1.0 / (1.0 + jnp.exp(-a))
    silu = a * sigma
    hidden = silu * u
    inner = jnp.sum(hidden * grad_hidden, axis=-1, keepdims=True)
    gated = (hidden * gate).astype(BF)
    grad_hidden = grad_hidden * gate
    grad_a = (grad_hidden * u) * (sigma + silu * (1.0 - sigma))
    grad_u = grad_hidden * silu
    grad_gate_up = jnp.concatenate([grad_a.astype(BF), grad_u.astype(BF)], axis=1)
    outs[...] = mm(gated, w_out[0]).astype(BF).reshape(outs.shape)
    backs[...] = mm_nt(grad_gate_up, w_in[0]).astype(BF).reshape(backs.shape)
    acc_in[...] += mm_tn(x, grad_gate_up)
    acc_out[...] += mm_tn(gated, grad)
    lane = lane_index()
    mine = base[0] + first + pl.program_id(0)
    high = inner.astype(BF).astype(F32)
    both = jnp.where(lane == mine, high, jnp.where(lane == mine + E, inner - high, 0.0))
    gate_grads[...] = both.astype(BF).reshape(gate_grads.shape)

    @pl.when(step == pl.num_programs(1) - 1)
    def _():
        in_depth, out_depth = width // 2, hidden_width // 2
        for share, core in ((keep, base[1]), (send, 1 - base[1])):
            span = pl.ds(pl.multiple_of(core * in_depth, in_depth), in_depth)
            share[0, :in_depth, :] = acc_in[span, :].astype(BF)
            span = pl.ds(pl.multiple_of(core * out_depth, out_depth), out_depth)
            share[0, in_depth:, :] = acc_out[span, :].astype(BF)


def settle_kernel(n_in, core, mine, other, *refs):
    grad_in, grad_out = refs[n_in:]
    depth = grad_in.shape[1]
    own = pl.program_id(1) == core[0]

    def write(share):
        grad_in[0] = share[0, :depth, :].astype(F32)
        grad_out[0] = share[0, depth:, :].astype(F32)

    pl.when(own)(lambda: write(mine))
    pl.when(jnp.logical_not(own))(lambda: write(other))


def settle(first, core, mine, other, in_shape, out_shape, earlier):
    earlier = list(earlier or [])

    def share_spec():
        return pl.BlockSpec((1,) + mine.shape[1:], lambda e, h, core: (e, 0, 0))

    def out_spec(dims):
        return pl.BlockSpec((1, dims[1] // 2, dims[2]), lambda e, h, core: (first + e, h, 0))

    return call(
        functools.partial(settle_kernel, len(earlier)),
        (mine.shape[0], 2),
        [share_spec(), share_spec()] + [pl.BlockSpec(memory_space=pl.ANY)] * len(earlier),
        [out_spec(in_shape), out_spec(out_shape)],
        [shape(in_shape, F32), shape(out_shape, F32)],
        prefetch=1,
        aliases={3 + i: i for i in range(len(earlier))},
        flops=0,
        nbytes=12 * mine.size,
    )(core, mine, other, *earlier)


def run_experts(first, number, base, rows, grads, gates, w_in, w_out, earlier):
    experts, pieces, cap, width = rows.shape
    group = max(1, 768 // cap)
    hidden_width = w_out.shape[1]

    def slot_spec(columns):
        return pl.BlockSpec((1, group, cap, columns), lambda e, c, base: (first + e, c, 0, 0))

    def expert_spec(array, offset):
        return pl.BlockSpec((1,) + array.shape[1:], lambda e, c, base: (offset + e, 0, 0))

    outs = [
        shape(rows.shape, BF),
        shape(rows.shape, BF),
        shape((experts, pieces, cap, LANES), BF),
        shape((number, (width + hidden_width) // 2, width), BF),
        shape((number, (width + hidden_width) // 2, width), BF),
    ]
    earlier = list(earlier or [])
    return call(
        functools.partial(lambda n_in, base, *refs: expert_kernel(n_in, first, base, *refs), len(earlier)),
        (number, pieces // group),
        [slot_spec(width), slot_spec(width), slot_spec(LANES), expert_spec(w_in, first), expert_spec(w_out, first)]
        + [pl.BlockSpec(memory_space=pl.ANY)] * len(earlier),
        [slot_spec(width), slot_spec(width), slot_spec(LANES), expert_spec(outs[3], 0), expert_spec(outs[4], 0)],
        outs,
        scratch=[pltpu.VMEM(w_in.shape[1:], F32), pltpu.VMEM(w_out.shape[1:], F32)],
        prefetch=1,
        aliases={6 + i: i for i in range(len(earlier))},
        flops=18 * number * pieces * cap * width * hidden_width,
        nbytes=number * (8 * pieces * cap * width + 12 * width * hidden_width),
    )(base, rows, grads, gates, w_in, w_out, *earlier)


def per_device(
    tokens, segments, routes, norm_in, q_weight, key_weight, value_weight, q_gain, k_gain,
    o_weight, norm_post, router, expert_in, expert_out, cotangent,
):
    size = lax.axis_size("group")
    me = lax.axis_index("group")
    sequences, length, width = tokens.shape
    half = width // 2
    parts = size // sequences
    rows = sequences * length
    full = length * size
    experts = expert_in.shape[0]
    cap = (length * TOPK * 4 // (3 * E) + 7) // 8 * 8
    bits = [1 << b for b in range(size.bit_length() - 1)]
    order_a, order_b = bits, bits[::-1]
    part, sequence = me // sequences, me % sequences
    exchange = [[q * sequences + s for s in range(sequences)] for q in range(parts)]
    fellows = [[q * sequences + s for q in range(parts)] for s in range(sequences)]

    def regroup(value):
        return lax.all_to_all(
            value, "group", 0, 0, tiled=True, axis_index_groups=exchange if parts > 1 else None
        )

    def gathered(value, order):
        return gather_relative(value, "group", size, order)

    replicas = lax.axis_size("replica")
    core = lax.axis_index("replica") % 2
    base = jnp.stack([me * experts, core])
    plan = Plan(base)

    def swap_core(value):
        return swap_bit(value, "replica", 1, replicas)

    n_norm, n_gain = norm_in.shape[0], q_gain.shape[0]
    gains = jnp.concatenate([norm_in, norm_post, q_gain, k_gain])
    n_small = gains.shape[0]
    named = jnp.concatenate([routes.transpose(0, 2, 1), segments[:, None, :]], axis=1)
    named = named.reshape(sequences * (TOPK + 1), length).astype(BF)
    gains = jnp.pad(gains, (0, -n_small % length)).reshape(-1, length)
    small = jnp.concatenate([named, gains], axis=0)
    small = jnp.stack([small] + [lax.ppermute(small, "group", [(i, i ^ j) for i in range(size)]) for j in range(1, size)])
    small = place(small, range(size), me)
    gains = small[:, named.shape[0] :].reshape(size, -1).astype(F32)
    named = small[:, : named.shape[0]].astype(I32).reshape(size, sequences, TOPK + 1, length)
    cuts = [0, n_norm, 2 * n_norm, 2 * n_norm + n_gain, 2 * n_norm + 2 * n_gain]
    gain_in, gain_post, gain_q, gain_k = (
        gains[:, a:b].reshape(1, -1) for a, b in zip(cuts[:-1], cuts[1:])
    )
    gain_q = jnp.concatenate([gain_q, gain_q], axis=1)
    gain_k = jnp.concatenate([gain_k, gain_k], axis=1)

    def own_half(shard):
        depth = shard.shape[0] // 2
        return lax.dynamic_slice_in_dim(shard, core * depth, depth)

    def both_cores(mine):
        other = swap_core(mine)
        return lax.select(
            core == 0,
            jnp.concatenate([mine, other], axis=1),
            jnp.concatenate([other, mine], axis=1),
        )

    key_width = key_weight.shape[1]
    orders = [
        jnp.stack([me ^ j for j in relative_order(order)]) for order in (order_a, order_b)
    ]
    half_a = gathered(own_half(jnp.concatenate([q_weight, o_weight[:, :half]], axis=1)), order_a)
    unused = jnp.zeros((router.shape[0], LANES - E), BF)
    half_b = jnp.concatenate([key_weight, value_weight, o_weight[:, half:], router, unused], axis=1)
    half_b = gathered(own_half(half_b), order_b)
    weight_a, weight_b = both_cores(half_a), both_cores(half_b)
    x = regroup(tokens).reshape(rows, width)
    shares = jnp.stack(
        [
            jnp.stack([(me ^ j) * n_norm + which * (n_norm // 2) for j in range(size)])
            for which in (core, 1 - core)
        ]
    )

    seg_full = lax.dynamic_index_in_dim(named[:, :, TOPK], sequence, 1, keepdims=False).reshape(full)
    place_of = part * rows + jnp.arange(rows, dtype=I32)
    seg_own = lax.dynamic_slice_in_dim(seg_full, part * rows, rows)
    first = jnp.sum((seg_full[None, :] < seg_own[:, None]).astype(I32), axis=1)
    frequency = jnp.exp(
        -(2.0 * jnp.arange(HEAD_SIZE // 2, dtype=F32) / HEAD_SIZE) * math.log(ROPE_BASE)
    )
    phase = (place_of - first).astype(F32)[:, None] * frequency
    cos, sin = jnp.cos(phase), jnp.sin(phase)
    cos = jnp.concatenate([cos] * 4, axis=1)
    sin = jnp.concatenate([-sin, sin, -sin, sin], axis=1)
    place_of = place_of[None, :]
    document = jnp.arange(LANES, dtype=I32)
    q_more = jnp.where((document < 8) & (seg_own[:, None] != document), -256.0, 0.0).astype(BF)
    k_more = jnp.where((document >= 8) & (document < 12), 1.0, 0.0)
    k_more = jnp.where(seg_full[:, None] == document, 1.0, k_more).astype(BF)

    pieces = size * sequences
    local = named.reshape(pieces, TOPK + 1, length)[:, :TOPK] - me * experts
    hit = jnp.zeros((pieces, experts, length), jnp.bool_)
    for k in range(TOPK):
        hit = hit | (local[:, k : k + 1, :] == jnp.arange(experts, dtype=I32)[:, None])
    before = (jnp.arange(length)[:, None] < jnp.arange(length)[None, :]).astype(BF)
    rank = jnp.einsum("pei,ij->pej", hit.astype(BF), before, preferred_element_type=F32)
    rank = jnp.where(hit, rank, -1.0)
    own_routes = lax.dynamic_slice(
        named, (part * sequences, sequence, 0, 0), (sequences, 1, TOPK, length)
    )
    own_routes = own_routes[:, 0].transpose(0, 2, 1).reshape(rows, TOPK)

    def sequence_pieces(j):
        other = me ^ j
        return (other // sequences * sequences + jnp.arange(sequences, dtype=I32)) * sequences + other % sequences

    def position_pieces(j):
        return (me ^ j) * sequences + jnp.arange(sequences, dtype=I32)

    cot = after(cotangent, half_a, half_b)
    cots, posts = ({}, {}), ({}, {})
    for value, order, result in ((cot[:, :, :half], order_a, cots[0]), (cot[:, :, half:], order_b, cots[1])):
        plan.start(gather_flow(plan, value, order, "group", size, result))

    plan.run(16.0)
    normed, q_pre, k_pre, queries, keys, values = project(
        orders, x, plan.tie(gain_in), weight_a, weight_b, gain_q, gain_k, cos, sin
    )
    plan.note(queries)
    plan.run(16.0)
    if parts > 1:
        keys = lax.all_gather(keys, "group", axis=0, tiled=True, axis_index_groups=fellows)
        values = lax.all_gather(values, "group", axis=0, tiled=True, axis_index_groups=fellows)
    attended, norms = attend(queries, keys, values, q_more, k_more, plan.tie(place_of))
    plan.note(attended)
    plan.run(22.0)
    middle, post_a, post_b, gates = route_rows(
        orders, x, plan.tie(attended), weight_a, weight_b, gain_post, own_routes
    )
    plan.note(post_a)
    plan.run(11.0)
    post_a, post_b = (v.reshape(sequences, length, -1) for v in (post_a, post_b))
    for value, order, result in ((post_a, order_a, posts[0]), (post_b, order_b, posts[1])):
        plan.start(gather_flow(plan, value, order, "group", size, result))

    def rows_of(j, part_a, part_b):
        nonlocal slot_rows
        slot_rows = dispatch(
            plan.tie(sequence_pieces(j)), base, rank, part_a, part_b, cap, width, slot_rows
        )
        plan.note(slot_rows[0])
        plan.run(8.5)

    slot_rows, slot_grads = None, None
    rows_of(0, (post_a[None], 0), (post_b[None], 0))
    plan.drain(lambda: cots[0] and cots[1])
    for j in range(size):
        slot_grads = dispatch(
            plan.tie(position_pieces(j)),
            base,
            rank,
            (cots[0][j], 0),
            (cots[1][j], 0),
            cap,
            width,
            slot_grads,
        )
        plan.note(slot_grads[0])
        plan.run(7.5)
    own_cot = jnp.zeros((sequences, length, width), BF)
    for j in range(sequences):
        for begin, held in ((0, cots[0][j]), (half, cots[1][j])):
            piece = lax.dynamic_slice(held, (0, sequence, 0, 0), (1, 1, length, half))[0]
            own_cot = lax.dynamic_update_slice(own_cot, piece, (sequence ^ j, 0, begin))
    own_cot = own_cot.reshape(rows, width)
    plan.note(own_cot)
    plan.run(10.0)
    plan.drain(lambda: posts[0] and posts[1])
    for j in range(1, size):
        rows_of(j, (posts[0][j], 0), (posts[1][j], 0))
    settled = []

    def expert_flow(e, keep, send):
        arrived = yield "core", travel(send, fast=True), swap_core(send)
        value = add_blocks(keep, plan.tie(arrived))
        plan.note(value, span=4.0)
        mine = []
        yield from line_flow(plan, value, "replica", replicas, mine)
        arrived = yield "core", travel(mine[0], fast=True), swap_core(mine[0])
        settled[:] = settle(
            e, core.reshape(1), mine[0], plan.tie(arrived), expert_in.shape, expert_out.shape, settled
        )
        plan.note(*settled, span=8.0)

    def owned_flow(keep_a, keep_b, send_a, send_b, result):
        arrived = yield (
            "core",
            travel(send_a, fast=True) + travel(send_b, fast=True),
            [swap_core(send) for send in (send_a, send_b)],
        )
        totals = [add_low(keep, plan.tie(a)) for keep, a in zip((keep_a, keep_b), arrived)]
        plan.note(*totals)
        mine = ([], [])
        for total, order, landed in zip(totals, (order_a, order_b), mine):
            have = {j: total[j] for j in range(size)}
            plan.start(scatter_flow(plan, order[0], have, order, "group", size, landed))
        while not (mine[0] and mine[1]):
            yield "wait", 10.0, None
        value = jnp.concatenate([mine[0][0], mine[1][0]], axis=1)
        mine = []
        yield from line_flow(plan, value, "replica", replicas, mine)
        mine = mine[0]
        arrived = yield "core", travel(mine, fast=True), swap_core(mine)
        other = plan.tie(arrived)
        result.append(
            jnp.where(
                core == 0,
                jnp.concatenate([mine, other], axis=0),
                jnp.concatenate([other, mine], axis=0),
            ).astype(F32)
        )
        plan.note(result[0])

    made, e = None, 0
    while e < experts:
        together = 2 if 0 < e < experts - 2 else 1
        *made, keep, send = run_experts(
            e, together, plan.tie(base), slot_rows[0], slot_grads[0], slot_rows[1], expert_in, expert_out, made
        )
        plan.note(keep)
        plan.run(7.0 + 17.0 * together)
        plan.start(expert_flow(e, keep, send))
        e += together

    summed, back, backs = None, ({}, {}), ([], [])
    waiting = [(order, have, result) for order, have, result in zip((order_a, order_b), back, backs)]
    for j in sorted(range(size), key=lambda j: (-bin(j).count("1"), j)):
        summed, back[0][j], back[1][j] = combine(
            plan.tie(sequence_pieces(j)),
            rank,
            *made,
            None if j else middle.reshape(sequences, length, width),
            summed,
        )
        plan.note(back[0][j], back[1][j])
        plan.now += 10.0
        for one in list(waiting):
            order, have, result = one
            if all(k in have for k in range(size) if k & order[0]):
                plan.start(scatter_flow(plan, order[0], have, order, "group", size, result))
                waiting.remove(one)
    plan.drain(lambda: backs[0] and backs[1])
    back_a, back_b = (b[0].reshape(rows, -1) for b in backs)
    arrived = lax.all_to_all(
        plan.tie(summed).reshape(size, sequences, length, width), "group", 0, 0, tiled=True
    )

    grad_middle, grad_att, *parts_o = route_back(
        shares, orders, middle, back_a, back_b, plan.tie(gates), own_cot, gain_post, weight_a, weight_b, attended
    )
    plan.note(grad_att)
    grads_o, grads_q = [], []
    plan.run(21.0)
    plan.start(owned_flow(*parts_o, grads_o))
    through = None
    span = KEY_VALUE_HEADS // 2
    for begin in range(0, KEY_VALUE_HEADS, span):
        through = attend_back(
            begin, span, queries, keys, values, grad_att, attended, norms, q_more, k_more,
            plan.tie(place_of), through,
        )
        plan.note(through[0])
        plan.run(24.0)
    dq, dk, dv = through
    if parts > 1:
        dk, dv = (
            lax.psum_scatter(
                d.astype(BF), "group", scatter_dimension=0, tiled=True, axis_index_groups=fellows
            ).astype(F32)
            for d in (dk, dv)
        )
    layer_out = jnp.sum(plan.tie(arrived).astype(F32), axis=0).astype(BF)
    plan.note(layer_out, span=8.0)
    tokens_grad, *parts_q = project_back(
        plan.tie(shares), orders, dq, dk, dv, q_pre, k_pre, x, normed, grad_middle, gain_in, weight_a, weight_b,
        gain_q, gain_k, cos, sin,
    )
    plan.note(tokens_grad)
    plan.now += 34.0
    waits = {"core": 35.0}
    last = max([flow[0] for flow in plan.flows if flow[3] == "out"] or [0.0])
    plan.flows = [
        (arrives + (-13.0 if arrives == last else waits.get(link, 15.0)), count, act, link)
        for arrives, count, act, link in plan.flows
    ]
    plan.free.pop("core", None)
    plan.start(owned_flow(*parts_q, grads_q))
    plan.run(0.0)
    tokens_grad = regroup(tokens_grad.reshape(sequences, length, width)).astype(F32)
    plan.drain(lambda: not plan.flows)
    grads_o, grads_q = grads_o[0], grads_q[0]
    expert_in_grad, expert_out_grad = settled
    extra = width + LANES
    return (
        layer_out,
        tokens_grad,
        grads_q[:, width],
        grads_q[:, :width],
        grads_q[:, extra : extra + key_width],
        grads_q[:, extra + key_width :],
        grads_q[:n_gain, width + 1],
        grads_q[:n_gain, width + 2],
        grads_o[:, :width],
        grads_o[:, width + E],
        grads_o[:, width : width + E],
        expert_in_grad,
        expert_out_grad,
    )


def solution(mesh):
    row, column = P("group", None), P("group")
    stream = P("replica", "group", None)
    expert = P("group", None, None)
    return jax.shard_map(
        per_device,
        mesh=mesh,
        in_specs=(
            stream, P("replica", "group"), stream, column, row, row, row, column, column,
            row, column, row, expert, expert, stream,
        ),
        out_specs=(
            stream, stream, column, row, row, row, column, column, row, column, row, expert, expert,
        ),
        check_vma=False,
    )
```
